32 devices in a mesh: section: 4 (over y, core), dp: 8 (over z, x).
Axes of the slice: x: 2, y: 2, z: 4, core: 2. Of those that a mesh axis runs over, the one named last changes fastest.
Arguments:
- horizon: bfloat16 [4, 8192, 256], P('section', 'dp'), may hold values from -6 to 6
- cotangent: bfloat16 [4, 8192, 256], P('section', 'dp'), may hold values from -6 to 6
- obs_tokens: bfloat16 [4, 256, 2, 256], P('section', 'dp'), may hold values from -6 to 6
- obs_repeat: int32 [4, 8, 32], P(None, 'dp'), may hold values from 1 to 4, 64 in all within a row
- noise_step: int32 [4, 512], P(None, 'dp'), may hold values from 0 to 99
- time_weight: bfloat16 [256, 256], replicated, may hold values from -0.375 to 0.375
- self_in: bfloat16 [4, 256, 768], P('section'), may hold values from -0.375 to 0.375
- self_out: bfloat16 [4, 256, 256], P('section'), may hold values from -0.75 to 0.75
- cross_q: bfloat16 [4, 256, 256], P('section'), may hold values from -0.375 to 0.375
- cross_kv: bfloat16 [4, 256, 512], P('section'), may hold values from -0.375 to 0.375
- cross_out: bfloat16 [4, 256, 256], P('section'), may hold values from -0.5 to 0.5
- mlp_up: bfloat16 [4, 256, 1024], P('section'), may hold values from -0.375 to 0.375
- mlp_down: bfloat16 [4, 1024, 256], P('section'), may hold values from -0.1875 to 0.1875
- gains: float32 [4, 3, 256], P('section'), may hold values from 0.5 to 1.5
- shifts: float32 [4, 10, 256], P('section'), may hold values from -2 to 2
- mlp_bias: float32 [4, 1024], P('section'), may hold values from -2 to 2
Outputs:
- predictions: bfloat16 [4, 8192, 256], P('section', 'dp')
- horizon_grad: bfloat16 [4, 8192, 256], P('section', 'dp')
- self_in_grad: float32 [4, 256, 768], P('section', 'dp')
- self_out_grad: float32 [4, 256, 256], P('section', 'dp')
- cross_q_grad: float32 [4, 256, 256], P('section', 'dp')
- cross_kv_grad: float32 [4, 256, 512], P('section', 'dp')
- cross_out_grad: float32 [4, 256, 256], P('section', 'dp')
- mlp_up_grad: float32 [4, 256, 1024], P('section', 'dp')
- mlp_down_grad: float32 [4, 1024, 256], P('section', 'dp')
- gains_grad: float32 [4, 3, 256], P('section', None, 'dp')
- shifts_grad: float32 [4, 10, 256], P('section', None, 'dp')
- mlp_bias_grad: float32 [4, 1024], P('section', 'dp')
- time_weight_grad: float32 [256, 256], P('dp')
The draws below stay inside these ranges and needn't reach their ends.
Inputs may be any that keep to these rules, and one draw needn't show every extreme that they name: `obs_repeat`: each row of 32 counts sums to 64.
All inputs are finite; a program needn't handle non-finite values.
Results may differ from the reference program's by a relative error of at most 0.025.
Values may be sent and summed in bfloat16 or wider, within the bound.
A program may use at most 384 MiB of HBM per device.

```python
import math
import jax
import jax.numpy as jnp
import numpy as np
from jax import lax

D = 256
HEADS = 4
HEAD_DIM = 64
FF = 1024
LPS = 1
HOR = 16
NOBS = 2
REPEAT = 4
SAMP_DEV = 64
OBS_DEV = 32
LAYERS = 4
MICRO = 4
ROWS = 8192
SAMPLES = 512
OBS_ALL = 256
N_DP = 8


def place_ends(result, own_key, least, high):
    index_at = [jax.random.randint(jax.random.fold_in(own_key, axis), (), 0, length) for axis, length in enumerate(result.shape)]
    main_axis = result.shape.index(max(result.shape))
    next_to = index_at[:main_axis] + [(index_at[main_axis] + 1) % result.shape[main_axis]] + index_at[main_axis + 1:]
    return result.at[tuple(index_at)].set(least).at[tuple(next_to)].set(high)


def block_levels(own_key, shape, split, least, largest):
    level = 1.0
    for position, shards_of in split:
        heights = jax.random.uniform(jax.random.fold_in(jax.random.fold_in(own_key, 6), position), (shards_of,), jnp.float32, least / len(split), largest / len(split))
        level = level * jnp.repeat(jnp.exp(heights), shape[position] // shards_of).reshape((-1,) + (1,) * (len(shape) - 1 - position))
    return level


def profile(count, total, reach, slope):
    portions = [(1 << 20) // math.isqrt(rank ** slope) + 1 for rank in range(2, count + 1)]
    rest, given = total - reach - (count - 1), [1] * (count - 1)
    while rest > 0:
        free = [i for i in range(count - 1) if given[i] < reach]
        whole, remaining = sum([portions[i] for i in free]), rest
        for i in free:
            more = min(reach - given[i], max(1, remaining * portions[i] // whole), rest)
            given[i] = given[i] + more
            rest = rest - more
    return np.array([reach] + given)


def ragged_sizes(rng, number_of, total, reach, lean):
    if number_of == 2:
        one = jax.random.randint(rng, (), max(1, total - reach), min(reach, total - 1) + 1)
        return jnp.stack([one, total - one])
    tallies = jnp.asarray(profile(number_of, total, reach, lean), jnp.int32)
    pairs = (number_of - 1) // 2
    donor, taker = tallies[1:1 + 2 * pairs:2], tallies[2:2 + 2 * pairs:2]
    room = jnp.minimum(donor - 1, reach - taker)
    passed = jax.random.randint(jax.random.fold_in(rng, 1), (pairs,), 0, 1 << 20) % (room + 1)
    tallies = tallies.at[1:1 + 2 * pairs:2].set(donor - passed).at[2:2 + 2 * pairs:2].set(taker + passed)
    return tallies[jax.random.permutation(jax.random.fold_in(rng, 2), number_of)]


def normal_values(own_key, extent, deviation, limit, pieces=(), held_as=jnp.bfloat16):
    values = jax.random.normal(own_key, extent, jnp.float32) * deviation
    if len(pieces) > 0:
        values = block_levels(own_key, extent, pieces, -0.22, 0.18) * values
    return jnp.clip(values, min=-limit, max=limit).astype(held_as)


def setup_inputs(seed: int = 0) -> dict:
    splits = jax.random.split(jax.random.key(seed), 17)
    return {
        "horizon": normal_values(splits[0], (MICRO, ROWS, D), 1.0, 6.0, ((0, 4), (1, 8))),
        "cotangent": normal_values(splits[1], (MICRO, ROWS, D), 1.0, 6.0, ((0, 4), (1, 8))),
        "obs_tokens": normal_values(splits[2], (MICRO, OBS_ALL, NOBS, D), 1.0, 6.0, ((0, 4), (1, 8))),
        "obs_repeat": jax.vmap(lambda own: ragged_sizes(own, OBS_DEV, SAMP_DEV, REPEAT, 2))(jax.random.split(splits[3], MICRO * N_DP)).reshape((MICRO, N_DP, OBS_DEV)).astype(jnp.int32),
        "noise_step": place_ends(jax.random.randint(splits[4], (MICRO, SAMPLES), 0, 100), jax.random.fold_in(splits[4], 1), 0, 99).astype(jnp.int32),
        "time_weight": normal_values(splits[5], (D, D), D ** -0.5, 0.375),
        "self_in": normal_values(splits[6], (LAYERS, D, 3 * D), D ** -0.5, 0.375, ((0, 4),)),
        "self_out": normal_values(splits[7], (LAYERS, D, D), (D // 4) ** -0.5, 0.75, ((0, 4),)),
        "cross_q": normal_values(splits[8], (LAYERS, D, D), D ** -0.5, 0.375, ((0, 4),)),
        "cross_kv": normal_values(splits[9], (LAYERS, D, 2 * D), D ** -0.5, 0.375, ((0, 4),)),
        "cross_out": normal_values(splits[10], (LAYERS, D, D), (D // 2) ** -0.5, 0.5, ((0, 4),)),
        "mlp_up": normal_values(splits[11], (LAYERS, D, FF), D ** -0.5, 0.375, ((0, 4),)),
        "mlp_down": normal_values(splits[12], (LAYERS, FF, D), FF ** -0.5, 0.1875, ((0, 4),)),
        "gains": jnp.clip(1.0 + 0.1 * jax.random.normal(splits[13], (LAYERS, 3, D), jnp.float32), 0.5, 1.5),
        "shifts": normal_values(splits[14], (LAYERS, 10, D), 0.3, 2.0, ((0, 4),), jnp.float32),
        "mlp_bias": normal_values(splits[15], (LAYERS, FF), 0.3, 2.0, ((0, 4),), jnp.float32),
    }


@jax.custom_vjp
def low(v):
    return lax.optimization_barrier(v.astype(jnp.bfloat16)).astype(jnp.float32)

@jax.custom_vjp
def low_back(v):
    return v

def low_keep(v):
    return (low(v), None)

def low_pass(kept, grad):
    return (grad,)

def back_keep(v):
    return (v, None)

def back_low(kept, grad):
    return (low(grad),)
low.defvjp(low_keep, low_pass)
low_back.defvjp(back_keep, back_low)

def round_both(values):
    return low_back(low(values))

def exact_dot(left_side, right_side):
    return jnp.dot(left_side, right_side, precision=lax.Precision.HIGHEST)

def exact_einsum(pattern, left_side, right_side):
    return jnp.einsum(pattern, left_side, right_side, precision=lax.Precision.HIGHEST)

def layer_norm(values, gain_row, shift_row):
    center = values - lax.optimization_barrier(jnp.mean(values, axis=-1, keepdims=True))
    spread = lax.optimization_barrier(jnp.mean(center * center, axis=-1, keepdims=True))
    return center * lax.rsqrt(spread + 1e-05) * gain_row + shift_row

def softmax_total(scores):
    row_top = lax.optimization_barrier(jnp.max(scores, axis=-1, keepdims=True))
    return row_top + jnp.log(lax.optimization_barrier(jnp.sum(jnp.exp(scores - row_top), axis=-1, keepdims=True)))

def sinus_table(noise_steps, columns):
    half_cols = columns // 2
    frequency = jnp.exp(-math.log(10000.0) * jnp.arange(half_cols).astype(jnp.float32) / half_cols)
    angles = noise_steps.astype(jnp.float32)[:, None] * frequency[None, :]
    return jnp.concatenate([jnp.sin(angles), jnp.cos(angles)], axis=1)

def block_forward(params, row_block, time_matrix, observed, counts, noise_steps):
    w_in, w_so, w_cq, w_ckv, w_co, w_up, w_dn, gain_all, shift_all, bias_up = params
    samples = noise_steps.shape[0]
    tokens = samples * HOR
    score_scale = HEAD_DIM ** (-0.5)
    head_shape = (samples, HOR, HEADS, HEAD_DIM)
    joined_shape = (samples, NOBS + 1, HEADS, HEAD_DIM)
    memory = low(exact_dot(low(sinus_table(noise_steps, D)), time_matrix))
    running_ends = jnp.cumsum(counts)
    owner_index = lax.optimization_barrier(jnp.sum((jnp.arange(samples)[:, None] >= running_ends[None, :]).astype(jnp.int32), axis=1))
    causal = jnp.arange(HOR)[:, None] >= jnp.arange(HOR)[None, :]
    residual = row_block
    for layer_index in range(LAYERS):
        gain_rows = gain_all[layer_index]
        shift_rows = shift_all[layer_index]
        normed = low(layer_norm(residual, gain_rows[0], shift_rows[0]))
        qkv_all = exact_dot(normed, w_in[layer_index])
        queries = round_both(qkv_all[:, :D] + shift_rows[3]).reshape(head_shape)
        keys_self = round_both(qkv_all[:, D:2 * D]).reshape(head_shape)
        vals_self = round_both(qkv_all[:, 2 * D:] + shift_rows[4]).reshape(head_shape)
        scores = low_back(exact_einsum('sqhe,skhe->shqk', queries, keys_self) * score_scale)
        scores = jnp.where(causal, scores, -1e+30)
        probs_low = low(jnp.exp(scores - softmax_total(scores)))
        context_self = round_both(exact_einsum('shqk,skhe->sqhe', probs_low, vals_self).reshape(tokens, D))
        residual = residual + low_back(exact_dot(context_self, w_so[layer_index]) + shift_rows[5])
        cross_in = low(layer_norm(residual, gain_rows[1], shift_rows[1]))
        cross_query = round_both(exact_dot(cross_in, w_cq[layer_index]) + shift_rows[6]).reshape(head_shape)
        time_kv = exact_dot(memory, w_ckv[layer_index])
        obs_kv = exact_dot(observed, w_ckv[layer_index])
        time_keys = round_both(time_kv[:, :D])
        time_vals = round_both(time_kv[:, D:] + shift_rows[7])
        obs_keys = round_both(obs_kv[:, :D]).reshape(-1, NOBS, D)
        obs_vals = round_both(obs_kv[:, D:] + shift_rows[7]).reshape(-1, NOBS, D)
        joined_keys = jnp.concatenate([time_keys[:, None, :], jnp.take(obs_keys, owner_index, axis=0)], axis=1).reshape(joined_shape)
        joined_vals = jnp.concatenate([time_vals[:, None, :], jnp.take(obs_vals, owner_index, axis=0)], axis=1).reshape(joined_shape)
        scores_cross = low_back(exact_einsum('sqhe,sjhe->shqj', cross_query, joined_keys) * score_scale)
        probs_cross = low(jnp.exp(scores_cross - softmax_total(scores_cross)))
        context_cross = round_both(exact_einsum('shqj,sjhe->sqhe', probs_cross, joined_vals).reshape(tokens, D))
        residual = residual + low_back(exact_dot(context_cross, w_co[layer_index]) + shift_rows[8])
        mlp_in = low(layer_norm(residual, gain_rows[2], shift_rows[2]))
        hidden_pre = low_back(exact_dot(mlp_in, w_up[layer_index]) + bias_up[layer_index])
        hidden = low(jax.nn.gelu(hidden_pre))
        residual = residual + low_back(exact_dot(hidden, w_dn[layer_index]) + shift_rows[9])
        if (layer_index + 1) % LPS == 0 and layer_index + 1 < LAYERS:
            residual = low_back(low(residual))
    return low(residual)

def reference(horizon, cotangent, obs_tokens, obs_repeat, noise_step, time_weight, self_in, self_out, cross_q, cross_kv, cross_out, mlp_up, mlp_down, gains, shifts, mlp_bias):
    params = tuple((weight.astype(jnp.float32) for weight in (self_in, self_out, cross_q, cross_kv, cross_out, mlp_up, mlp_down, gains, shifts, mlp_bias)))
    time_matrix = time_weight.astype(jnp.float32)
    tokens = SAMP_DEV * HOR

    def one_block(carried, block_index):
        micro_index = block_index // N_DP
        group_index = block_index % N_DP
        row_start = (group_index * tokens).astype(jnp.int32)
        rows_in = lax.dynamic_slice_in_dim(lax.dynamic_index_in_dim(horizon, micro_index, 0, keepdims=False), row_start, tokens, 0).astype(jnp.float32)
        rows_cot = lax.dynamic_slice_in_dim(lax.dynamic_index_in_dim(cotangent, micro_index, 0, keepdims=False), row_start, tokens, 0).astype(jnp.float32)
        observed = lax.dynamic_slice_in_dim(lax.dynamic_index_in_dim(obs_tokens, micro_index, 0, keepdims=False), (group_index * OBS_DEV).astype(jnp.int32), OBS_DEV, 0)
        observed = observed.reshape(OBS_DEV * NOBS, D).astype(jnp.float32)
        counts = lax.dynamic_index_in_dim(lax.dynamic_index_in_dim(obs_repeat, micro_index, 0, keepdims=False), group_index, 0, keepdims=False)
        noise_steps = lax.dynamic_slice_in_dim(lax.dynamic_index_in_dim(noise_step, micro_index, 0, keepdims=False), (group_index * SAMP_DEV).astype(jnp.int32), SAMP_DEV, 0)

        def forward(param_set, row_block, matrix):
            return block_forward(param_set, row_block, matrix, observed, counts, noise_steps)
        predicted, pullback = jax.vjp(forward, params, rows_in, time_matrix)
        param_grads, rows_grad, matrix_grad = pullback(rows_cot)
        summed = tuple((running + addend for running, addend in zip(carried[0], param_grads)))
        return ((summed, carried[1] + matrix_grad), (predicted.astype(jnp.bfloat16), rows_grad.astype(jnp.bfloat16)))
    initial = (tuple((jnp.zeros_like(weight) for weight in params)), jnp.zeros_like(time_matrix))
    (param_sums, matrix_sum), (predicted, rows_grads) = lax.scan(one_block, initial, jnp.arange(MICRO * N_DP).astype(jnp.int32))
    predictions = predicted.reshape(MICRO, N_DP * tokens, D)
    horizon_grad = rows_grads.reshape(MICRO, N_DP * tokens, D)
    return (predictions, horizon_grad, param_sums[0], param_sums[1], param_sums[2], param_sums[3], param_sums[4], param_sums[5], param_sums[6], param_sums[7], param_sums[8], param_sums[9], matrix_sum)
```

```python
import functools
import math

import jax
import jax.numpy as jnp
from jax import lax
from jax.experimental import pallas as pl
from jax.experimental.pallas import tpu as pltpu
from jax.sharding import PartitionSpec as P

HEADS = 4
VMEM_BYTES = 63 * 1024 * 1024
SUB = 128
F32 = jnp.float32
BF16 = jnp.bfloat16

W_IN, W_SO, W_CKV, W_CQ, W_CO, W_UP, W_END = 0, 768, 1024, 1536, 1792, 2048, 3072
SHIFT, BIAS, KEYSUM, VEC_ROWS = 3, 13, 17, 24
SENT = ((W_IN, 512), (512, W_CKV), (W_CKV, W_CQ), (W_CQ, W_UP), (W_UP, W_END))
DOWN_PIECE, PIECES = 5, 6
DOWN, UP, CROSS, SELF, TIME, VECTOR = range(6)
WIDTHS = (512, 512, 640, 384, 128, 128)
FORWARD_SELF, FORWARD_CROSS, FORWARD_FF = 1024, 1024, 1024
BACK_FF, BACK_CROSS, BACK_SELF = 1024, 1024, 1024
ROWS, NZ, NX = 32, 4, 2
GROUPS = NZ * NX
KEYS, WIDE = 24, 96


def dot(left, right):
    return jnp.dot(left, right, preferred_element_type=F32)


def dot_nt(left, right):
    return lax.dot_general(left, right, (((1,), (1,)), ((), ())), preferred_element_type=F32)


def dot_tn(left, right):
    return lax.dot_general(left, right, (((0,), (0,)), ((), ())), preferred_element_type=F32)


def iota(shape, axis):
    return lax.broadcasted_iota(jnp.int32, shape, axis)


def low(values):
    return jnp.asarray(values, BF16)


def normalize(values):
    center = values - jnp.mean(values, axis=-1, keepdims=True)
    scale = lax.rsqrt(jnp.mean(center * center, axis=-1, keepdims=True) + 1e-05)
    return center * scale, scale


def normalize_back(grad, unit, scale, gain):
    ahead = grad * unit
    grad_unit = grad * gain
    mean_grad = jnp.mean(grad_unit, axis=-1, keepdims=True)
    mean_along = jnp.mean(ahead * gain, axis=-1, keepdims=True)
    back = (grad_unit - mean_grad - unit * mean_along) * scale
    return back, jnp.sum(ahead, axis=0, keepdims=True), jnp.sum(grad, axis=0, keepdims=True)


def half_masks():
    lane = iota((1, SUB), 1)
    first = (lane < SUB // 2).astype(F32)
    return low(first), low(1.0 - first)


def add_low(left, right):
    return left + right


def place_row(column):
    size = column.shape[0]
    diagonal = iota((size, size), 0) == iota((size, size), 1)
    return jnp.sum(jnp.where(diagonal, column, 0.0), axis=0, keepdims=True)


def place_column(row):
    size = row.shape[1]
    diagonal = iota((size, size), 0) == iota((size, size), 1)
    return jnp.sum(jnp.where(diagonal, row, 0.0), axis=1, keepdims=True)


class Links:
    def __init__(self, w_s, wd_s, vec_s, wsend, wrecv, sets):
        self.w, self.wd, self.vec, self.wsend, self.wrecv, self.sets = w_s, wd_s, vec_s, wsend, wrecv, sets
        self.section = lax.axis_index("section")
        self.group = lax.axis_index("dp")
        self.core, self.y = self.section % 2, self.section // 2
        self.x, self.z = self.group % NX, self.group // NX
        self.x_peer = self.z * NX + (self.x + 1) % NX

    def relative(self, step):
        return (self.y + step // 2) % 2 * 2 + (self.core + step % 2) % 2

    def relation(self, block):
        return (self.y + block // 2) % 2 * 2 + (self.core + block % 2) % 2

    def z_peer(self, step):
        return (self.z + step) % NZ * NX + self.x

    def greet(self):
        barrier = pltpu.get_barrier_semaphore()
        peers = [{"section": self.relative(step)} for step in (1, 2, 3)]
        peers += [{"dp": self.x_peer}] + [{"dp": self.z_peer(step)} for step in range(1, NZ)]
        for peer in peers:
            pl.semaphore_signal(barrier, inc=1, device_id=peer, device_id_type=pl.DeviceIdType.MESH)
        pl.semaphore_wait(barrier, len(peers))

    def remote(self, src, dst, send, recv, peer):
        return pltpu.make_async_remote_copy(
            src_ref=src, dst_ref=dst, send_sem=send, recv_sem=recv, device_id=peer,
            device_id_type=pl.DeviceIdType.MESH,
        )

    def weight_copy(self, slot, block, piece, half, peer):
        array, lanes = (self.wd, slice(None)) if piece == DOWN_PIECE else (self.w, slice(*SENT[piece]))
        part = array.at[block, :, lanes]
        if half is not None:
            rows = array.shape[1] // 2
            part = array.at[block, pl.ds(pl.multiple_of(half * rows, rows), rows), lanes]
        return self.remote(part, part, self.wsend.at[slot], self.wrecv.at[slot], peer)

    def vector_copy(self, slot, block, peer):
        part = self.vec.at[block]
        return self.remote(part, part, self.wsend.at[slot], self.wrecv.at[slot], peer)

    def to_sibling(self, piece, block):
        return self.weight_copy(piece, block, piece, None, {"section": self.relative(1)})

    def over_y(self, piece, block):
        return self.weight_copy(PIECES + piece, block, piece, self.x, {"section": self.relative(2)})

    def over_x(self, piece, block, half):
        return self.weight_copy(2 * PIECES + piece, block, piece, half, {"dp": self.x_peer})

    def forwarded(self, piece, block, half, which):
        return self.weight_copy((3 + which) * PIECES + piece, block, piece, half, {"section": self.relative(1)})

    def vectors(self, step, block, peer):
        return self.vector_copy(5 * PIECES + step, block, {"section": peer})

    def start_y(self, when, pieces):
        @pl.when(when & (self.core == 1))
        def _():
            for piece in pieces:
                self.over_y(piece, self.section).start()

    def pass_first(self, piece, block):
        self.over_y(piece, block).wait_recv()
        self.over_x(piece, block, self.x).start()
        self.forwarded(piece, block, self.x, 0).start()

    def pass_second(self, piece, block):
        self.over_x(piece, block, 1 - self.x).wait_recv()
        self.forwarded(piece, block, 1 - self.x, 1).start()

    def pass_on(self, block, when, *works):
        @pl.when(self.relation(block) == 2 if when is True else when & (self.relation(block) == 2))
        def _():
            for stage, piece in works:
                if stage == 1 and piece == 0:
                    self.vectors(1, block, self.relative(2)).wait_recv()
                    self.vectors(2, block, self.relative(1)).start()
                (self.pass_first if stage == 1 else self.pass_second)(piece, block)

    def arrive(self, block, pieces):
        relation = self.relation(block)

        @pl.when(relation == 1)
        def _():
            if 0 in pieces:
                self.vectors(0, block, self.relative(1)).wait_recv()
            for piece in pieces:
                self.to_sibling(piece, block).wait_recv()

        @pl.when(relation == 3)
        def _():
            if 0 in pieces:
                self.vectors(2, block, self.relative(1)).wait_recv()
            for piece in pieces:
                self.forwarded(piece, block, self.x, 0).wait_recv()
                self.forwarded(piece, block, 1 - self.x, 1).wait_recv()

    def finish_weights(self):
        own, passed = self.section, self.relative(2)
        self.vectors(0, own, self.relative(1)).wait_send()
        self.vectors(1, own, self.relative(2)).wait_send()
        self.vectors(2, passed, self.relative(1)).wait_send()
        for piece in range(PIECES):
            self.to_sibling(piece, own).wait_send()
            self.over_y(piece, own).wait_send()
            self.over_x(piece, passed, self.x).wait_send()
            self.forwarded(piece, passed, self.x, 0).wait_send()
            self.forwarded(piece, passed, 1 - self.x, 1).wait_send()

    def near(self, kind):
        group_s, near_s, _, _, _, _, _, send, recv = self.sets[kind]
        return self.remote(group_s.at[1 - self.core], near_s, send.at[0], recv.at[0],
                           {"section": self.relative(1)})

    def row(self, kind):
        group_s, _, row_s, _, _, _, _, send, recv = self.sets[kind]
        return self.remote(group_s.at[self.core, :, 1 - self.x], row_s, send.at[1], recv.at[1],
                           {"dp": self.x_peer})

    def far(self, kind, step):
        far_s, _, _, fold_s, send, recv = self.sets[kind][3:]
        return self.remote(fold_s.at[(self.z + step) % NZ], far_s.at[step - 1],
                           send.at[1 + step], recv.at[1 + step], {"dp": self.z_peer(step)})

    def last(self, kind, step, peer):
        last_s, sum_s, _, send, recv = self.sets[kind][4:]
        slot = NZ + step
        return self.remote(sum_s, last_s.at[step - 1],
                           send.at[slot], recv.at[slot], {"section": peer})

    def after_near(self, kind):
        group_s, near_s = self.sets[kind][:2]
        self.near(kind).wait()
        group_s[self.core] = add_low(group_s[self.core], near_s[...])
        self.row(kind).start()

    def after_row(self, kind):
        group_s, row_s, fold_s = self.sets[kind][0], self.sets[kind][2], self.sets[kind][6]
        self.row(kind).wait()
        fold_s[...] = add_low(group_s[self.core, :, self.x], row_s[...])
        for step in range(1, NZ):
            self.far(kind, step).start()

    def sum_far(self, kind):
        far_s, _, sum_s, fold_s = self.sets[kind][3:7]
        for step in range(1, NZ):
            self.far(kind, step).wait()
        total = fold_s[self.z].astype(F32)
        for step in range(1, NZ):
            total = total + far_s[step - 1].astype(F32)
        sum_s[...] = low(total)

    def after_far(self, kind, block):
        self.sum_far(kind)
        relation = self.relation(block)

        @pl.when(relation > 0)
        def _():
            self.last(kind, relation, block).start()

    def halves(self, kind):
        last_s, sum_s = self.sets[kind][4:6]
        here = sum_s[...].astype(F32) + last_s[1].astype(F32)
        there = last_s[0].astype(F32) + last_s[2].astype(F32)
        return jnp.where(self.core == 0, here, there), jnp.where(self.core == 0, there, here)

    def after_last(self, kind, block, store):
        relation = self.relation(block)

        @pl.when(relation > 0)
        def _():
            self.last(kind, relation, block).wait_send()

        @pl.when(relation == 0)
        def _():
            for step in (1, 2, 3):
                self.last(kind, step, self.relative(step)).wait_recv()
            store(*self.halves(kind))

    def after_far_all(self, kind):
        self.sum_far(kind)
        for step in (1, 2, 3):
            self.last(kind, step, self.relative(step)).start()

    def after_last_all(self, kind):
        for step in (1, 2, 3):
            self.last(kind, step, self.relative(step)).wait()
        return self.halves(kind)


def block_kernel(remote, *refs):
    (x_ref, cot_ref, obs_ref, repeat_ref, noise_ref, tw_ref), refs = refs[:6], refs[6:]
    if remote:
        in_refs, refs = refs[:10], refs[10:]
        (pred_ref, grad_ref, in_out, so_out, cq_out, ckv_out, co_out, up_out, dn_out,
         gains_out, shifts_out, bias_out, time_out, hid_hbm, slope_hbm), refs = refs[:15], refs[15:]
    else:
        (w_hbm, wd_hbm, vec_hbm), refs = refs[:3], refs[3:]
        (pred_ref, grad_ref), dw_refs, refs = refs[:2], refs[2:6], refs[6:]
        (dvec_ref, time_out, hid_hbm, slope_hbm), refs = refs[:4], refs[4:]
    (unit_s, scale_s, qkv_s, prob_s, ctx_s, cq_s, cprob_s, cctx_s, hid_s, slope_s, dy_s, g_s,
     w_s, wd_s, vec_s, dvec_s, select_s, turned_s, tok_s, wide_s, folded_s, dmem_s, sinus_s, causal_s,
     own_s, flat_s, load_sem), groups, refs = refs[:27], refs[27:31], refs[31:]
    tokens, cols = x_ref.shape
    samples = noise_ref.shape[1]
    horizon = tokens // samples
    blocks = w_s.shape[0]
    per_sub = SUB // horizon
    score_scale = (cols // HEADS) ** (-0.5)
    section = lax.axis_index("section")
    ring = blocks - 1
    kept = ((hid_s, hid_hbm, load_sem.at[0]), (slope_s, slope_hbm, load_sem.at[1]))
    out_copies = [pltpu.make_async_copy(held.at[0], away, sem) for held, away, sem in kept]
    back_copies = [pltpu.make_async_copy(away, held.at[0], sem) for held, away, sem in kept]

    loads = [pltpu.make_async_copy(x_ref, pred_ref, load_sem.at[0]),
             pltpu.make_async_copy(cot_ref, grad_ref, load_sem.at[1])]
    if remote:
        gains_ref, shifts_ref, bias_ref = in_refs[7:]
        starts_at = (W_IN, W_SO, W_CKV, W_CQ, W_CO, W_UP)
        pieces = []
        for index, start in enumerate(starts_at):
            ref = in_refs[(0, 1, 3, 2, 4, 5)[index]]
            pieces.append(pltpu.make_async_copy(
                ref.at[0], w_s.at[section, :, start : start + ref.shape[2]], load_sem.at[2 + index]))
        pieces.append(pltpu.make_async_copy(in_refs[6].at[0], wd_s.at[section], load_sem.at[8]))
        for copy in pieces + loads:
            copy.start()
        vec_s[section] = jnp.zeros((VEC_ROWS, cols), F32)
        for row in range(SHIFT):
            vec_s[section, row : row + 1, :] = gains_ref[row]
        for row in range(SHIFT, BIAS):
            vec_s[section, row : row + 1, :] = shifts_ref[row - SHIFT]
        for part in range(4):
            vec_s[section, BIAS + part : BIAS + part + 1, :] = bias_ref[:, part * cols : (part + 1) * cols]
        sets = [(group,) + refs[2 + 8 * kind : 10 + 8 * kind] for kind, group in enumerate(groups)]
        sets += [refs[34 + 9 * index : 43 + 9 * index] for index in range(2)]
        links = Links(w_s, wd_s, vec_s, refs[0], refs[1], sets)
        links.greet()
        links.vectors(0, section, links.relative(1)).start()
        links.vectors(1, section, links.relative(2)).start()
        for piece, copies in enumerate((pieces[:1], pieces[1:2], pieces[2:3], pieces[3:5], pieces[5:6], pieces[6:])):
            for copy in copies:
                copy.wait()
            links.to_sibling(piece, section).start()

            @pl.when(links.core == 0)
            def _():
                links.over_y(piece, section).start()
    else:
        loads += [pltpu.make_async_copy(w_hbm, w_s, load_sem.at[2]),
                  pltpu.make_async_copy(wd_hbm, wd_s, load_sem.at[3]),
                  pltpu.make_async_copy(vec_hbm, vec_s, load_sem.at[4])]
        for copy in loads:
            copy.start()

    wide_masks = [jnp.concatenate([mask, mask], axis=1) for mask in half_masks()]
    lane_sub = iota((SUB, SUB), 1)
    row_sub = iota((SUB, SUB), 0)

    noise_row = noise_ref[pl.ds(section, 1), :].astype(F32)
    diagonal = iota((samples, samples), 0) == iota((samples, samples), 1)
    noise_col = jnp.sum(jnp.where(diagonal, noise_row, 0.0), axis=1, keepdims=True)
    half = cols // 2
    frequency = jnp.exp(iota((1, half), 1).astype(F32) * (-math.log(10000.0) / half))
    angles = noise_col * frequency
    sinus = low(jnp.concatenate([jnp.sin(angles), jnp.cos(angles)], axis=1))
    sinus_s[...] = sinus
    tok_s[:samples, :] = low(dot(sinus, tw_ref[...]))
    obs_count = repeat_ref.shape[-1]
    for index in range(obs_ref.shape[1]):
        tok_s[samples + index * obs_count : samples + (index + 1) * obs_count, :] = obs_ref[:, index, :]
    counts = low(repeat_ref[section].astype(F32))
    token_of = iota((obs_count, SUB), 1) - samples
    owner_of = iota((obs_count, SUB), 0)
    is_obs = token_of >= 0
    before = low((is_obs & (owner_of < token_of % obs_count)).astype(F32))
    upto = low((is_obs & (owner_of <= token_of % obs_count)).astype(F32))
    counts8 = jnp.broadcast_to(counts, (8, obs_count))
    starts = dot(counts8, before)[:1, :]
    ends = dot(counts8, upto)[:1, :]

    def select_rows(index, carried):
        key = iota((KEYS, SUB), 0) // per_sub
        lane = iota((KEYS, SUB), 1)
        sample = index * per_sub + iota((KEYS, SUB), 0) % per_sub
        sample_f = sample.astype(F32)
        time_hit = (key == 0) & (lane == sample)
        token = lane - samples
        owned = (sample_f >= starts) & (sample_f < ends)
        obs_hit = (token >= 0) & (token // obs_count == key - 1) & owned
        folded_s[index, :, :SUB] = (time_hit | obs_hit).astype(F32)
        return carried

    lax.fori_loop(0, tokens // SUB, select_rows, 0)
    selected = folded_s[...].reshape(-1, 2 * cols)[:, :SUB]
    select_s[...] = low(selected)
    selected = jnp.concatenate([selected, jnp.zeros((2 * SUB - selected.shape[0], SUB), F32)], axis=0)
    turned_s[...] = low(jnp.transpose(selected))
    same = row_sub // horizon == lane_sub // horizon
    causal_s[...] = jnp.where(same & (row_sub <= lane_sub), 0.0, -1e30)
    third = WIDE // 3
    own_s[...] = (iota((third, SUB), 0) % per_sub == iota((third, SUB), 1) // horizon).astype(F32)
    head_mask = (iota((third, cols), 0) // per_sub == iota((third, cols), 1) // (cols // HEADS)).astype(F32)
    dmem_s[...] = jnp.zeros_like(dmem_s)
    dvec_s[...] = jnp.zeros_like(dvec_s)
    for copy in loads:
        copy.wait()

    def vec(block, row):
        return vec_s[block, row : row + 1, :]

    def weight(block, start, stop):
        return w_s[block, :, start:stop]

    def condition(block):
        kv = dot(tok_s[...], weight(block, W_CKV, W_CQ))
        keys = low(kv[:, :cols])
        vals = low(kv[:, cols:] + vec(block, SHIFT + 7))

        spread = dot(select_s[...], jnp.concatenate([keys, vals], axis=1))
        both_masks = jnp.concatenate([head_mask, head_mask], axis=1)
        for index in range(tokens // SUB):
            for key in range(3):
                start = index * KEYS + key * per_sub
                copies = jnp.concatenate([spread[start : start + per_sub]] * HEADS, axis=0)
                wide_s[index, key * third : (key + 1) * third, :] = low(copies * both_masks)

    def fold(values):
        parts = []
        for part in thirds(values):
            part = part * head_mask
            parts.append(sum(part[head * per_sub : (head + 1) * per_sub] for head in range(HEADS)))
        return jnp.concatenate(parts, axis=0)

    def thirds(values):
        return [values[third * key : third * (key + 1)] for key in range(3)]

    def over_heads(values):
        return jnp.concatenate([values[:, :SUB], values[:, SUB:]], axis=0)

    def each_chunk(chunk, body):
        def at(step, carried):
            start = step * chunk
            body(pl.ds(start if isinstance(start, int) else pl.multiple_of(start, chunk), chunk), step)
            return carried

        if chunk == tokens:
            at(0, 0)
        else:
            lax.fori_loop(0, tokens // chunk, at, 0)

    def scale_of(block, rows, place):
        held = scale_s[rows, :]
        lane = iota(held.shape, 1)
        return jnp.sum(jnp.where(lane == 3 * block + place, held, 0.0), axis=1, keepdims=True)

    def keep_scale(block, rows, place, scale):
        held = scale_s[rows, :]
        scale_s[rows, :] = jnp.where(iota(held.shape, 1) == 3 * block + place, scale, held)

    def wide(values):
        return jnp.concatenate(values, axis=1)

    def both_heads(values):
        return jnp.concatenate([values * wide_masks[0], values * wide_masks[1]], axis=0)

    def both_pairs(values):
        zero = jnp.zeros((SUB, SUB), BF16)
        return jnp.concatenate([wide([values[:, :SUB], zero]), wide([zero, values[:, SUB:]])], axis=0)

    def forward(block, carried):
        after = jnp.minimum(block + 1, blocks - 1)
        if remote:
            links.arrive(block, (0, 1, 2))
            links.start_y(block == 0, range(3))
        condition(block)

        def self_attention(rows, step):
            x = pred_ref[rows, :].astype(F32)
            unit0, scale0 = normalize(x)
            unit_s[block, 0, rows, :] = low(unit0)
            a = low(unit0 * vec(block, 0) + vec(block, SHIFT))
            q = low((dot(a, weight(block, 0, cols)) + vec(block, SHIFT + 3)) * score_scale)
            k = low(dot(a, weight(block, cols, 2 * cols)))
            v = low(dot(a, weight(block, 2 * cols, 3 * cols)) + vec(block, SHIFT + 4))
            qkv_s[block, rows, :cols] = q
            qkv_s[block, rows, cols : 2 * cols] = k
            qkv_s[block, rows, 2 * cols :] = v
            causal2 = wide([causal_s[...]] * 2)
            parts = []
            for sub in range(rows.size // SUB):
                span = slice(sub * SUB, (sub + 1) * SUB)
                scores = dot_nt(both_pairs(k[span]), both_heads(q[span]))
                stacked = []
                for pair in range(2):
                    score = scores[pair * SUB : (pair + 1) * SUB] + causal2
                    top = jnp.max(score, axis=0, keepdims=True)
                    expo = jnp.exp(score - top)
                    prob = low(expo * (1.0 / jnp.sum(expo, axis=0, keepdims=True)))
                    prob_s[block, step * (rows.size // SUB) + sub, pair] = prob
                    stacked.append(over_heads(prob))
                both = dot_tn(wide(stacked), both_heads(v[span]))
                parts.append(low(wide([both[:SUB, :SUB], both[SUB:, SUB:]])))
            context = jnp.concatenate(parts, axis=0)
            ctx_s[block, rows, :] = context
            x = x + (dot(context, weight(block, W_SO, W_CKV)) + vec(block, SHIFT + 5))
            g_s[rows, :] = x
            keep_scale(block, rows, 0, scale0)
            if remote:
                links.pass_on(block, True, (1, 5), (2, 3), (2, 4))
                links.pass_on(after, block + 1 < blocks, (1, 0), (1, 1), (1, 2))
                links.start_y(block == 0, range(3, PIECES))


        each_chunk(FORWARD_SELF, self_attention)
        if remote:
            links.arrive(block, (3,))

        def cross_attention(rows, step):
            x = g_s[rows, :]
            unit1, scale1 = normalize(x)
            unit_s[block, 1, rows, :] = low(unit1)
            c = low(unit1 * vec(block, 1) + vec(block, SHIFT + 1))
            cq = low((dot(c, weight(block, W_CQ, W_CO)) + vec(block, SHIFT + 6)) * score_scale)
            cq_s[block, rows, :] = cq
            parts = []
            for sub in range(rows.size // SUB):
                index = step * (rows.size // SUB) + sub
                scores = thirds(dot_nt(wide_s[index, :, :cols], cq[sub * SUB : (sub + 1) * SUB]))
                top = jnp.maximum(jnp.maximum(scores[0], scores[1]), scores[2])
                expos = [jnp.exp(score - top) for score in scores]
                inverse = own_s[...] / (expos[0] + expos[1] + expos[2])
                prob = low(jnp.concatenate([expo * inverse for expo in expos], axis=0))
                cprob_s[block, index] = prob
                parts.append(low(dot_tn(prob, wide_s[index, :, cols:])))
            context = jnp.concatenate(parts, axis=0)
            cctx_s[block, rows, :] = context
            x = x + (dot(context, weight(block, W_CO, W_UP)) + vec(block, SHIFT + 8))
            unit2, scale2 = normalize(x)
            unit_s[block, 2, rows, :] = low(unit2)
            keep_scale(block, rows, 1, scale1)
            keep_scale(block, rows, 2, scale2)
            g_s[rows, :] = x + vec(block, SHIFT + 9)
            dy_s[0, rows, :] = low(unit2 * vec(block, 2) + vec(block, SHIFT + 2))
            if remote:
                links.pass_on(block, True, (2, 5))
                links.pass_on(after, block + 1 < blocks, (2, 0), (2, 1))

        each_chunk(FORWARD_CROSS, cross_attention)
        if remote:
            links.arrive(block, (4, 5))

        def feed_forward(rows, step):
            e = dy_s[0, rows, :]
            root = math.sqrt(2.0 / math.pi)
            cube = root * 0.044715
            for part in range(4):
                lanes = slice(part * cols, (part + 1) * cols)
                u = low(dot(e, weight(block, W_UP + part * cols, W_UP + (part + 1) * cols)) + vec(
                    block, BIAS + part
                ))
                square = u * u
                gate = jnp.tanh(u * (square * low(cube) + low(root))) * low(0.5) + low(0.5)
                hidden = u * gate
                slope = gate + hidden * (low(1.0) - gate) * (square * low(6.0 * cube) + low(2.0 * root))
                hid_s[block % ring, rows, lanes] = hidden
                slope_s[block % ring, rows, lanes] = slope
            pred_ref[rows, :] = low(g_s[rows, :] + dot(hid_s[block % ring, rows, :], wd_s[block]))
            if remote:
                links.pass_on(after, block + 1 < blocks, (2, 2), (1, 3), (1, 4))

        @pl.when(block == ring)
        def _():
            for copy in out_copies:
                copy.wait()

        each_chunk(FORWARD_FF, feed_forward)

        @pl.when(block == 0)
        def _():
            for copy in out_copies:
                copy.start()

        return carried

    if remote:
        links.pass_on(0, True, (1, 0), (1, 1), (2, 0), (1, 2), (2, 1), (1, 3), (2, 2), (1, 4))
    lax.fori_loop(0, blocks, forward, 0)

    def put(kind, start, value):
        width, taken = WIDTHS[kind], 0
        while taken < value.shape[1]:
            index, place = (start + taken) // width, (start + taken) % width
            count = min(value.shape[1] - taken, width - place)
            part = low(value[:, taken : taken + count]).reshape(NZ, NX, ROWS, count)
            groups[kind][index, :, :, :, place : place + count] = part
            taken += count

    def emit(block, kind):
        if remote:
            links.near(kind).start()
        else:
            copy = pltpu.make_async_copy(groups[kind], dw_refs[kind].at[block], load_sem.at[2])
            copy.start()
            copy.wait()

    def store_down(first, second):
        blocks_of = [value[:, q * SUB : (q + 1) * SUB] for value in (first, second) for q in range(4)]
        dn_out[...] = jnp.transpose(jnp.concatenate(blocks_of, axis=0))

    def store_up(first, second):
        up_out[...] = wide([first, second])

    def store_cross(first, second):
        joined = wide([first, second])
        ckv_out[...] = joined[:, : 2 * cols]
        for place, out in enumerate((cq_out, co_out, so_out)):
            out[...] = joined[:, (2 + place) * cols : (3 + place) * cols]

    def store_self(first, second):
        in_out[...] = wide([first, second])

    stores = (store_down, store_up, store_cross, store_self)

    def advance(works):
        if not remote:
            return
        for kind, stage, block, there in works:

            def run(kind=kind, stage=stage, block=block):
                if stage == 1:
                    links.after_near(kind)
                elif stage == 2:
                    links.after_row(kind)
                elif stage == 3:
                    links.after_far(kind, block)
                else:
                    links.after_last(kind, block, stores[kind])

            if there is True:
                run()
            else:
                pl.when(there)(run)

    def time_gradient():
        dmem = dmem_s[...]
        dmem_high = low(dmem)
        dmem_low = low(dmem - dmem_high.astype(F32))
        return dot_tn(sinus_s[...], dmem_high) + dot_tn(sinus_s[...], dmem_low)

    def emit_vectors():
        vectors = dvec_s[...].reshape(blocks * VEC_ROWS, cols)
        vectors = jnp.concatenate([vectors, jnp.zeros((SUB - blocks * VEC_ROWS, cols), F32)], axis=0)
        turned = jnp.transpose(vectors).reshape(GROUPS, ROWS, SUB)
        lane = iota((ROWS, SUB), 1) % VEC_ROWS
        rows_out = []
        for group in range(GROUPS):
            part, high = group // 2, group % 2
            piece = turned[group]
            for j in range(4):
                source = turned[4 * high + j]
                if j != part:
                    source = pltpu.roll(source, (j - part) % SUB, 1)
                piece = jnp.where(lane == BIAS + j, source, piece)
            rows_out.append(piece)
        turned = jnp.concatenate(rows_out, axis=0)
        for index in range(2):
            sets[VECTOR][0][index] = low(turned).reshape(NZ, NX, ROWS, SUB)
        links.near(VECTOR).start()

    def backward(turn, carried):
        block = blocks - 1 - turn
        earlier, before = block + 1, block + 2
        again, third_turn = turn > 0, turn > 1

        def add_vec(row, values):
            dvec_s[block, row : row + 1, :] += values

        def turn_over_ones(left):
            return jnp.concatenate([jnp.transpose(left), jnp.ones((16, tokens), BF16)], axis=0)

        def put_scaled(kind, start, unit_row, right, sum_rows):
            turned = turn_over_ones(unit_s[block, unit_row])
            gain = place_column(vec(block, unit_row))
            shift = place_column(vec(block, SHIFT + unit_row))
            parts = []
            for place, row in enumerate(sum_rows):
                both = dot(turned, right[:, place * cols : (place + 1) * cols])
                sums = both[cols : cols + 1]
                dvec_s[block, row : row + 1, :] = sums
                put(kind, start + place * cols, both[:cols] * gain + shift * sums)
                parts.append((both[:cols], sums))
            return parts

        def put_plain(kind, start, left, right, row):
            both = dot(turn_over_ones(left), right)
            dvec_s[block, row : row + 1, :] = both[cols : cols + 1]
            put(kind, start, both[:cols])

        @pl.when(block == 0)
        def _():
            for copy in back_copies:
                copy.wait()

        turned = jnp.transpose(grad_ref[...])
        for part in range(4):
            piece = low(dot(turned, hid_s[block % ring, :, part * cols : (part + 1) * cols]))
            for index in range(2):
                for x in range(NX):
                    for q in range(4):
                        row = SUB * index + ROWS * q
                        groups[DOWN][index, part, x, :, q * SUB : (q + 1) * SUB] = piece[
                            row : row + ROWS, x * SUB : (x + 1) * SUB
                        ]
        def feed_forward(rows, step):
            dy3 = grad_ref[rows, :]
            g = dy3.astype(F32)
            add_vec(SHIFT + 9, jnp.sum(g, axis=0, keepdims=True))
            for part in range(4):
                lanes = slice(part * cols, (part + 1) * cols)
                dh = dot_nt(dy3, wd_s[block, lanes, :])
                slope_s[block % ring, rows, lanes] = low(dh) * slope_s[block % ring, rows, lanes]
            de = dot_nt(slope_s[block % ring, rows, :], weight(block, W_UP, W_END))
            back, along, flat = normalize_back(
                de, unit_s[block, 2, rows, :].astype(F32), scale_of(block, rows, 2), vec(block, 2)
            )
            add_vec(2, along)
            add_vec(SHIFT + 2, flat)
            g = g + back
            g_s[rows, :] = g
            dy_s[0, rows, :] = low(g)

        each_chunk(BACK_FF, feed_forward)
        advance((
            (DOWN, 3, earlier, again), (CROSS, 2, earlier, again), (SELF, 1, earlier, again),
            (CROSS, 4, before, third_turn), (SELF, 4, before, third_turn),
        ))
        emit(block, DOWN)
        pl.when(turn == 0)(back_copies[0].start)

        put_scaled(UP, 0, 2, slope_s[block % ring], [BIAS + part for part in range(4)])
        condition(block)
        emit(block, UP)
        pl.when(turn == 0)(back_copies[1].start)

        def cross_attention(rows, step):
            dctx = low(dot_nt(dy_s[0, rows, :], weight(block, W_CO, W_UP)))
            for sub in range(rows.size // SUB):
                index = step * (rows.size // SUB) + sub
                span = pl.ds(index * SUB if isinstance(index, int) else pl.multiple_of(index * SUB, SUB), SUB)
                keys, vals = wide_s[index, :, :cols], wide_s[index, :, cols:]
                part = dctx[sub * SUB : (sub + 1) * SUB]
                prob = cprob_s[block, index]
                prob32 = prob.astype(F32)
                weighted = prob32 * dot_nt(vals, part)
                inner = sum(thirds(weighted))
                dscore = low(weighted - prob32 * jnp.concatenate([inner] * 3, axis=0))
                folded_s[index, :, :cols] = fold(dot(dscore, cq_s[block, span, :]))
                folded_s[index, :, cols:] = fold(dot(prob, part))
                cq_s[block, span, :] = low(dot_tn(dscore, keys) * score_scale)
            dcq = cq_s[block, rows, :]
            dc = dot_nt(dcq, weight(block, W_CQ, W_CO))
            back, along, flat = normalize_back(
                dc, unit_s[block, 1, rows, :].astype(F32), scale_of(block, rows, 1), vec(block, 1)
            )
            add_vec(1, along)
            add_vec(SHIFT + 1, flat)
            g = g_s[rows, :] + back
            g_s[rows, :] = g
            dy_s[1, rows, :] = low(g)

        each_chunk(BACK_CROSS, cross_attention)
        advance(((DOWN, 1, block, True), (DOWN, 4, earlier, again), (UP, 3, earlier, again)))

        folded = folded_s[...].reshape(-1, 2 * cols)
        dkv32 = dot(turned_s[:, : folded.shape[0]], low(folded))
        dkv = low(dkv32)
        add_vec(SHIFT + 7, jnp.sum(dkv32[:, cols:], axis=0, keepdims=True))
        dmem_s[...] += dot_nt(dkv[:samples], weight(block, W_CKV, W_CQ))
        put(CROSS, 0, dot_tn(tok_s[...], dkv))
        put_scaled(CROSS, 2 * cols, 1, cq_s[block], [SHIFT + 6])
        put_plain(CROSS, 3 * cols, cctx_s[block], dy_s[0], SHIFT + 8)
        put_plain(CROSS, 4 * cols, ctx_s[block], dy_s[1], SHIFT + 5)
        advance(((SELF, 2, earlier, again), (UP, 1, block, True)))
        emit(block, CROSS)
        if remote:

            @pl.when(block == 0)
            def _():
                dtime = time_gradient()
                for index in range(2):
                    part = low(dtime[:, index * SUB : (index + 1) * SUB])
                    sets[TIME][0][index] = part.reshape(NZ, NX, ROWS, SUB)
                links.near(TIME).start()

        def self_attention(rows, step):
            dctx = low(dot_nt(dy_s[1, rows, :], weight(block, W_SO, W_CKV)))
            for sub in range(rows.size // SUB):
                index = step * (rows.size // SUB) + sub
                span = pl.ds(index * SUB if isinstance(index, int) else pl.multiple_of(index * SUB, SUB), SUB)
                part = dctx[sub * SUB : (sub + 1) * SUB]
                queries, keys, values = (qkv_s[block, span, place * cols : (place + 1) * cols] for place in range(3))
                sides = (slice(0, SUB), slice(SUB, 2 * SUB))
                dstack = both_heads(part)
                qstack = both_heads(queries)
                kstack = both_heads(keys)
                probs = [prob_s[block, index, pair] for pair in range(2)]
                dprobs = dot_nt(both_pairs(values), dstack)
                dprobs = [dprobs[side] for side in sides]
                dscores = []
                for prob, dprob in zip(probs, dprobs):
                    prob32 = prob.astype(F32)
                    weighted = prob32 * dprob
                    dscores.append(low(weighted - prob32 * jnp.sum(weighted, axis=0, keepdims=True)))
                dq = dot_tn(wide([over_heads(dscore) for dscore in dscores]), kstack)
                dq = [dq[side, side] for side in sides]
                dk = dot(jnp.concatenate(dscores, axis=0), qstack)
                dk = [dk[side, side] for side in sides]
                dv = dot(jnp.concatenate(probs, axis=0), dstack)
                dv = [dv[side, side] for side in sides]
                qkv_s[block, span, :cols] = low(wide(dq) * score_scale)
                qkv_s[block, span, cols : 2 * cols] = low(wide(dk))
                qkv_s[block, span, 2 * cols :] = low(wide(dv))

        each_chunk(BACK_SELF, self_attention)
        advance((
            (CROSS, 3, earlier, again), (SELF, 3, earlier, again), (DOWN, 2, block, True),
            (CROSS, 1, block, True), (TIME, 1, block, block == 0), (UP, 4, earlier, again),
        ))

        gain_column, shift_column = 0.0, 0.0
        for place, (both, sums) in enumerate(
            put_scaled(SELF, 0, 0, qkv_s[block], (SHIFT + 3, KEYSUM, SHIFT + 4))
        ):
            matrix = weight(block, place * cols, (place + 1) * cols).astype(F32)
            gain_column += jnp.sum(both * matrix, axis=1, keepdims=True)
            shift_column += jnp.sum(sums * matrix, axis=1, keepdims=True)
        dvec_s[block, 0:1, :] = place_row(gain_column)
        dvec_s[block, SHIFT : SHIFT + 1, :] = place_row(shift_column)
        emit(block, SELF)
        if remote:
            pl.when(block == 0)(emit_vectors)

        def self_norm(rows, step):
            da = dot_nt(qkv_s[block, rows, :], weight(block, 0, 3 * cols))
            back, _, _ = normalize_back(
                da, unit_s[block, 0, rows, :].astype(F32), scale_of(block, rows, 0), vec(block, 0)
            )
            grad_ref[rows, :] = low(g_s[rows, :] + back)

        each_chunk(BACK_SELF, self_norm)
        advance(((UP, 2, block, True),))
        return carried

    lax.fori_loop(0, blocks, backward, 0)
    if not remote:
        time_out[...] = time_gradient()
        dvec_ref[...] = dvec_s[...]
        return

    links.after_last(CROSS, 1, store_cross)
    links.after_last(SELF, 1, store_self)
    links.after_near(SELF)
    links.after_near(VECTOR)
    links.after_far(DOWN, 0)
    links.after_row(CROSS)
    links.after_row(TIME)
    links.after_far(UP, 0)
    links.after_last(DOWN, 0, store_down)
    links.after_row(SELF)
    links.after_row(VECTOR)
    links.after_far(CROSS, 0)
    links.after_far_all(TIME)
    links.after_last(UP, 0, store_up)
    links.after_far(SELF, 0)
    links.after_far_all(VECTOR)
    links.after_last(CROSS, 0, store_cross)
    time_out[...] = wide(links.after_last_all(TIME))
    links.after_last(SELF, 0, store_self)
    mine, _ = links.after_last_all(VECTOR)
    padded = jnp.concatenate([mine, jnp.zeros((SUB - ROWS, SUB), F32)], axis=0)
    flat_s[...] = jnp.transpose(padded)
    mine = flat_s[pl.ds(pl.multiple_of(section * VEC_ROWS, 8), VEC_ROWS), :]
    for row in range(SHIFT):
        gains_out[row] = mine[row : row + 1, :ROWS]
    for row in range(SHIFT, BIAS):
        shifts_out[row - SHIFT] = mine[row : row + 1, :ROWS]
    bias = mine[BIAS : BIAS + 1, :]
    for part in range(1, 4):
        bias = bias + pltpu.roll(mine[BIAS + part : BIAS + part + 1, :], part * ROWS, 1)
    bias_out[...] = bias
    links.finish_weights()


def run_blocks(remote, x, cot, obs, repeat, noise, time_weight, *weights, interpret=False):
    tokens, cols = x.shape
    blocks = 4
    samples = noise.shape[1]
    vmem = pl.BlockSpec(memory_space=pltpu.VMEM)
    hbm = pl.BlockSpec(memory_space=pl.ANY)
    half_rows = (NZ, NX, ROWS)
    scratch = [
        pltpu.VMEM((blocks, 3, tokens, cols), BF16),
        pltpu.VMEM((tokens, SUB), F32),
        pltpu.VMEM((blocks, tokens, 3 * cols), BF16),
        pltpu.VMEM((blocks, tokens // SUB, 2, SUB, 2 * SUB), BF16),
        pltpu.VMEM((blocks, tokens, cols), BF16),
        pltpu.VMEM((blocks, tokens, cols), BF16),
        pltpu.VMEM((blocks, tokens // SUB, WIDE, SUB), BF16),
        pltpu.VMEM((blocks, tokens, cols), BF16),
        pltpu.VMEM((blocks - 1, tokens, 4 * cols), BF16),
        pltpu.VMEM((blocks - 1, tokens, 4 * cols), BF16),
        pltpu.VMEM((2, tokens, cols), BF16),
        pltpu.VMEM((tokens, cols), F32),
        pltpu.VMEM((blocks, cols, W_END), BF16),
        pltpu.VMEM((blocks, 4 * cols, cols), BF16),
        pltpu.VMEM((blocks, VEC_ROWS, cols), F32),
        pltpu.VMEM((blocks, VEC_ROWS, cols), F32),
        pltpu.VMEM((tokens // SUB * KEYS, SUB), BF16),
        pltpu.VMEM((SUB, 2 * SUB), BF16),
        pltpu.VMEM((SUB, cols), BF16),
        pltpu.VMEM((tokens // SUB, WIDE, 2 * cols), BF16),
        pltpu.VMEM((tokens // SUB, KEYS, 2 * cols), F32),
        pltpu.VMEM((samples, cols), F32),
        pltpu.VMEM((samples, cols), BF16),
        pltpu.VMEM((SUB, SUB), F32),
        pltpu.VMEM((WIDE // 3, SUB), F32),
        pltpu.VMEM((SUB, SUB), F32),
        pltpu.SemaphoreType.DMA((12,)),
    ]
    scratch += [pltpu.VMEM((2,) + half_rows + (width,), BF16) for width in WIDTHS[:TIME]]
    if remote:
        scratch += [pltpu.SemaphoreType.DMA((5 * PIECES + 3,))] * 2
        for kind, width in enumerate(WIDTHS):
            if kind >= TIME:
                scratch.append(pltpu.VMEM((2,) + half_rows + (width,), BF16))
            scratch += [
                pltpu.VMEM(half_rows + (width,), BF16),
                pltpu.VMEM((NZ, ROWS, width), BF16),
                pltpu.VMEM((NZ - 1, ROWS, width), BF16),
                pltpu.VMEM((3, ROWS, width), BF16),
                pltpu.VMEM((ROWS, width), BF16),
                pltpu.VMEM((NZ, ROWS, width), BF16),
                pltpu.SemaphoreType.DMA((4 + NZ,)),
                pltpu.SemaphoreType.DMA((4 + NZ,)),
            ]
        shapes = ((ROWS, 3 * cols), (ROWS, cols), (ROWS, cols), (ROWS, 2 * cols), (ROWS, cols),
                  (ROWS, 4 * cols), (4 * ROWS, cols), (SHIFT, 1, ROWS), (BIAS - SHIFT, 1, ROWS), (1, 4 * ROWS),
                  (ROWS, cols))
        outs = tuple(jax.ShapeDtypeStruct(shape, F32) for shape in shapes)
        in_specs = [hbm, hbm] + [vmem] * 4 + [hbm] * 7 + [vmem] * 3
        out_specs = (vmem,) * (2 + len(outs))
        params = pltpu.CompilerParams(
            vmem_limit_bytes=VMEM_BYTES, collective_id=0, has_side_effects=True)
    else:
        outs = (
            jax.ShapeDtypeStruct((blocks, VEC_ROWS, cols), F32),
            jax.ShapeDtypeStruct((cols, cols), F32),
        )
        outs = tuple(
            jax.ShapeDtypeStruct((blocks, 2) + half_rows + (width,), BF16) for width in WIDTHS[:TIME]
        ) + outs
        in_specs = [hbm, hbm] + [vmem] * 4 + [hbm] * 3
        out_specs = (vmem, vmem) + (hbm,) * 4 + (vmem, vmem)
        params = pltpu.CompilerParams(vmem_limit_bytes=VMEM_BYTES)
    low_out = jax.ShapeDtypeStruct((tokens, cols), BF16)
    away = jax.ShapeDtypeStruct((tokens, 4 * cols), BF16)
    return pl.pallas_call(
        functools.partial(block_kernel, remote),
        out_shape=(low_out, low_out) + outs + (away, away),
        in_specs=in_specs,
        out_specs=out_specs + (hbm, hbm),
        scratch_shapes=scratch,
        compiler_params=params,
        interpret=interpret,
    )(x, cot, obs, repeat, noise, time_weight, *weights)


def hand_out(*refs):
    count = (len(refs) - 1) // 3
    held, sem = refs[2 * count : 3 * count], refs[-1]
    arriving = [pltpu.make_async_copy(refs[i], held[i], sem.at[i]) for i in range(count)]
    leaving = []
    for copy in arriving:
        copy.start()
    for index in range(count):
        target = refs[count + index]
        if len(target.shape) > len(held[index].shape):
            target = target.at[0]
        arriving[index].wait()
        leaving.append(pltpu.make_async_copy(held[index], target, sem.at[index]))
        leaving[-1].start()
    for copy in leaving:
        copy.wait()


def finished(results):
    hbm = pl.BlockSpec(memory_space=pl.ANY)
    shapes = [(1,) + result.shape for result in results[:9]] + [result.shape for result in results[9:]]
    return pl.pallas_call(
        hand_out,
        out_shape=tuple(jax.ShapeDtypeStruct(shape, result.dtype) for shape, result in zip(shapes, results)),
        in_specs=[hbm] * len(results),
        out_specs=(hbm,) * len(results),
        scratch_shapes=[pltpu.VMEM(result.shape, result.dtype) for result in results]
        + [pltpu.SemaphoreType.DMA((len(results),))],
    )(*results)


def pack_weights(self_in, self_out, cross_q, cross_kv, cross_out, mlp_up, mlp_down):
    parts = (self_in, self_out, cross_kv, cross_q, cross_out, mlp_up)
    return jnp.concatenate([part[0] for part in parts], axis=1), mlp_down[0]


def pack_vectors(gains, shifts, mlp_bias):
    cols = gains.shape[-1]
    rows = jnp.concatenate([gains[0], shifts[0], mlp_bias.reshape(4, cols)], axis=0)
    return jnp.pad(rows, ((0, VEC_ROWS - rows.shape[0]), (0, 0)))


def natural(dweights):
    def joined(kind):
        parts = dweights[kind].reshape(-1, 2, GROUPS * ROWS, WIDTHS[kind])
        return jnp.concatenate([parts[:, 0], parts[:, 1]], axis=-1)

    blocks = dweights[DOWN].shape[0]
    down = dweights[DOWN].reshape(blocks, 2, GROUPS, ROWS, 4, SUB).transpose(0, 2, 5, 1, 4, 3)
    return joined(UP), joined(CROSS), joined(SELF), down.reshape(blocks, GROUPS * SUB, -1)


def gathered(data, packed_weights, packed_vectors):
    sections = lax.axis_size("section")
    groups = lax.axis_size("dp")
    cols = data[0].shape[-1]
    weights = [lax.all_gather(part, "section", axis=0) for part in packed_weights]
    vectors = lax.all_gather(packed_vectors, "section", axis=0)
    pred, grad, *dweights, dvectors, dtime, _, _ = run_blocks(False, *data, *weights, vectors)
    rows = cols // groups
    up, cross, own, down = natural(dweights)
    rest = jnp.concatenate([up, cross, own], axis=2).reshape(sections, groups, -1)
    down = down.reshape(sections, groups, -1)
    small = dvectors[:, :BIAS].reshape(sections, BIAS, groups, rows).transpose(0, 2, 1, 3)
    small = small.reshape(sections, groups, BIAS * rows)
    bias = dvectors[:, BIAS:KEYSUM].reshape(sections, groups, 4 * rows)
    term = jnp.broadcast_to(dtime.reshape(1, groups, rows * cols), (sections, groups, rows * cols))
    sent = jnp.concatenate([rest, down], axis=2).reshape(sections * groups, -1)
    sent_small = jnp.concatenate([small, bias, term], axis=2).reshape(sections * groups, -1)
    got = lax.psum_scatter(sent, ("section", "dp"), scatter_dimension=0, tiled=True)[0].astype(F32)
    got_small = lax.psum_scatter(sent_small, ("section", "dp"), scatter_dimension=0, tiled=True)[0]
    widths = (up.shape[-1], cross.shape[-1], own.shape[-1])
    split = sum(widths) * rows
    rest = got[:split].reshape(rows, sum(widths))
    down = got[split:].reshape(4 * rows, cols)
    small = got_small[: BIAS * rows].reshape(BIAS, rows)
    bias = got_small[BIAS * rows : (BIAS + 4) * rows].reshape(4, rows)
    term = got_small[(BIAS + 4) * rows :].reshape(rows, cols)
    up, cross, own = jnp.split(rest, (widths[0], widths[0] + widths[1]), axis=1)
    kv, query, out, self_out = jnp.split(cross, (2 * cols, 3 * cols, 4 * cols), axis=1)
    return (pred, grad, own, self_out, query, kv, out, up, down, small[:SHIFT], small[SHIFT:], bias, term)


def local(
    horizon, cotangent, obs_tokens, obs_repeat, noise_step, time_weight,
    self_in, self_out, cross_q, cross_kv, cross_out, mlp_up, mlp_down, gains, shifts, mlp_bias,
):
    cols = horizon.shape[-1]
    data = (horizon[0], cotangent[0], obs_tokens[0], obs_repeat, noise_step, time_weight)
    weights = (self_in, self_out, cross_q, cross_kv, cross_out, mlp_up, mlp_down)
    if lax.axis_size("dp") == GROUPS:
        vectors = (gains.transpose(1, 0, 2), shifts.transpose(1, 0, 2), mlp_bias)
        results = finished(run_blocks(True, *data, *weights, *vectors)[:-2])
        return results[:9] + (results[9].transpose(1, 0, 2), results[10].transpose(1, 0, 2)) + results[11:]
    results = gathered(data, pack_weights(*weights), pack_vectors(gains, shifts, mlp_bias))
    return tuple(result[None] for result in results[:11]) + (results[11].reshape(1, -1), results[12])


def solution(mesh):
    whole = P("section", None, None)
    return jax.shard_map(
        local,
        mesh=mesh,
        in_specs=(
            P("section", "dp", None), P("section", "dp", None), P("section", "dp", None, None),
            P(None, "dp", None), P(None, "dp"), P(),
            whole, whole, whole, whole, whole, whole, whole, whole, whole, P("section", None),
        ),
        out_specs=(P("section", "dp", None),) * 9
        + (P("section", None, "dp"), P("section", None, "dp"), P("section", "dp"), P("dp", None)),
        check_vma=False,
    )
```

```python
import functools
import math

import jax
import jax.numpy as jnp
from jax import lax
from jax.experimental import pallas as pl
from jax.experimental.pallas import tpu as pltpu
from jax.sharding import PartitionSpec as P

HEADS = 4
VMEM_BYTES = 63 * 1024 * 1024
SUB = 128
F32 = jnp.float32
BF16 = jnp.bfloat16

W_IN, W_SO, W_CKV, W_CQ, W_CO, W_UP, W_END = 0, 768, 1024, 1536, 1792, 2048, 3072
SHIFT, BIAS, KEYSUM, VEC_ROWS = 3, 13, 17, 24
SENT = ((W_IN, 512), (512, W_CKV), (W_CKV, W_CQ), (W_CQ, W_UP), (W_UP, W_END))
DOWN_PIECE, PIECES = 5, 6
DOWN, UP, CROSS, SELF, TIME, VECTOR = range(6)
WIDTHS = (512, 512, 640, 384, 128, 128)
FORWARD_SELF, FORWARD_CROSS, FORWARD_FF = 1024, 1024, 1024
BACK_FF, BACK_CROSS, BACK_SELF = 1024, 1024, 1024
ROWS, NZ, NX = 32, 4, 2
TURNS = (UP, SELF)
GROUPS = NZ * NX
KEYS, WIDE = 24, 96


def dot(left, right):
    return jnp.dot(left, right, preferred_element_type=F32)


def dot_nt(left, right):
    return lax.dot_general(left, right, (((1,), (1,)), ((), ())), preferred_element_type=F32)


def dot_tn(left, right):
    return lax.dot_general(left, right, (((0,), (0,)), ((), ())), preferred_element_type=F32)


def iota(shape, axis):
    return lax.broadcasted_iota(jnp.int32, shape, axis)


def low(values):
    return jnp.asarray(values, BF16)


def normalize(values):
    center = values - jnp.mean(values, axis=-1, keepdims=True)
    scale = lax.rsqrt(jnp.mean(center * center, axis=-1, keepdims=True) + 1e-05)
    return center * scale, scale


def normalize_back(grad, unit, scale, gain):
    ahead = grad * unit
    grad_unit = grad * gain
    mean_grad = jnp.mean(grad_unit, axis=-1, keepdims=True)
    mean_along = jnp.mean(ahead * gain, axis=-1, keepdims=True)
    back = (grad_unit - mean_grad - unit * mean_along) * scale
    return back, jnp.sum(ahead, axis=0, keepdims=True), jnp.sum(grad, axis=0, keepdims=True)


def half_masks():
    lane = iota((1, SUB), 1)
    first = (lane < SUB // 2).astype(F32)
    return low(first), low(1.0 - first)


def add_low(left, right):
    return left + right


def place_row(column):
    size = column.shape[0]
    diagonal = iota((size, size), 0) == iota((size, size), 1)
    return jnp.sum(jnp.where(diagonal, column, 0.0), axis=0, keepdims=True)


def place_column(row):
    size = row.shape[1]
    diagonal = iota((size, size), 0) == iota((size, size), 1)
    return jnp.sum(jnp.where(diagonal, row, 0.0), axis=1, keepdims=True)


class Links:
    def __init__(self, w_s, wd_s, vec_s, wsend, wrecv, sets):
        self.w, self.wd, self.vec, self.wsend, self.wrecv, self.sets = w_s, wd_s, vec_s, wsend, wrecv, sets
        self.section = lax.axis_index("section")
        self.group = lax.axis_index("dp")
        self.core, self.y = self.section % 2, self.section // 2
        self.x, self.z = self.group % NX, self.group // NX
        self.x_peer = self.z * NX + (self.x + 1) % NX

    def relative(self, step):
        return (self.y + step // 2) % 2 * 2 + (self.core + step % 2) % 2

    def relation(self, block):
        return (self.y + block // 2) % 2 * 2 + (self.core + block % 2) % 2

    def z_peer(self, step):
        return (self.z + step) % NZ * NX + self.x

    def greet(self):
        barrier = pltpu.get_barrier_semaphore()
        peers = [{"section": self.relative(step)} for step in (1, 2, 3)]
        peers += [{"dp": self.x_peer}] + [{"dp": self.z_peer(step)} for step in range(1, NZ)]
        for peer in peers:
            pl.semaphore_signal(barrier, inc=1, device_id=peer, device_id_type=pl.DeviceIdType.MESH)
        pl.semaphore_wait(barrier, len(peers))

    def remote(self, src, dst, send, recv, peer):
        return pltpu.make_async_remote_copy(
            src_ref=src, dst_ref=dst, send_sem=send, recv_sem=recv, device_id=peer,
            device_id_type=pl.DeviceIdType.MESH,
        )

    def weight_copy(self, slot, block, piece, half, peer):
        array, lanes = (self.wd, slice(None)) if piece == DOWN_PIECE else (self.w, slice(*SENT[piece]))
        part = array.at[block, :, lanes]
        if half is not None:
            rows = array.shape[1] // 2
            part = array.at[block, pl.ds(pl.multiple_of(half * rows, rows), rows), lanes]
        return self.remote(part, part, self.wsend.at[slot], self.wrecv.at[slot], peer)

    def vector_copy(self, slot, block, peer):
        part = self.vec.at[block]
        return self.remote(part, part, self.wsend.at[slot], self.wrecv.at[slot], peer)

    def to_sibling(self, piece, block):
        return self.weight_copy(piece, block, piece, None, {"section": self.relative(1)})

    def over_y(self, piece, block):
        return self.weight_copy(PIECES + piece, block, piece, self.x, {"section": self.relative(2)})

    def over_x(self, piece, block, half):
        return self.weight_copy(2 * PIECES + piece, block, piece, half, {"dp": self.x_peer})

    def forwarded(self, piece, block, half, which):
        return self.weight_copy((3 + which) * PIECES + piece, block, piece, half, {"section": self.relative(1)})

    def vectors(self, step, block, peer):
        return self.vector_copy(5 * PIECES + step, block, {"section": peer})

    def start_y(self, when, pieces):
        @pl.when(when & (self.core == 1))
        def _():
            for piece in pieces:
                self.over_y(piece, self.section).start()

    def pass_first(self, piece, block):
        self.over_y(piece, block).wait_recv()
        self.over_x(piece, block, self.x).start()
        self.forwarded(piece, block, self.x, 0).start()

    def pass_second(self, piece, block):
        self.over_x(piece, block, 1 - self.x).wait_recv()
        self.forwarded(piece, block, 1 - self.x, 1).start()

    def pass_on(self, block, when, *works):
        @pl.when(self.relation(block) == 2 if when is True else when & (self.relation(block) == 2))
        def _():
            for stage, piece in works:
                if stage == 1 and piece == 0:
                    self.vectors(1, block, self.relative(2)).wait_recv()
                    self.vectors(2, block, self.relative(1)).start()
                (self.pass_first if stage == 1 else self.pass_second)(piece, block)

    def arrive(self, block, pieces):
        relation = self.relation(block)

        @pl.when(relation == 1)
        def _():
            if 0 in pieces:
                self.vectors(0, block, self.relative(1)).wait_recv()
            for piece in pieces:
                self.to_sibling(piece, block).wait_recv()

        @pl.when(relation == 3)
        def _():
            if 0 in pieces:
                self.vectors(2, block, self.relative(1)).wait_recv()
            for piece in pieces:
                self.forwarded(piece, block, self.x, 0).wait_recv()
                self.forwarded(piece, block, 1 - self.x, 1).wait_recv()

    def finish_weights(self):
        own, passed = self.section, self.relative(2)
        self.vectors(0, own, self.relative(1)).wait_send()
        self.vectors(1, own, self.relative(2)).wait_send()
        self.vectors(2, passed, self.relative(1)).wait_send()
        for piece in range(PIECES):
            self.to_sibling(piece, own).wait_send()
            self.over_y(piece, own).wait_send()
            self.over_x(piece, passed, self.x).wait_send()
            self.forwarded(piece, passed, self.x, 0).wait_send()
            self.forwarded(piece, passed, 1 - self.x, 1).wait_send()

    def near(self, kind):
        group_s, near_s, _, _, _, _, _, send, recv = self.sets[kind]
        return self.remote(group_s.at[1 - self.core], near_s, send.at[0], recv.at[0],
                           {"section": self.relative(1)})

    def row(self, kind):
        group_s, _, row_s, _, _, _, _, send, recv = self.sets[kind]
        return self.remote(group_s.at[self.core, :, 1 - self.x], row_s, send.at[1], recv.at[1],
                           {"dp": self.x_peer})

    def far_slot(self, kind, step, block):
        return (block % 2) * (NZ - 1) + step - 1 if kind in TURNS else step - 1

    def far(self, kind, step, block):
        far_s, _, _, fold_s, send, recv = self.sets[kind][3:]
        slot = self.far_slot(kind, step, block)
        sem = slot + 2 if kind not in TURNS else 1 + step + (block % 2) * (NZ + 2)
        return self.remote(fold_s.at[(self.z + step) % NZ], far_s.at[slot], send.at[sem], recv.at[sem],
                           {"dp": self.z_peer(step)})

    def last(self, kind, step, peer):
        last_s, sum_s, _, send, recv = self.sets[kind][4:]
        slot = NZ + step
        return self.remote(sum_s, last_s.at[step - 1],
                           send.at[slot], recv.at[slot], {"section": peer})

    def after_near(self, kind):
        group_s, near_s = self.sets[kind][:2]
        self.near(kind).wait()
        group_s[self.core] = add_low(group_s[self.core], near_s[...])
        self.row(kind).start()

    def after_row(self, kind, block):
        group_s, row_s, fold_s = self.sets[kind][0], self.sets[kind][2], self.sets[kind][6]
        self.row(kind).wait()
        fold_s[...] = add_low(group_s[self.core, :, self.x], row_s[...])
        for step in range(1, NZ):
            self.far(kind, step, block).start()

    def sum_far(self, kind, block):
        far_s, _, sum_s, fold_s = self.sets[kind][3:7]
        for step in range(1, NZ):
            self.far(kind, step, block).wait()
        total = fold_s[self.z].astype(F32)
        for step in range(1, NZ):
            total = total + far_s[self.far_slot(kind, step, block)].astype(F32)
        sum_s[...] = low(total)

    def after_far(self, kind, block):
        self.sum_far(kind, block)
        relation = self.relation(block)

        @pl.when(relation > 0)
        def _():
            self.last(kind, relation, block).start()

    def halves(self, kind):
        last_s, sum_s = self.sets[kind][4:6]
        here = sum_s[...].astype(F32) + last_s[1].astype(F32)
        there = last_s[0].astype(F32) + last_s[2].astype(F32)
        return jnp.where(self.core == 0, here, there), jnp.where(self.core == 0, there, here)

    def after_last(self, kind, block, store):
        relation = self.relation(block)

        @pl.when(relation > 0)
        def _():
            self.last(kind, relation, block).wait_send()

        @pl.when(relation == 0)
        def _():
            for step in (1, 2, 3):
                self.last(kind, step, self.relative(step)).wait_recv()
            store(*self.halves(kind))

    def after_far_all(self, kind):
        self.sum_far(kind, 0)
        for step in (1, 2, 3):
            self.last(kind, step, self.relative(step)).start()

    def after_last_all(self, kind):
        for step in (1, 2, 3):
            self.last(kind, step, self.relative(step)).wait()
        return self.halves(kind)


def block_kernel(remote, *refs):
    (x_ref, cot_ref, obs_ref, repeat_ref, noise_ref, tw_ref), refs = refs[:6], refs[6:]
    if remote:
        in_refs, refs = refs[:10], refs[10:]
        (pred_ref, grad_ref, in_out, so_out, cq_out, ckv_out, co_out, up_out, dn_out,
         gains_out, shifts_out, bias_out, time_out, hid_hbm, slope_hbm), refs = refs[:15], refs[15:]
    else:
        (w_hbm, wd_hbm, vec_hbm), refs = refs[:3], refs[3:]
        (pred_ref, grad_ref), dw_refs, refs = refs[:2], refs[2:6], refs[6:]
        (dvec_ref, time_out, hid_hbm, slope_hbm), refs = refs[:4], refs[4:]
    (unit_s, scale_s, qkv_s, prob_s, ctx_s, cq_s, cprob_s, cctx_s, hid_s, slope_s, dy_s, g_s,
     w_s, wd_s, vec_s, dvec_s, select_s, turned_s, tok_s, wide_s, folded_s, dmem_s, sinus_s, causal_s,
     own_s, flat_s, load_sem), groups, refs = refs[:27], refs[27:31], refs[31:]
    tokens, cols = x_ref.shape
    samples = noise_ref.shape[1]
    horizon = tokens // samples
    blocks = w_s.shape[0]
    per_sub = SUB // horizon
    score_scale = (cols // HEADS) ** (-0.5)
    section = lax.axis_index("section")
    ring = blocks - 1
    kept = ((hid_s, hid_hbm, load_sem.at[0]), (slope_s, slope_hbm, load_sem.at[1]))
    out_copies = [pltpu.make_async_copy(held.at[0], away, sem) for held, away, sem in kept]
    back_copies = [pltpu.make_async_copy(away, held.at[0], sem) for held, away, sem in kept]

    loads = [pltpu.make_async_copy(x_ref, pred_ref, load_sem.at[0]),
             pltpu.make_async_copy(cot_ref, grad_ref, load_sem.at[1])]
    if remote:
        gains_ref, shifts_ref, bias_ref = in_refs[7:]
        starts_at = (W_IN, W_SO, W_CKV, W_CQ, W_CO, W_UP)
        pieces = []
        for index, start in enumerate(starts_at):
            ref = in_refs[(0, 1, 3, 2, 4, 5)[index]]
            pieces.append(pltpu.make_async_copy(
                ref.at[0], w_s.at[section, :, start : start + ref.shape[2]], load_sem.at[2 + index]))
        pieces.append(pltpu.make_async_copy(in_refs[6].at[0], wd_s.at[section], load_sem.at[8]))
        for copy in pieces + loads:
            copy.start()
        vec_s[section] = jnp.zeros((VEC_ROWS, cols), F32)
        for row in range(SHIFT):
            vec_s[section, row : row + 1, :] = gains_ref[row]
        for row in range(SHIFT, BIAS):
            vec_s[section, row : row + 1, :] = shifts_ref[row - SHIFT]
        for part in range(4):
            vec_s[section, BIAS + part : BIAS + part + 1, :] = bias_ref[:, part * cols : (part + 1) * cols]
        sets = [(group,) + refs[2 + 8 * kind : 10 + 8 * kind] for kind, group in enumerate(groups)]
        sets += [refs[34 + 9 * index : 43 + 9 * index] for index in range(2)]
        links = Links(w_s, wd_s, vec_s, refs[0], refs[1], sets)
        links.greet()
        links.vectors(0, section, links.relative(1)).start()
        links.vectors(1, section, links.relative(2)).start()
        for piece, copies in enumerate((pieces[:1], pieces[1:2], pieces[2:3], pieces[3:5], pieces[5:6], pieces[6:])):
            for copy in copies:
                copy.wait()
            links.to_sibling(piece, section).start()

            @pl.when(links.core == 0)
            def _():
                links.over_y(piece, section).start()
    else:
        loads += [pltpu.make_async_copy(w_hbm, w_s, load_sem.at[2]),
                  pltpu.make_async_copy(wd_hbm, wd_s, load_sem.at[3]),
                  pltpu.make_async_copy(vec_hbm, vec_s, load_sem.at[4])]
        for copy in loads:
            copy.start()

    wide_masks = [jnp.concatenate([mask, mask], axis=1) for mask in half_masks()]
    lane_sub = iota((SUB, SUB), 1)
    row_sub = iota((SUB, SUB), 0)

    noise_row = noise_ref[pl.ds(section, 1), :].astype(F32)
    diagonal = iota((samples, samples), 0) == iota((samples, samples), 1)
    noise_col = jnp.sum(jnp.where(diagonal, noise_row, 0.0), axis=1, keepdims=True)
    half = cols // 2
    frequency = jnp.exp(iota((1, half), 1).astype(F32) * (-math.log(10000.0) / half))
    angles = noise_col * frequency
    sinus = low(jnp.concatenate([jnp.sin(angles), jnp.cos(angles)], axis=1))
    sinus_s[...] = sinus
    tok_s[:samples, :] = low(dot(sinus, tw_ref[...]))
    obs_count = repeat_ref.shape[-1]
    for index in range(obs_ref.shape[1]):
        tok_s[samples + index * obs_count : samples + (index + 1) * obs_count, :] = obs_ref[:, index, :]
    counts = low(repeat_ref[section].astype(F32))
    token_of = iota((obs_count, SUB), 1) - samples
    owner_of = iota((obs_count, SUB), 0)
    is_obs = token_of >= 0
    before = low((is_obs & (owner_of < token_of % obs_count)).astype(F32))
    upto = low((is_obs & (owner_of <= token_of % obs_count)).astype(F32))
    counts8 = jnp.broadcast_to(counts, (8, obs_count))
    starts = dot(counts8, before)[:1, :]
    ends = dot(counts8, upto)[:1, :]

    def select_rows(index, carried):
        key = iota((KEYS, SUB), 0) // per_sub
        lane = iota((KEYS, SUB), 1)
        sample = index * per_sub + iota((KEYS, SUB), 0) % per_sub
        sample_f = sample.astype(F32)
        time_hit = (key == 0) & (lane == sample)
        token = lane - samples
        owned = (sample_f >= starts) & (sample_f < ends)
        obs_hit = (token >= 0) & (token // obs_count == key - 1) & owned
        folded_s[index, :, :SUB] = (time_hit | obs_hit).astype(F32)
        return carried

    lax.fori_loop(0, tokens // SUB, select_rows, 0)
    selected = folded_s[...].reshape(-1, 2 * cols)[:, :SUB]
    select_s[...] = low(selected)
    selected = jnp.concatenate([selected, jnp.zeros((2 * SUB - selected.shape[0], SUB), F32)], axis=0)
    turned_s[...] = low(jnp.transpose(selected))
    same = row_sub // horizon == lane_sub // horizon
    causal_s[...] = jnp.where(same & (row_sub <= lane_sub), 0.0, -1e30)
    third = WIDE // 3
    own_s[...] = (iota((third, SUB), 0) % per_sub == iota((third, SUB), 1) // horizon).astype(F32)
    head_mask = (iota((third, cols), 0) // per_sub == iota((third, cols), 1) // (cols // HEADS)).astype(F32)
    dmem_s[...] = jnp.zeros_like(dmem_s)
    dvec_s[...] = jnp.zeros_like(dvec_s)
    for copy in loads:
        copy.wait()

    def vec(block, row):
        return vec_s[block, row : row + 1, :]

    def weight(block, start, stop):
        return w_s[block, :, start:stop]

    def condition(block):
        kv = dot(tok_s[...], weight(block, W_CKV, W_CQ))
        keys = low(kv[:, :cols])
        vals = low(kv[:, cols:] + vec(block, SHIFT + 7))

        spread = dot(select_s[...], jnp.concatenate([keys, vals], axis=1))
        both_masks = jnp.concatenate([head_mask, head_mask], axis=1)
        for index in range(tokens // SUB):
            for key in range(3):
                start = index * KEYS + key * per_sub
                copies = jnp.concatenate([spread[start : start + per_sub]] * HEADS, axis=0)
                wide_s[index, key * third : (key + 1) * third, :] = low(copies * both_masks)

    def fold(values):
        parts = []
        for part in thirds(values):
            part = part * head_mask
            parts.append(sum(part[head * per_sub : (head + 1) * per_sub] for head in range(HEADS)))
        return jnp.concatenate(parts, axis=0)

    def thirds(values):
        return [values[third * key : third * (key + 1)] for key in range(3)]

    def over_heads(values):
        return jnp.concatenate([values[:, :SUB], values[:, SUB:]], axis=0)

    def each_chunk(chunk, body):
        def at(step, carried):
            start = step * chunk
            body(pl.ds(start if isinstance(start, int) else pl.multiple_of(start, chunk), chunk), step)
            return carried

        if chunk == tokens:
            at(0, 0)
        else:
            lax.fori_loop(0, tokens // chunk, at, 0)

    def scale_of(block, rows, place):
        held = scale_s[rows, :]
        lane = iota(held.shape, 1)
        return jnp.sum(jnp.where(lane == 3 * block + place, held, 0.0), axis=1, keepdims=True)

    def keep_scale(block, rows, place, scale):
        held = scale_s[rows, :]
        scale_s[rows, :] = jnp.where(iota(held.shape, 1) == 3 * block + place, scale, held)

    def wide(values):
        return jnp.concatenate(values, axis=1)

    def both_heads(values):
        return jnp.concatenate([values * wide_masks[0], values * wide_masks[1]], axis=0)

    def both_pairs(values):
        zero = jnp.zeros((SUB, SUB), BF16)
        return jnp.concatenate([wide([values[:, :SUB], zero]), wide([zero, values[:, SUB:]])], axis=0)

    def forward(block, carried):
        after = jnp.minimum(block + 1, blocks - 1)
        if remote:
            links.arrive(block, (0, 1, 2))
            links.start_y(block == 0, range(3))
        condition(block)

        def self_attention(rows, step):
            x = pred_ref[rows, :].astype(F32)
            unit0, scale0 = normalize(x)
            unit_s[block, 0, rows, :] = low(unit0)
            a = low(unit0 * vec(block, 0) + vec(block, SHIFT))
            q = low((dot(a, weight(block, 0, cols)) + vec(block, SHIFT + 3)) * score_scale)
            k = low(dot(a, weight(block, cols, 2 * cols)))
            v = low(dot(a, weight(block, 2 * cols, 3 * cols)) + vec(block, SHIFT + 4))
            qkv_s[block, rows, :cols] = q
            qkv_s[block, rows, cols : 2 * cols] = k
            qkv_s[block, rows, 2 * cols :] = v
            causal2 = wide([causal_s[...]] * 2)
            parts = []
            for sub in range(rows.size // SUB):
                span = slice(sub * SUB, (sub + 1) * SUB)
                scores = dot_nt(both_pairs(k[span]), both_heads(q[span]))
                stacked = []
                for pair in range(2):
                    score = scores[pair * SUB : (pair + 1) * SUB] + causal2
                    top = jnp.max(score, axis=0, keepdims=True)
                    expo = jnp.exp(score - top)
                    prob = low(expo * (1.0 / jnp.sum(expo, axis=0, keepdims=True)))
                    prob_s[block, step * (rows.size // SUB) + sub, pair] = prob
                    stacked.append(over_heads(prob))
                both = dot_tn(wide(stacked), both_heads(v[span]))
                parts.append(low(wide([both[:SUB, :SUB], both[SUB:, SUB:]])))
            context = jnp.concatenate(parts, axis=0)
            ctx_s[block, rows, :] = context
            x = x + (dot(context, weight(block, W_SO, W_CKV)) + vec(block, SHIFT + 5))
            g_s[rows, :] = x
            keep_scale(block, rows, 0, scale0)
            if remote:
                links.pass_on(block, True, (1, 5), (2, 3), (2, 4))
                links.pass_on(after, block + 1 < blocks, (1, 0), (1, 1), (1, 2))
                links.start_y(block == 0, range(3, PIECES))


        each_chunk(FORWARD_SELF, self_attention)
        if remote:
            links.arrive(block, (3,))

        def cross_attention(rows, step):
            x = g_s[rows, :]
            unit1, scale1 = normalize(x)
            unit_s[block, 1, rows, :] = low(unit1)
            c = low(unit1 * vec(block, 1) + vec(block, SHIFT + 1))
            cq = low((dot(c, weight(block, W_CQ, W_CO)) + vec(block, SHIFT + 6)) * score_scale)
            cq_s[block, rows, :] = cq
            parts = []
            for sub in range(rows.size // SUB):
                index = step * (rows.size // SUB) + sub
                scores = thirds(dot_nt(wide_s[index, :, :cols], cq[sub * SUB : (sub + 1) * SUB]))
                top = jnp.maximum(jnp.maximum(scores[0], scores[1]), scores[2])
                expos = [jnp.exp(score - top) for score in scores]
                inverse = own_s[...] / (expos[0] + expos[1] + expos[2])
                prob = low(jnp.concatenate([expo * inverse for expo in expos], axis=0))
                cprob_s[block, index] = prob
                parts.append(low(dot_tn(prob, wide_s[index, :, cols:])))
            context = jnp.concatenate(parts, axis=0)
            cctx_s[block, rows, :] = context
            x = x + (dot(context, weight(block, W_CO, W_UP)) + vec(block, SHIFT + 8))
            unit2, scale2 = normalize(x)
            unit_s[block, 2, rows, :] = low(unit2)
            keep_scale(block, rows, 1, scale1)
            keep_scale(block, rows, 2, scale2)
            g_s[rows, :] = x + vec(block, SHIFT + 9)
            dy_s[0, rows, :] = low(unit2 * vec(block, 2) + vec(block, SHIFT + 2))
            if remote:
                links.pass_on(block, True, (2, 5))
                links.pass_on(after, block + 1 < blocks, (2, 0), (2, 1))

        each_chunk(FORWARD_CROSS, cross_attention)
        if remote:
            links.arrive(block, (4, 5))

        def feed_forward(rows, step):
            e = dy_s[0, rows, :]
            root = math.sqrt(2.0 / math.pi)
            cube = root * 0.044715
            for part in range(4):
                lanes = slice(part * cols, (part + 1) * cols)
                u = low(dot(e, weight(block, W_UP + part * cols, W_UP + (part + 1) * cols)) + vec(
                    block, BIAS + part
                ))
                square = u * u
                gate = jnp.tanh(u * (square * low(cube) + low(root))) * low(0.5) + low(0.5)
                hidden = u * gate
                slope = gate + hidden * (low(1.0) - gate) * (square * low(6.0 * cube) + low(2.0 * root))
                hid_s[block % ring, rows, lanes] = hidden
                slope_s[block % ring, rows, lanes] = slope
            pred_ref[rows, :] = low(g_s[rows, :] + dot(hid_s[block % ring, rows, :], wd_s[block]))
            if remote:
                links.pass_on(after, block + 1 < blocks, (2, 2), (1, 3), (1, 4))

        @pl.when(block == ring)
        def _():
            for copy in out_copies:
                copy.wait()

        each_chunk(FORWARD_FF, feed_forward)

        @pl.when(block == 0)
        def _():
            for copy in out_copies:
                copy.start()

        return carried

    if remote:
        links.pass_on(0, True, (1, 0), (1, 1), (2, 0), (1, 2), (2, 1), (1, 3), (2, 2), (1, 4))
    lax.fori_loop(0, blocks, forward, 0)

    def put(kind, start, value):
        width, taken = WIDTHS[kind], 0
        while taken < value.shape[1]:
            index, place = (start + taken) // width, (start + taken) % width
            count = min(value.shape[1] - taken, width - place)
            part = low(value[:, taken : taken + count]).reshape(NZ, NX, ROWS, count)
            groups[kind][index, :, :, :, place : place + count] = part
            taken += count

    def emit(block, kind):
        if remote:
            links.near(kind).start()
        else:
            copy = pltpu.make_async_copy(groups[kind], dw_refs[kind].at[block], load_sem.at[2])
            copy.start()
            copy.wait()

    def store_down(first, second):
        blocks_of = [value[:, q * SUB : (q + 1) * SUB] for value in (first, second) for q in range(4)]
        dn_out[...] = jnp.transpose(jnp.concatenate(blocks_of, axis=0))

    def store_up(first, second):
        up_out[...] = wide([first, second])

    def store_cross(first, second):
        joined = wide([first, second])
        ckv_out[...] = joined[:, : 2 * cols]
        for place, out in enumerate((cq_out, co_out, so_out)):
            out[...] = joined[:, (2 + place) * cols : (3 + place) * cols]

    def store_self(first, second):
        in_out[...] = wide([first, second])

    stores = (store_down, store_up, store_cross, store_self)

    def advance(works):
        if not remote:
            return
        for kind, stage, block, there in works:

            def run(kind=kind, stage=stage, block=block):
                if stage == 1:
                    links.after_near(kind)
                elif stage == 2:
                    links.after_row(kind, block)
                elif stage == 3:
                    links.after_far(kind, block)
                else:
                    links.after_last(kind, block, stores[kind])

            if there is True:
                run()
            else:
                pl.when(there)(run)

    def time_gradient():
        dmem = dmem_s[...]
        dmem_high = low(dmem)
        dmem_low = low(dmem - dmem_high.astype(F32))
        return dot_tn(sinus_s[...], dmem_high) + dot_tn(sinus_s[...], dmem_low)

    def emit_vectors():
        vectors = dvec_s[...].reshape(blocks * VEC_ROWS, cols)
        vectors = jnp.concatenate([vectors, jnp.zeros((SUB - blocks * VEC_ROWS, cols), F32)], axis=0)
        turned = jnp.transpose(vectors).reshape(GROUPS, ROWS, SUB)
        lane = iota((ROWS, SUB), 1) % VEC_ROWS
        rows_out = []
        for group in range(GROUPS):
            part, high = group // 2, group % 2
            piece = turned[group]
            for j in range(4):
                source = turned[4 * high + j]
                if j != part:
                    source = pltpu.roll(source, (j - part) % SUB, 1)
                piece = jnp.where(lane == BIAS + j, source, piece)
            rows_out.append(piece)
        turned = jnp.concatenate(rows_out, axis=0)
        for index in range(2):
            sets[VECTOR][0][index] = low(turned).reshape(NZ, NX, ROWS, SUB)
        links.near(VECTOR).start()

    def backward(turn, carried):
        block = blocks - 1 - turn
        earlier, before = block + 1, block + 2
        again, third_turn = turn > 0, turn > 1

        def add_vec(row, values):
            dvec_s[block, row : row + 1, :] += values

        def turn_over_ones(left):
            return jnp.concatenate([jnp.transpose(left), jnp.ones((16, tokens), BF16)], axis=0)

        def put_scaled(kind, start, unit_row, right, sum_rows):
            turned = turn_over_ones(unit_s[block, unit_row])
            gain = place_column(vec(block, unit_row))
            shift = place_column(vec(block, SHIFT + unit_row))
            parts = []
            for place, row in enumerate(sum_rows):
                both = dot(turned, right[:, place * cols : (place + 1) * cols])
                sums = both[cols : cols + 1]
                dvec_s[block, row : row + 1, :] = sums
                put(kind, start + place * cols, both[:cols] * gain + shift * sums)
                parts.append((both[:cols], sums))
            return parts

        def put_plain(kind, start, left, right, row):
            both = dot(turn_over_ones(left), right)
            dvec_s[block, row : row + 1, :] = both[cols : cols + 1]
            put(kind, start, both[:cols])

        @pl.when(block == 0)
        def _():
            for copy in back_copies:
                copy.wait()

        turned = jnp.transpose(grad_ref[...])
        for part in range(4):
            piece = low(dot(turned, hid_s[block % ring, :, part * cols : (part + 1) * cols]))
            for index in range(2):
                for x in range(NX):
                    for q in range(4):
                        row = SUB * index + ROWS * q
                        groups[DOWN][index, part, x, :, q * SUB : (q + 1) * SUB] = piece[
                            row : row + ROWS, x * SUB : (x + 1) * SUB
                        ]
        def feed_forward(rows, step):
            dy3 = grad_ref[rows, :]
            g = dy3.astype(F32)
            add_vec(SHIFT + 9, jnp.sum(g, axis=0, keepdims=True))
            for part in range(4):
                lanes = slice(part * cols, (part + 1) * cols)
                dh = dot_nt(dy3, wd_s[block, lanes, :])
                slope_s[block % ring, rows, lanes] = low(dh) * slope_s[block % ring, rows, lanes]
            de = dot_nt(slope_s[block % ring, rows, :], weight(block, W_UP, W_END))
            back, along, flat = normalize_back(
                de, unit_s[block, 2, rows, :].astype(F32), scale_of(block, rows, 2), vec(block, 2)
            )
            add_vec(2, along)
            add_vec(SHIFT + 2, flat)
            g = g + back
            g_s[rows, :] = g
            dy_s[0, rows, :] = low(g)

        each_chunk(BACK_FF, feed_forward)
        advance((
            (DOWN, 3, earlier, again), (UP, 2, earlier, again), (SELF, 1, earlier, again),
            (UP, 4, before, third_turn), (CROSS, 4, before, third_turn), (SELF, 4, before, third_turn),
        ))
        emit(block, DOWN)
        pl.when(turn == 0)(back_copies[0].start)

        put_scaled(UP, 0, 2, slope_s[block % ring], [BIAS + part for part in range(4)])
        condition(block)
        advance(((CROSS, 2, earlier, again),))
        emit(block, UP)
        pl.when(turn == 0)(back_copies[1].start)

        def cross_attention(rows, step):
            dctx = low(dot_nt(dy_s[0, rows, :], weight(block, W_CO, W_UP)))
            for sub in range(rows.size // SUB):
                index = step * (rows.size // SUB) + sub
                span = pl.ds(index * SUB if isinstance(index, int) else pl.multiple_of(index * SUB, SUB), SUB)
                keys, vals = wide_s[index, :, :cols], wide_s[index, :, cols:]
                part = dctx[sub * SUB : (sub + 1) * SUB]
                prob = cprob_s[block, index]
                prob32 = prob.astype(F32)
                weighted = prob32 * dot_nt(vals, part)
                inner = sum(thirds(weighted))
                dscore = low(weighted - prob32 * jnp.concatenate([inner] * 3, axis=0))
                folded_s[index, :, :cols] = fold(dot(dscore, cq_s[block, span, :]))
                folded_s[index, :, cols:] = fold(dot(prob, part))
                cq_s[block, span, :] = low(dot_tn(dscore, keys) * score_scale)
            dcq = cq_s[block, rows, :]
            dc = dot_nt(dcq, weight(block, W_CQ, W_CO))
            back, along, flat = normalize_back(
                dc, unit_s[block, 1, rows, :].astype(F32), scale_of(block, rows, 1), vec(block, 1)
            )
            add_vec(1, along)
            add_vec(SHIFT + 1, flat)
            g = g_s[rows, :] + back
            g_s[rows, :] = g
            dy_s[1, rows, :] = low(g)

        each_chunk(BACK_CROSS, cross_attention)
        advance(((DOWN, 1, block, True), (DOWN, 4, earlier, again)))

        folded = folded_s[...].reshape(-1, 2 * cols)
        dkv32 = dot(turned_s[:, : folded.shape[0]], low(folded))
        dkv = low(dkv32)
        add_vec(SHIFT + 7, jnp.sum(dkv32[:, cols:], axis=0, keepdims=True))
        dmem_s[...] += dot_nt(dkv[:samples], weight(block, W_CKV, W_CQ))
        put(CROSS, 0, dot_tn(tok_s[...], dkv))
        put_scaled(CROSS, 2 * cols, 1, cq_s[block], [SHIFT + 6])
        put_plain(CROSS, 3 * cols, cctx_s[block], dy_s[0], SHIFT + 8)
        put_plain(CROSS, 4 * cols, ctx_s[block], dy_s[1], SHIFT + 5)
        advance(((SELF, 2, earlier, again), (UP, 1, block, True)))
        emit(block, CROSS)
        if remote:

            @pl.when(block == 0)
            def _():
                dtime = time_gradient()
                for index in range(2):
                    part = low(dtime[:, index * SUB : (index + 1) * SUB])
                    sets[TIME][0][index] = part.reshape(NZ, NX, ROWS, SUB)
                links.near(TIME).start()

        def self_attention(rows, step):
            dctx = low(dot_nt(dy_s[1, rows, :], weight(block, W_SO, W_CKV)))
            for sub in range(rows.size // SUB):
                index = step * (rows.size // SUB) + sub
                span = pl.ds(index * SUB if isinstance(index, int) else pl.multiple_of(index * SUB, SUB), SUB)
                part = dctx[sub * SUB : (sub + 1) * SUB]
                queries, keys, values = (qkv_s[block, span, place * cols : (place + 1) * cols] for place in range(3))
                sides = (slice(0, SUB), slice(SUB, 2 * SUB))
                dstack = both_heads(part)
                qstack = both_heads(queries)
                kstack = both_heads(keys)
                probs = [prob_s[block, index, pair] for pair in range(2)]
                dprobs = dot_nt(both_pairs(values), dstack)
                dprobs = [dprobs[side] for side in sides]
                dscores = []
                for prob, dprob in zip(probs, dprobs):
                    prob32 = prob.astype(F32)
                    weighted = prob32 * dprob
                    dscores.append(low(weighted - prob32 * jnp.sum(weighted, axis=0, keepdims=True)))
                dq = dot_tn(wide([over_heads(dscore) for dscore in dscores]), kstack)
                dq = [dq[side, side] for side in sides]
                dk = dot(jnp.concatenate(dscores, axis=0), qstack)
                dk = [dk[side, side] for side in sides]
                dv = dot(jnp.concatenate(probs, axis=0), dstack)
                dv = [dv[side, side] for side in sides]
                qkv_s[block, span, :cols] = low(wide(dq) * score_scale)
                qkv_s[block, span, cols : 2 * cols] = low(wide(dk))
                qkv_s[block, span, 2 * cols :] = low(wide(dv))

        each_chunk(BACK_SELF, self_attention)
        advance((
            (UP, 3, earlier, again), (CROSS, 3, earlier, again), (DOWN, 2, block, True),
            (CROSS, 1, block, True), (TIME, 1, block, block == 0),
        ))

        gain_column, shift_column = 0.0, 0.0
        for place, (both, sums) in enumerate(
            put_scaled(SELF, 0, 0, qkv_s[block], (SHIFT + 3, KEYSUM, SHIFT + 4))
        ):
            matrix = weight(block, place * cols, (place + 1) * cols).astype(F32)
            gain_column += jnp.sum(both * matrix, axis=1, keepdims=True)
            shift_column += jnp.sum(sums * matrix, axis=1, keepdims=True)
        dvec_s[block, 0:1, :] = place_row(gain_column)
        dvec_s[block, SHIFT : SHIFT + 1, :] = place_row(shift_column)
        emit(block, SELF)
        if remote:
            pl.when(block == 0)(emit_vectors)

        def self_norm(rows, step):
            da = dot_nt(qkv_s[block, rows, :], weight(block, 0, 3 * cols))
            back, _, _ = normalize_back(
                da, unit_s[block, 0, rows, :].astype(F32), scale_of(block, rows, 0), vec(block, 0)
            )
            grad_ref[rows, :] = low(g_s[rows, :] + back)

        each_chunk(BACK_SELF, self_norm)
        advance(((SELF, 3, earlier, again),))
        return carried

    lax.fori_loop(0, blocks, backward, 0)
    if not remote:
        time_out[...] = time_gradient()
        dvec_ref[...] = dvec_s[...]
        return

    links.after_row(UP, 0)
    links.after_near(SELF)
    links.after_near(VECTOR)
    links.after_far(DOWN, 0)
    links.after_row(CROSS, 0)
    links.after_row(TIME, 0)
    links.after_last(UP, 1, store_up)
    links.after_last(CROSS, 1, store_cross)
    links.after_far(UP, 0)
    links.after_row(SELF, 0)
    links.after_row(VECTOR, 0)
    links.after_last(SELF, 1, store_self)
    links.after_last(DOWN, 0, store_down)
    links.after_far(CROSS, 0)
    links.after_far_all(TIME)
    links.after_last(UP, 0, store_up)
    links.after_far(SELF, 0)
    links.after_far_all(VECTOR)
    links.after_last(CROSS, 0, store_cross)
    time_out[...] = wide(links.after_last_all(TIME))
    links.after_last(SELF, 0, store_self)
    mine, _ = links.after_last_all(VECTOR)
    padded = jnp.concatenate([mine, jnp.zeros((SUB - ROWS, SUB), F32)], axis=0)
    flat_s[...] = jnp.transpose(padded)
    mine = flat_s[pl.ds(pl.multiple_of(section * VEC_ROWS, 8), VEC_ROWS), :]
    for row in range(SHIFT):
        gains_out[row] = mine[row : row + 1, :ROWS]
    for row in range(SHIFT, BIAS):
        shifts_out[row - SHIFT] = mine[row : row + 1, :ROWS]
    bias = mine[BIAS : BIAS + 1, :]
    for part in range(1, 4):
        bias = bias + pltpu.roll(mine[BIAS + part : BIAS + part + 1, :], part * ROWS, 1)
    bias_out[...] = bias
    links.finish_weights()


def run_blocks(remote, x, cot, obs, repeat, noise, time_weight, *weights, interpret=False):
    tokens, cols = x.shape
    blocks = 4
    samples = noise.shape[1]
    vmem = pl.BlockSpec(memory_space=pltpu.VMEM)
    hbm = pl.BlockSpec(memory_space=pl.ANY)
    half_rows = (NZ, NX, ROWS)
    scratch = [
        pltpu.VMEM((blocks, 3, tokens, cols), BF16),
        pltpu.VMEM((tokens, SUB), F32),
        pltpu.VMEM((blocks, tokens, 3 * cols), BF16),
        pltpu.VMEM((blocks, tokens // SUB, 2, SUB, 2 * SUB), BF16),
        pltpu.VMEM((blocks, tokens, cols), BF16),
        pltpu.VMEM((blocks, tokens, cols), BF16),
        pltpu.VMEM((blocks, tokens // SUB, WIDE, SUB), BF16),
        pltpu.VMEM((blocks, tokens, cols), BF16),
        pltpu.VMEM((blocks - 1, tokens, 4 * cols), BF16),
        pltpu.VMEM((blocks - 1, tokens, 4 * cols), BF16),
        pltpu.VMEM((2, tokens, cols), BF16),
        pltpu.VMEM((tokens, cols), F32),
        pltpu.VMEM((blocks, cols, W_END), BF16),
        pltpu.VMEM((blocks, 4 * cols, cols), BF16),
        pltpu.VMEM((blocks, VEC_ROWS, cols), F32),
        pltpu.VMEM((blocks, VEC_ROWS, cols), F32),
        pltpu.VMEM((tokens // SUB * KEYS, SUB), BF16),
        pltpu.VMEM((SUB, 2 * SUB), BF16),
        pltpu.VMEM((SUB, cols), BF16),
        pltpu.VMEM((tokens // SUB, WIDE, 2 * cols), BF16),
        pltpu.VMEM((tokens // SUB, KEYS, 2 * cols), F32),
        pltpu.VMEM((samples, cols), F32),
        pltpu.VMEM((samples, cols), BF16),
        pltpu.VMEM((SUB, SUB), F32),
        pltpu.VMEM((WIDE // 3, SUB), F32),
        pltpu.VMEM((SUB, SUB), F32),
        pltpu.SemaphoreType.DMA((12,)),
    ]
    scratch += [pltpu.VMEM((2,) + half_rows + (width,), BF16) for width in WIDTHS[:TIME]]
    if remote:
        scratch += [pltpu.SemaphoreType.DMA((5 * PIECES + 3,))] * 2
        for kind, width in enumerate(WIDTHS):
            if kind >= TIME:
                scratch.append(pltpu.VMEM((2,) + half_rows + (width,), BF16))
            scratch += [
                pltpu.VMEM(half_rows + (width,), BF16),
                pltpu.VMEM((NZ, ROWS, width), BF16),
                pltpu.VMEM(((2 if kind in TURNS else 1) * (NZ - 1), ROWS, width), BF16),
                pltpu.VMEM((3, ROWS, width), BF16),
                pltpu.VMEM((ROWS, width), BF16),
                pltpu.VMEM((NZ, ROWS, width), BF16),
                pltpu.SemaphoreType.DMA((3 + 2 * NZ,)),
                pltpu.SemaphoreType.DMA((3 + 2 * NZ,)),
            ]
        shapes = ((ROWS, 3 * cols), (ROWS, cols), (ROWS, cols), (ROWS, 2 * cols), (ROWS, cols),
                  (ROWS, 4 * cols), (4 * ROWS, cols), (SHIFT, 1, ROWS), (BIAS - SHIFT, 1, ROWS), (1, 4 * ROWS),
                  (ROWS, cols))
        outs = tuple(jax.ShapeDtypeStruct(shape, F32) for shape in shapes)
        in_specs = [hbm, hbm] + [vmem] * 4 + [hbm] * 7 + [vmem] * 3
        out_specs = (vmem,) * (2 + len(outs))
        params = pltpu.CompilerParams(
            vmem_limit_bytes=VMEM_BYTES, collective_id=0, has_side_effects=True)
    else:
        outs = (
            jax.ShapeDtypeStruct((blocks, VEC_ROWS, cols), F32),
            jax.ShapeDtypeStruct((cols, cols), F32),
        )
        outs = tuple(
            jax.ShapeDtypeStruct((blocks, 2) + half_rows + (width,), BF16) for width in WIDTHS[:TIME]
        ) + outs
        in_specs = [hbm, hbm] + [vmem] * 4 + [hbm] * 3
        out_specs = (vmem, vmem) + (hbm,) * 4 + (vmem, vmem)
        params = pltpu.CompilerParams(vmem_limit_bytes=VMEM_BYTES)
    low_out = jax.ShapeDtypeStruct((tokens, cols), BF16)
    away = jax.ShapeDtypeStruct((tokens, 4 * cols), BF16)
    return pl.pallas_call(
        functools.partial(block_kernel, remote),
        out_shape=(low_out, low_out) + outs + (away, away),
        in_specs=in_specs,
        out_specs=out_specs + (hbm, hbm),
        scratch_shapes=scratch,
        compiler_params=params,
        interpret=interpret,
    )(x, cot, obs, repeat, noise, time_weight, *weights)


def hand_out(*refs):
    count = (len(refs) - 1) // 3
    held, sem = refs[2 * count : 3 * count], refs[-1]
    arriving = [pltpu.make_async_copy(refs[i], held[i], sem.at[i]) for i in range(count)]
    leaving = []
    for copy in arriving:
        copy.start()
    for index in range(count):
        target = refs[count + index]
        if len(target.shape) > len(held[index].shape):
            target = target.at[0]
        arriving[index].wait()
        leaving.append(pltpu.make_async_copy(held[index], target, sem.at[index]))
        leaving[-1].start()
    for copy in leaving:
        copy.wait()


def finished(results):
    hbm = pl.BlockSpec(memory_space=pl.ANY)
    shapes = [(1,) + result.shape for result in results[:9]] + [result.shape for result in results[9:]]
    return pl.pallas_call(
        hand_out,
        out_shape=tuple(jax.ShapeDtypeStruct(shape, result.dtype) for shape, result in zip(shapes, results)),
        in_specs=[hbm] * len(results),
        out_specs=(hbm,) * len(results),
        scratch_shapes=[pltpu.VMEM(result.shape, result.dtype) for result in results]
        + [pltpu.SemaphoreType.DMA((len(results),))],
    )(*results)


def pack_weights(self_in, self_out, cross_q, cross_kv, cross_out, mlp_up, mlp_down):
    parts = (self_in, self_out, cross_kv, cross_q, cross_out, mlp_up)
    return jnp.concatenate([part[0] for part in parts], axis=1), mlp_down[0]


def pack_vectors(gains, shifts, mlp_bias):
    cols = gains.shape[-1]
    rows = jnp.concatenate([gains[0], shifts[0], mlp_bias.reshape(4, cols)], axis=0)
    return jnp.pad(rows, ((0, VEC_ROWS - rows.shape[0]), (0, 0)))


def natural(dweights):
    def joined(kind):
        parts = dweights[kind].reshape(-1, 2, GROUPS * ROWS, WIDTHS[kind])
        return jnp.concatenate([parts[:, 0], parts[:, 1]], axis=-1)

    blocks = dweights[DOWN].shape[0]
    down = dweights[DOWN].reshape(blocks, 2, GROUPS, ROWS, 4, SUB).transpose(0, 2, 5, 1, 4, 3)
    return joined(UP), joined(CROSS), joined(SELF), down.reshape(blocks, GROUPS * SUB, -1)


def gathered(data, packed_weights, packed_vectors):
    sections = lax.axis_size("section")
    groups = lax.axis_size("dp")
    cols = data[0].shape[-1]
    weights = [lax.all_gather(part, "section", axis=0) for part in packed_weights]
    vectors = lax.all_gather(packed_vectors, "section", axis=0)
    pred, grad, *dweights, dvectors, dtime, _, _ = run_blocks(False, *data, *weights, vectors)
    rows = cols // groups
    up, cross, own, down = natural(dweights)
    rest = jnp.concatenate([up, cross, own], axis=2).reshape(sections, groups, -1)
    down = down.reshape(sections, groups, -1)
    small = dvectors[:, :BIAS].reshape(sections, BIAS, groups, rows).transpose(0, 2, 1, 3)
    small = small.reshape(sections, groups, BIAS * rows)
    bias = dvectors[:, BIAS:KEYSUM].reshape(sections, groups, 4 * rows)
    term = jnp.broadcast_to(dtime.reshape(1, groups, rows * cols), (sections, groups, rows * cols))
    sent = jnp.concatenate([rest, down], axis=2).reshape(sections * groups, -1)
    sent_small = jnp.concatenate([small, bias, term], axis=2).reshape(sections * groups, -1)
    got = lax.psum_scatter(sent, ("section", "dp"), scatter_dimension=0, tiled=True)[0].astype(F32)
    got_small = lax.psum_scatter(sent_small, ("section", "dp"), scatter_dimension=0, tiled=True)[0]
    widths = (up.shape[-1], cross.shape[-1], own.shape[-1])
    split = sum(widths) * rows
    rest = got[:split].reshape(rows, sum(widths))
    down = got[split:].reshape(4 * rows, cols)
    small = got_small[: BIAS * rows].reshape(BIAS, rows)
    bias = got_small[BIAS * rows : (BIAS + 4) * rows].reshape(4, rows)
    term = got_small[(BIAS + 4) * rows :].reshape(rows, cols)
    up, cross, own = jnp.split(rest, (widths[0], widths[0] + widths[1]), axis=1)
    kv, query, out, self_out = jnp.split(cross, (2 * cols, 3 * cols, 4 * cols), axis=1)
    return (pred, grad, own, self_out, query, kv, out, up, down, small[:SHIFT], small[SHIFT:], bias, term)


def local(
    horizon, cotangent, obs_tokens, obs_repeat, noise_step, time_weight,
    self_in, self_out, cross_q, cross_kv, cross_out, mlp_up, mlp_down, gains, shifts, mlp_bias,
):
    cols = horizon.shape[-1]
    data = (horizon[0], cotangent[0], obs_tokens[0], obs_repeat, noise_step, time_weight)
    weights = (self_in, self_out, cross_q, cross_kv, cross_out, mlp_up, mlp_down)
    if lax.axis_size("dp") == GROUPS:
        vectors = (gains.transpose(1, 0, 2), shifts.transpose(1, 0, 2), mlp_bias)
        results = finished(run_blocks(True, *data, *weights, *vectors)[:-2])
        return results[:9] + (results[9].transpose(1, 0, 2), results[10].transpose(1, 0, 2)) + results[11:]
    results = gathered(data, pack_weights(*weights), pack_vectors(gains, shifts, mlp_bias))
    return tuple(result[None] for result in results[:11]) + (results[11].reshape(1, -1), results[12])


def solution(mesh):
    whole = P("section", None, None)
    return jax.shard_map(
        local,
        mesh=mesh,
        in_specs=(
            P("section", "dp", None), P("section", "dp", None), P("section", "dp", None, None),
            P(None, "dp", None), P(None, "dp"), P(),
            whole, whole, whole, whole, whole, whole, whole, whole, whole, P("section", None),
        ),
        out_specs=(P("section", "dp", None),) * 9
        + (P("section", None, "dp"), P("section", None, "dp"), P("section", "dp"), P("dp", None)),
        check_vma=False,
    )
```

```python
import functools
import math

import jax
import jax.numpy as jnp
from jax import lax
from jax.experimental import pallas as pl
from jax.experimental.pallas import tpu as pltpu
from jax.sharding import PartitionSpec as P

HEADS = 4
VMEM_BYTES = 63 * 1024 * 1024
SUB = 128
F32 = jnp.float32
BF16 = jnp.bfloat16

W_IN, W_SO, W_CKV, W_CQ, W_CO, W_UP, W_END = 0, 768, 1024, 1536, 1792, 2048, 3072
SHIFT, BIAS, KEYSUM, VEC_ROWS = 3, 13, 17, 24
SENT = ((W_IN, 512), (512, W_CKV), (W_CKV, W_CQ), (W_CQ, W_UP), (W_UP, W_END))
DOWN_PIECE, PIECES = 5, 6
DOWN, UP, CROSS, SELF, TIME, VECTOR = range(6)
WIDTHS = (512, 512, 640, 384, 128, 128)
FORWARD_SELF, FORWARD_CROSS, FORWARD_FF = 1024, 1024, 1024
BACK_FF, BACK_CROSS, BACK_SELF = 1024, 1024, 1024
ROWS, NZ, NX = 32, 4, 2
TURNS = (UP, SELF)
GROUPS = NZ * NX
KEYS, WIDE = 24, 96


def dot(left, right):
    return jnp.dot(left, right, preferred_element_type=F32)


def dot_nt(left, right):
    return lax.dot_general(left, right, (((1,), (1,)), ((), ())), preferred_element_type=F32)


def dot_tn(left, right):
    return lax.dot_general(left, right, (((0,), (0,)), ((), ())), preferred_element_type=F32)


def iota(shape, axis):
    return lax.broadcasted_iota(jnp.int32, shape, axis)


def low(values):
    return jnp.asarray(values, BF16)


def normalize(values):
    center = values - jnp.mean(values, axis=-1, keepdims=True)
    scale = lax.rsqrt(jnp.mean(center * center, axis=-1, keepdims=True) + 1e-05)
    return center * scale, scale


def normalize_back(grad, unit, scale, gain):
    ahead = grad * unit
    grad_unit = grad * gain
    mean_grad = jnp.mean(grad_unit, axis=-1, keepdims=True)
    mean_along = jnp.mean(ahead * gain, axis=-1, keepdims=True)
    back = (grad_unit - mean_grad - unit * mean_along) * scale
    return back, jnp.sum(ahead, axis=0, keepdims=True), jnp.sum(grad, axis=0, keepdims=True)


def half_masks():
    lane = iota((1, SUB), 1)
    first = (lane < SUB // 2).astype(F32)
    return low(first), low(1.0 - first)


def add_low(left, right):
    return left + right


def place_row(column):
    size = column.shape[0]
    diagonal = iota((size, size), 0) == iota((size, size), 1)
    return jnp.sum(jnp.where(diagonal, column, 0.0), axis=0, keepdims=True)


def place_column(row):
    size = row.shape[1]
    diagonal = iota((size, size), 0) == iota((size, size), 1)
    return jnp.sum(jnp.where(diagonal, row, 0.0), axis=1, keepdims=True)


class Links:
    def __init__(self, w_s, wd_s, vec_s, wsend, wrecv, sets):
        self.w, self.wd, self.vec, self.wsend, self.wrecv, self.sets = w_s, wd_s, vec_s, wsend, wrecv, sets
        self.section = lax.axis_index("section")
        self.group = lax.axis_index("dp")
        self.core, self.y = self.section % 2, self.section // 2
        self.x, self.z = self.group % NX, self.group // NX
        self.x_peer = self.z * NX + (self.x + 1) % NX

    def relative(self, step):
        return (self.y + step // 2) % 2 * 2 + (self.core + step % 2) % 2

    def relation(self, block):
        return (self.y + block // 2) % 2 * 2 + (self.core + block % 2) % 2

    def z_peer(self, step):
        return (self.z + step) % NZ * NX + self.x

    def greet(self):
        barrier = pltpu.get_barrier_semaphore()
        peers = [{"section": self.relative(step)} for step in (1, 2, 3)]
        peers += [{"dp": self.x_peer}] + [{"dp": self.z_peer(step)} for step in range(1, NZ)]
        for peer in peers:
            pl.semaphore_signal(barrier, inc=1, device_id=peer, device_id_type=pl.DeviceIdType.MESH)
        pl.semaphore_wait(barrier, len(peers))

    def remote(self, src, dst, send, recv, peer):
        return pltpu.make_async_remote_copy(
            src_ref=src, dst_ref=dst, send_sem=send, recv_sem=recv, device_id=peer,
            device_id_type=pl.DeviceIdType.MESH,
        )

    def weight_copy(self, slot, block, piece, half, peer):
        array, lanes = (self.wd, slice(None)) if piece == DOWN_PIECE else (self.w, slice(*SENT[piece]))
        part = array.at[block, :, lanes]
        if half is not None:
            rows = array.shape[1] // 2
            part = array.at[block, pl.ds(pl.multiple_of(half * rows, rows), rows), lanes]
        return self.remote(part, part, self.wsend.at[slot], self.wrecv.at[slot], peer)

    def vector_copy(self, slot, block, peer):
        part = self.vec.at[block]
        return self.remote(part, part, self.wsend.at[slot], self.wrecv.at[slot], peer)

    def to_sibling(self, piece, block):
        return self.weight_copy(piece, block, piece, None, {"section": self.relative(1)})

    def over_y(self, piece, block):
        return self.weight_copy(PIECES + piece, block, piece, self.x, {"section": self.relative(2)})

    def over_x(self, piece, block, half):
        return self.weight_copy(2 * PIECES + piece, block, piece, half, {"dp": self.x_peer})

    def forwarded(self, piece, block, half, which):
        return self.weight_copy((3 + which) * PIECES + piece, block, piece, half, {"section": self.relative(1)})

    def vectors(self, step, block, peer):
        return self.vector_copy(5 * PIECES + step, block, {"section": peer})

    def start_y(self, when, pieces):
        @pl.when(when & (self.core == 1))
        def _():
            for piece in pieces:
                self.over_y(piece, self.section).start()

    def pass_first(self, piece, block):
        self.over_y(piece, block).wait_recv()
        self.over_x(piece, block, self.x).start()
        self.forwarded(piece, block, self.x, 0).start()

    def pass_second(self, piece, block):
        self.over_x(piece, block, 1 - self.x).wait_recv()
        self.forwarded(piece, block, 1 - self.x, 1).start()

    def pass_on(self, block, when, *works):
        @pl.when(self.relation(block) == 2 if when is True else when & (self.relation(block) == 2))
        def _():
            for stage, piece in works:
                if stage == 1 and piece == 0:
                    self.vectors(1, block, self.relative(2)).wait_recv()
                    self.vectors(2, block, self.relative(1)).start()
                (self.pass_first if stage == 1 else self.pass_second)(piece, block)

    def arrive(self, block, pieces):
        relation = self.relation(block)

        @pl.when(relation == 1)
        def _():
            if 0 in pieces:
                self.vectors(0, block, self.relative(1)).wait_recv()
            for piece in pieces:
                self.to_sibling(piece, block).wait_recv()

        @pl.when(relation == 3)
        def _():
            if 0 in pieces:
                self.vectors(2, block, self.relative(1)).wait_recv()
            for piece in pieces:
                self.forwarded(piece, block, self.x, 0).wait_recv()
                self.forwarded(piece, block, 1 - self.x, 1).wait_recv()

    def finish_weights(self):
        own, passed = self.section, self.relative(2)
        self.vectors(0, own, self.relative(1)).wait_send()
        self.vectors(1, own, self.relative(2)).wait_send()
        self.vectors(2, passed, self.relative(1)).wait_send()
        for piece in range(PIECES):
            self.to_sibling(piece, own).wait_send()
            self.over_y(piece, own).wait_send()
            self.over_x(piece, passed, self.x).wait_send()
            self.forwarded(piece, passed, self.x, 0).wait_send()
            self.forwarded(piece, passed, 1 - self.x, 1).wait_send()

    def near(self, kind):
        group_s, near_s, _, _, _, _, _, send, recv = self.sets[kind]
        return self.remote(group_s.at[1 - self.core], near_s, send.at[0], recv.at[0],
                           {"section": self.relative(1)})

    def row(self, kind):
        group_s, _, row_s, _, _, _, _, send, recv = self.sets[kind]
        return self.remote(group_s.at[self.core, :, 1 - self.x], row_s, send.at[1], recv.at[1],
                           {"dp": self.x_peer})

    def far_slot(self, kind, step, block):
        return (block % 2) * (NZ - 1) + step - 1 if kind in TURNS else step - 1

    def far(self, kind, step, block):
        far_s, _, _, fold_s, send, recv = self.sets[kind][3:]
        slot = self.far_slot(kind, step, block)
        sem = slot + 2 if kind not in TURNS else 1 + step + (block % 2) * (NZ + 2)
        return self.remote(fold_s.at[(self.z + step) % NZ], far_s.at[slot], send.at[sem], recv.at[sem],
                           {"dp": self.z_peer(step)})

    def last(self, kind, step, peer):
        last_s, sum_s, _, send, recv = self.sets[kind][4:]
        slot = NZ + step
        return self.remote(sum_s, last_s.at[step - 1],
                           send.at[slot], recv.at[slot], {"section": peer})

    def after_near(self, kind):
        group_s, near_s = self.sets[kind][:2]
        self.near(kind).wait()
        group_s[self.core] = add_low(group_s[self.core], near_s[...])
        self.row(kind).start()

    def after_row(self, kind, block):
        group_s, row_s, fold_s = self.sets[kind][0], self.sets[kind][2], self.sets[kind][6]
        self.row(kind).wait()
        fold_s[...] = add_low(group_s[self.core, :, self.x], row_s[...])
        for step in range(1, NZ):
            self.far(kind, step, block).start()

    def sum_far(self, kind, block):
        far_s, _, sum_s, fold_s = self.sets[kind][3:7]
        for step in range(1, NZ):
            self.far(kind, step, block).wait()
        total = fold_s[self.z].astype(F32)
        for step in range(1, NZ):
            total = total + far_s[self.far_slot(kind, step, block)].astype(F32)
        sum_s[...] = low(total)

    def after_far(self, kind, block):
        self.sum_far(kind, block)
        relation = self.relation(block)

        @pl.when(relation > 0)
        def _():
            self.last(kind, relation, block).start()

    def halves(self, kind):
        last_s, sum_s = self.sets[kind][4:6]
        here = sum_s[...].astype(F32) + last_s[1].astype(F32)
        there = last_s[0].astype(F32) + last_s[2].astype(F32)
        return jnp.where(self.core == 0, here, there), jnp.where(self.core == 0, there, here)

    def after_last(self, kind, block, store):
        relation = self.relation(block)

        @pl.when(relation > 0)
        def _():
            self.last(kind, relation, block).wait_send()

        @pl.when(relation == 0)
        def _():
            for step in (1, 2, 3):
                self.last(kind, step, self.relative(step)).wait_recv()
            store(*self.halves(kind))

    def after_far_all(self, kind):
        self.sum_far(kind, 0)
        for step in (1, 2, 3):
            self.last(kind, step, self.relative(step)).start()

    def after_last_all(self, kind):
        for step in (1, 2, 3):
            self.last(kind, step, self.relative(step)).wait()
        return self.halves(kind)


def block_kernel(remote, *refs):
    (x_ref, cot_ref, obs_ref, repeat_ref, noise_ref, tw_ref), refs = refs[:6], refs[6:]
    if remote:
        in_refs, refs = refs[:10], refs[10:]
        (pred_ref, grad_ref, in_out, so_out, cq_out, ckv_out, co_out, up_out, dn_out,
         gains_out, shifts_out, bias_out, time_out, hid_hbm, slope_hbm), refs = refs[:15], refs[15:]
    else:
        (w_hbm, wd_hbm, vec_hbm), refs = refs[:3], refs[3:]
        (pred_ref, grad_ref), dw_refs, refs = refs[:2], refs[2:6], refs[6:]
        (dvec_ref, time_out, hid_hbm, slope_hbm), refs = refs[:4], refs[4:]
    (unit_s, scale_s, qkv_s, prob_s, ctx_s, cq_s, cprob_s, cctx_s, hid_s, slope_s, dy_s, g_s,
     w_s, wd_s, vec_s, dvec_s, select_s, turned_s, tok_s, wide_s, folded_s, dmem_s, sinus_s, causal_s,
     own_s, flat_s, load_sem), groups, refs = refs[:27], refs[27:31], refs[31:]
    tokens, cols = x_ref.shape
    samples = noise_ref.shape[1]
    horizon = tokens // samples
    blocks = w_s.shape[0]
    per_sub = SUB // horizon
    score_scale = (cols // HEADS) ** (-0.5)
    section = lax.axis_index("section")
    ring = blocks - 1
    kept = ((hid_s, hid_hbm, load_sem.at[0]), (slope_s, slope_hbm, load_sem.at[1]))
    out_copies = [pltpu.make_async_copy(held.at[0], away, sem) for held, away, sem in kept]
    back_copies = [pltpu.make_async_copy(away, held.at[0], sem) for held, away, sem in kept]

    loads = [pltpu.make_async_copy(x_ref, pred_ref, load_sem.at[0]),
             pltpu.make_async_copy(cot_ref, grad_ref, load_sem.at[1])]
    if remote:
        gains_ref, shifts_ref, bias_ref = in_refs[7:]
        starts_at = (W_IN, W_SO, W_CKV, W_CQ, W_CO, W_UP)
        pieces = []
        for index, start in enumerate(starts_at):
            ref = in_refs[(0, 1, 3, 2, 4, 5)[index]]
            pieces.append(pltpu.make_async_copy(
                ref.at[0], w_s.at[section, :, start : start + ref.shape[2]], load_sem.at[2 + index]))
        pieces.append(pltpu.make_async_copy(in_refs[6].at[0], wd_s.at[section], load_sem.at[8]))
        for copy in pieces + loads:
            copy.start()
        vec_s[section] = jnp.zeros((VEC_ROWS, cols), F32)
        for row in range(SHIFT):
            vec_s[section, row : row + 1, :] = gains_ref[row]
        for row in range(SHIFT, BIAS):
            vec_s[section, row : row + 1, :] = shifts_ref[row - SHIFT]
        for part in range(4):
            vec_s[section, BIAS + part : BIAS + part + 1, :] = bias_ref[:, part * cols : (part + 1) * cols]
        sets = [(group,) + refs[2 + 8 * kind : 10 + 8 * kind] for kind, group in enumerate(groups)]
        sets += [refs[34 + 9 * index : 43 + 9 * index] for index in range(2)]
        links = Links(w_s, wd_s, vec_s, refs[0], refs[1], sets)
        links.greet()
        links.vectors(0, section, links.relative(1)).start()
        links.vectors(1, section, links.relative(2)).start()
        for piece, copies in enumerate((pieces[:1], pieces[1:2], pieces[2:3], pieces[3:5], pieces[5:6], pieces[6:])):
            for copy in copies:
                copy.wait()
            links.to_sibling(piece, section).start()

            @pl.when(links.core == 0)
            def _():
                links.over_y(piece, section).start()
    else:
        loads += [pltpu.make_async_copy(w_hbm, w_s, load_sem.at[2]),
                  pltpu.make_async_copy(wd_hbm, wd_s, load_sem.at[3]),
                  pltpu.make_async_copy(vec_hbm, vec_s, load_sem.at[4])]
        for copy in loads:
            copy.start()

    wide_masks = [jnp.concatenate([mask, mask], axis=1) for mask in half_masks()]
    lane_sub = iota((SUB, SUB), 1)
    row_sub = iota((SUB, SUB), 0)

    noise_row = noise_ref[pl.ds(section, 1), :].astype(F32)
    diagonal = iota((samples, samples), 0) == iota((samples, samples), 1)
    noise_col = jnp.sum(jnp.where(diagonal, noise_row, 0.0), axis=1, keepdims=True)
    half = cols // 2
    frequency = jnp.exp(iota((1, half), 1).astype(F32) * (-math.log(10000.0) / half))
    angles = noise_col * frequency
    sinus = low(jnp.concatenate([jnp.sin(angles), jnp.cos(angles)], axis=1))
    sinus_s[...] = sinus
    tok_s[:samples, :] = low(dot(sinus, tw_ref[...]))
    obs_count = repeat_ref.shape[-1]
    for index in range(obs_ref.shape[1]):
        tok_s[samples + index * obs_count : samples + (index + 1) * obs_count, :] = obs_ref[:, index, :]
    counts = low(repeat_ref[section].astype(F32))
    token_of = iota((obs_count, SUB), 1) - samples
    owner_of = iota((obs_count, SUB), 0)
    is_obs = token_of >= 0
    before = low((is_obs & (owner_of < token_of % obs_count)).astype(F32))
    upto = low((is_obs & (owner_of <= token_of % obs_count)).astype(F32))
    counts8 = jnp.broadcast_to(counts, (8, obs_count))
    starts = dot(counts8, before)[:1, :]
    ends = dot(counts8, upto)[:1, :]

    def select_rows(index, carried):
        key = iota((KEYS, SUB), 0) // per_sub
        lane = iota((KEYS, SUB), 1)
        sample = index * per_sub + iota((KEYS, SUB), 0) % per_sub
        sample_f = sample.astype(F32)
        time_hit = (key == 0) & (lane == sample)
        token = lane - samples
        owned = (sample_f >= starts) & (sample_f < ends)
        obs_hit = (token >= 0) & (token // obs_count == key - 1) & owned
        folded_s[index, :, :SUB] = (time_hit | obs_hit).astype(F32)
        return carried

    lax.fori_loop(0, tokens // SUB, select_rows, 0)
    selected = folded_s[...].reshape(-1, 2 * cols)[:, :SUB]
    select_s[...] = low(selected)
    selected = jnp.concatenate([selected, jnp.zeros((2 * SUB - selected.shape[0], SUB), F32)], axis=0)
    turned_s[...] = low(jnp.transpose(selected))
    same = row_sub // horizon == lane_sub // horizon
    causal_s[...] = jnp.where(same & (row_sub <= lane_sub), 0.0, -1e30)
    third = WIDE // 3
    own_s[...] = (iota((third, SUB), 0) % per_sub == iota((third, SUB), 1) // horizon).astype(F32)
    head_mask = (iota((third, cols), 0) // per_sub == iota((third, cols), 1) // (cols // HEADS)).astype(F32)
    dmem_s[...] = jnp.zeros_like(dmem_s)
    dvec_s[...] = jnp.zeros_like(dvec_s)
    for copy in loads:
        copy.wait()

    def vec(block, row):
        return vec_s[block, row : row + 1, :]

    def weight(block, start, stop):
        return w_s[block, :, start:stop]

    def condition(block):
        kv = dot(tok_s[...], weight(block, W_CKV, W_CQ))
        keys = low(kv[:, :cols])
        vals = low(kv[:, cols:] + vec(block, SHIFT + 7))

        spread = dot(select_s[...], jnp.concatenate([keys, vals], axis=1))
        both_masks = jnp.concatenate([head_mask, head_mask], axis=1)
        for index in range(tokens // SUB):
            for key in range(3):
                start = index * KEYS + key * per_sub
                copies = jnp.concatenate([spread[start : start + per_sub]] * HEADS, axis=0)
                wide_s[index, key * third : (key + 1) * third, :] = low(copies * both_masks)

    def fold(values):
        parts = []
        for part in thirds(values):
            part = part * head_mask
            parts.append(sum(part[head * per_sub : (head + 1) * per_sub] for head in range(HEADS)))
        return jnp.concatenate(parts, axis=0)

    def thirds(values):
        return [values[third * key : third * (key + 1)] for key in range(3)]

    def over_heads(values):
        return jnp.concatenate([values[:, :SUB], values[:, SUB:]], axis=0)

    def each_chunk(chunk, body):
        def at(step, carried):
            start = step * chunk
            body(pl.ds(start if isinstance(start, int) else pl.multiple_of(start, chunk), chunk), step)
            return carried

        if chunk == tokens:
            at(0, 0)
        else:
            lax.fori_loop(0, tokens // chunk, at, 0)

    def scale_of(block, rows, place):
        held = scale_s[rows, :]
        lane = iota(held.shape, 1)
        return jnp.sum(jnp.where(lane == 3 * block + place, held, 0.0), axis=1, keepdims=True)

    def keep_scale(block, rows, place, scale):
        held = scale_s[rows, :]
        scale_s[rows, :] = jnp.where(iota(held.shape, 1) == 3 * block + place, scale, held)

    def wide(values):
        return jnp.concatenate(values, axis=1)

    def both_heads(values):
        return jnp.concatenate([values * wide_masks[0], values * wide_masks[1]], axis=0)

    def both_pairs(values):
        zero = jnp.zeros((SUB, SUB), BF16)
        return jnp.concatenate([wide([values[:, :SUB], zero]), wide([zero, values[:, SUB:]])], axis=0)

    def forward(block, carried):
        after = jnp.minimum(block + 1, blocks - 1)
        if remote:
            links.arrive(block, (0, 1, 2))
        condition(block)

        def self_attention(rows, step):
            x = pred_ref[rows, :].astype(F32)
            unit0, scale0 = normalize(x)
            unit_s[block, 0, rows, :] = low(unit0)
            a = low(unit0 * vec(block, 0) + vec(block, SHIFT))
            q = low((dot(a, weight(block, 0, cols)) + vec(block, SHIFT + 3)) * score_scale)
            k = low(dot(a, weight(block, cols, 2 * cols)))
            v = low(dot(a, weight(block, 2 * cols, 3 * cols)) + vec(block, SHIFT + 4))
            qkv_s[block, rows, :cols] = q
            qkv_s[block, rows, cols : 2 * cols] = k
            qkv_s[block, rows, 2 * cols :] = v
            causal2 = wide([causal_s[...]] * 2)
            parts = []
            for sub in range(rows.size // SUB):
                span = slice(sub * SUB, (sub + 1) * SUB)
                scores = dot_nt(both_pairs(k[span]), both_heads(q[span]))
                stacked = []
                for pair in range(2):
                    score = scores[pair * SUB : (pair + 1) * SUB] + causal2
                    top = jnp.max(score, axis=0, keepdims=True)
                    expo = jnp.exp(score - top)
                    prob = low(expo * (1.0 / jnp.sum(expo, axis=0, keepdims=True)))
                    prob_s[block, step * (rows.size // SUB) + sub, pair] = prob
                    stacked.append(over_heads(prob))
                both = dot_tn(wide(stacked), both_heads(v[span]))
                parts.append(low(wide([both[:SUB, :SUB], both[SUB:, SUB:]])))
            context = jnp.concatenate(parts, axis=0)
            ctx_s[block, rows, :] = context
            x = x + (dot(context, weight(block, W_SO, W_CKV)) + vec(block, SHIFT + 5))
            g_s[rows, :] = x
            keep_scale(block, rows, 0, scale0)
            if remote:
                links.pass_on(block, block > 0, (2, 3))
                links.pass_on(block, block == 0, (2, 4), (2, 5))
                links.pass_on(after, block + 1 < blocks, (1, 0), (1, 1), (1, 2))
                links.start_y(block == 0, range(PIECES))

        each_chunk(FORWARD_SELF, self_attention)
        if remote:
            links.arrive(block, (3,))

        def cross_attention(rows, step):
            x = g_s[rows, :]
            unit1, scale1 = normalize(x)
            unit_s[block, 1, rows, :] = low(unit1)
            c = low(unit1 * vec(block, 1) + vec(block, SHIFT + 1))
            cq = low((dot(c, weight(block, W_CQ, W_CO)) + vec(block, SHIFT + 6)) * score_scale)
            cq_s[block, rows, :] = cq
            parts = []
            for sub in range(rows.size // SUB):
                index = step * (rows.size // SUB) + sub
                scores = thirds(dot_nt(wide_s[index, :, :cols], cq[sub * SUB : (sub + 1) * SUB]))
                top = jnp.maximum(jnp.maximum(scores[0], scores[1]), scores[2])
                expos = [jnp.exp(score - top) for score in scores]
                inverse = own_s[...] / (expos[0] + expos[1] + expos[2])
                prob = low(jnp.concatenate([expo * inverse for expo in expos], axis=0))
                cprob_s[block, index] = prob
                parts.append(low(dot_tn(prob, wide_s[index, :, cols:])))
            context = jnp.concatenate(parts, axis=0)
            cctx_s[block, rows, :] = context
            x = x + (dot(context, weight(block, W_CO, W_UP)) + vec(block, SHIFT + 8))
            unit2, scale2 = normalize(x)
            unit_s[block, 2, rows, :] = low(unit2)
            keep_scale(block, rows, 1, scale1)
            keep_scale(block, rows, 2, scale2)
            g_s[rows, :] = x + vec(block, SHIFT + 9)
            dy_s[0, rows, :] = low(unit2 * vec(block, 2) + vec(block, SHIFT + 2))
            if remote:
                links.pass_on(block, block > 0, (2, 4), (2, 5))
                links.pass_on(after, block + 1 < blocks, (1, 3))

        each_chunk(FORWARD_CROSS, cross_attention)
        if remote:
            links.arrive(block, (4, 5))

        def feed_forward(rows, step):
            e = dy_s[0, rows, :]
            root = math.sqrt(2.0 / math.pi)
            cube = root * 0.044715
            for part in range(4):
                lanes = slice(part * cols, (part + 1) * cols)
                u = low(dot(e, weight(block, W_UP + part * cols, W_UP + (part + 1) * cols)) + vec(
                    block, BIAS + part
                ))
                square = u * u
                gate = jnp.tanh(u * (square * low(cube) + low(root))) * low(0.5) + low(0.5)
                hidden = u * gate
                slope = gate + hidden * (low(1.0) - gate) * (square * low(6.0 * cube) + low(2.0 * root))
                hid_s[block % ring, rows, lanes] = hidden
                slope_s[block % ring, rows, lanes] = slope
            pred_ref[rows, :] = low(g_s[rows, :] + dot(hid_s[block % ring, rows, :], wd_s[block]))
            if remote:
                links.pass_on(after, block + 1 < blocks, (2, 0), (2, 1), (2, 2), (1, 4), (1, 5))

        @pl.when(block == ring)
        def _():
            for copy in out_copies:
                copy.wait()

        each_chunk(FORWARD_FF, feed_forward)

        @pl.when(block == 0)
        def _():
            for copy in out_copies:
                copy.start()

        return carried

    if remote:
        links.pass_on(0, True, (1, 0), (1, 1), (2, 0), (1, 2), (2, 1), (1, 3), (2, 2), (1, 4), (2, 3), (1, 5))
    lax.fori_loop(0, blocks, forward, 0)

    def put(kind, start, value):
        width, taken = WIDTHS[kind], 0
        while taken < value.shape[1]:
            index, place = (start + taken) // width, (start + taken) % width
            count = min(value.shape[1] - taken, width - place)
            part = low(value[:, taken : taken + count]).reshape(NZ, NX, ROWS, count)
            groups[kind][index, :, :, :, place : place + count] = part
            taken += count

    def emit(block, kind):
        if remote:
            links.near(kind).start()
        else:
            copy = pltpu.make_async_copy(groups[kind], dw_refs[kind].at[block], load_sem.at[2])
            copy.start()
            copy.wait()

    def store_down(first, second):
        blocks_of = [value[:, q * SUB : (q + 1) * SUB] for value in (first, second) for q in range(4)]
        dn_out[...] = jnp.transpose(jnp.concatenate(blocks_of, axis=0))

    def store_up(first, second):
        up_out[...] = wide([first, second])

    def store_cross(first, second):
        joined = wide([first, second])
        ckv_out[...] = joined[:, : 2 * cols]
        for place, out in enumerate((cq_out, co_out, so_out)):
            out[...] = joined[:, (2 + place) * cols : (3 + place) * cols]

    def store_self(first, second):
        in_out[...] = wide([first, second])

    stores = (store_down, store_up, store_cross, store_self)

    def advance(works):
        if not remote:
            return
        for kind, stage, block, there in works:

            def run(kind=kind, stage=stage, block=block):
                if stage == 1:
                    links.after_near(kind)
                elif stage == 2:
                    links.after_row(kind, block)
                elif stage == 3:
                    links.after_far(kind, block)
                else:
                    links.after_last(kind, block, stores[kind])

            if there is True:
                run()
            else:
                pl.when(there)(run)

    def time_gradient():
        dmem = dmem_s[...]
        dmem_high = low(dmem)
        dmem_low = low(dmem - dmem_high.astype(F32))
        return dot_tn(sinus_s[...], dmem_high) + dot_tn(sinus_s[...], dmem_low)

    def emit_vectors():
        vectors = dvec_s[...].reshape(blocks * VEC_ROWS, cols)
        vectors = jnp.concatenate([vectors, jnp.zeros((SUB - blocks * VEC_ROWS, cols), F32)], axis=0)
        turned = jnp.transpose(vectors).reshape(GROUPS, ROWS, SUB)
        lane = iota((ROWS, SUB), 1) % VEC_ROWS
        rows_out = []
        for group in range(GROUPS):
            part, high = group // 2, group % 2
            piece = turned[group]
            for j in range(4):
                source = turned[4 * high + j]
                if j != part:
                    source = pltpu.roll(source, (j - part) % SUB, 1)
                piece = jnp.where(lane == BIAS + j, source, piece)
            rows_out.append(piece)
        turned = jnp.concatenate(rows_out, axis=0)
        for index in range(2):
            sets[VECTOR][0][index] = low(turned).reshape(NZ, NX, ROWS, SUB)
        links.near(VECTOR).start()

    def backward(turn, carried):
        block = blocks - 1 - turn
        earlier, before = block + 1, block + 2
        again, third_turn = turn > 0, turn > 1

        def add_vec(row, values):
            dvec_s[block, row : row + 1, :] += values

        def turn_over_ones(left):
            return jnp.concatenate([jnp.transpose(left), jnp.ones((16, tokens), BF16)], axis=0)

        def put_scaled(kind, start, unit_row, right, sum_rows):
            turned = turn_over_ones(unit_s[block, unit_row])
            gain = place_column(vec(block, unit_row))
            shift = place_column(vec(block, SHIFT + unit_row))
            parts = []
            for place, row in enumerate(sum_rows):
                both = dot(turned, right[:, place * cols : (place + 1) * cols])
                sums = both[cols : cols + 1]
                dvec_s[block, row : row + 1, :] = sums
                put(kind, start + place * cols, both[:cols] * gain + shift * sums)
                parts.append((both[:cols], sums))
            return parts

        def put_plain(kind, start, left, right, row):
            both = dot(turn_over_ones(left), right)
            dvec_s[block, row : row + 1, :] = both[cols : cols + 1]
            put(kind, start, both[:cols])

        @pl.when(block == 0)
        def _():
            for copy in back_copies:
                copy.wait()

        turned = jnp.transpose(grad_ref[...])
        for part in range(4):
            piece = low(dot(turned, hid_s[block % ring, :, part * cols : (part + 1) * cols]))
            for index in range(2):
                for x in range(NX):
                    for q in range(4):
                        row = SUB * index + ROWS * q
                        groups[DOWN][index, part, x, :, q * SUB : (q + 1) * SUB] = piece[
                            row : row + ROWS, x * SUB : (x + 1) * SUB
                        ]
        def feed_forward(rows, step):
            dy3 = grad_ref[rows, :]
            g = dy3.astype(F32)
            add_vec(SHIFT + 9, jnp.sum(g, axis=0, keepdims=True))
            for part in range(4):
                lanes = slice(part * cols, (part + 1) * cols)
                dh = dot_nt(dy3, wd_s[block, lanes, :])
                slope_s[block % ring, rows, lanes] = low(dh) * slope_s[block % ring, rows, lanes]
            de = dot_nt(slope_s[block % ring, rows, :], weight(block, W_UP, W_END))
            back, along, flat = normalize_back(
                de, unit_s[block, 2, rows, :].astype(F32), scale_of(block, rows, 2), vec(block, 2)
            )
            add_vec(2, along)
            add_vec(SHIFT + 2, flat)
            g = g + back
            g_s[rows, :] = g
            dy_s[0, rows, :] = low(g)

        each_chunk(BACK_FF, feed_forward)
        advance((
            (DOWN, 3, earlier, again), (UP, 2, earlier, again), (SELF, 1, earlier, again),
            (UP, 4, before, third_turn), (CROSS, 4, before, third_turn), (SELF, 4, before, third_turn),
        ))
        emit(block, DOWN)
        pl.when(turn == 0)(back_copies[0].start)

        put_scaled(UP, 0, 2, slope_s[block % ring], [BIAS + part for part in range(4)])
        condition(block)
        advance(((CROSS, 2, earlier, again),))
        emit(block, UP)
        pl.when(turn == 0)(back_copies[1].start)

        def cross_attention(rows, step):
            dctx = low(dot_nt(dy_s[0, rows, :], weight(block, W_CO, W_UP)))
            for sub in range(rows.size // SUB):
                index = step * (rows.size // SUB) + sub
                span = pl.ds(index * SUB if isinstance(index, int) else pl.multiple_of(index * SUB, SUB), SUB)
                keys, vals = wide_s[index, :, :cols], wide_s[index, :, cols:]
                part = dctx[sub * SUB : (sub + 1) * SUB]
                prob = cprob_s[block, index]
                prob32 = prob.astype(F32)
                weighted = prob32 * dot_nt(vals, part)
                inner = sum(thirds(weighted))
                dscore = low(weighted - prob32 * jnp.concatenate([inner] * 3, axis=0))
                folded_s[index, :, :cols] = fold(dot(dscore, cq_s[block, span, :]))
                folded_s[index, :, cols:] = fold(dot(prob, part))
                cq_s[block, span, :] = low(dot_tn(dscore, keys) * score_scale)
            dcq = cq_s[block, rows, :]
            dc = dot_nt(dcq, weight(block, W_CQ, W_CO))
            back, along, flat = normalize_back(
                dc, unit_s[block, 1, rows, :].astype(F32), scale_of(block, rows, 1), vec(block, 1)
            )
            add_vec(1, along)
            add_vec(SHIFT + 1, flat)
            g = g_s[rows, :] + back
            g_s[rows, :] = g
            dy_s[1, rows, :] = low(g)

        each_chunk(BACK_CROSS, cross_attention)
        advance(((DOWN, 1, block, True), (DOWN, 4, earlier, again)))

        folded = folded_s[...].reshape(-1, 2 * cols)
        dkv32 = dot(turned_s[:, : folded.shape[0]], low(folded))
        dkv = low(dkv32)
        add_vec(SHIFT + 7, jnp.sum(dkv32[:, cols:], axis=0, keepdims=True))
        dmem_s[...] += dot_nt(dkv[:samples], weight(block, W_CKV, W_CQ))
        put(CROSS, 0, dot_tn(tok_s[...], dkv))
        put_scaled(CROSS, 2 * cols, 1, cq_s[block], [SHIFT + 6])
        put_plain(CROSS, 3 * cols, cctx_s[block], dy_s[0], SHIFT + 8)
        put_plain(CROSS, 4 * cols, ctx_s[block], dy_s[1], SHIFT + 5)
        advance(((SELF, 2, earlier, again), (UP, 1, block, True)))
        emit(block, CROSS)
        if remote:

            @pl.when(block == 0)
            def _():
                dtime = time_gradient()
                for index in range(2):
                    part = low(dtime[:, index * SUB : (index + 1) * SUB])
                    sets[TIME][0][index] = part.reshape(NZ, NX, ROWS, SUB)
                links.near(TIME).start()

        def self_attention(rows, step):
            dctx = low(dot_nt(dy_s[1, rows, :], weight(block, W_SO, W_CKV)))
            for sub in range(rows.size // SUB):
                index = step * (rows.size // SUB) + sub
                span = pl.ds(index * SUB if isinstance(index, int) else pl.multiple_of(index * SUB, SUB), SUB)
                part = dctx[sub * SUB : (sub + 1) * SUB]
                queries, keys, values = (qkv_s[block, span, place * cols : (place + 1) * cols] for place in range(3))
                sides = (slice(0, SUB), slice(SUB, 2 * SUB))
                dstack = both_heads(part)
                qstack = both_heads(queries)
                kstack = both_heads(keys)
                probs = [prob_s[block, index, pair] for pair in range(2)]
                dprobs = dot_nt(both_pairs(values), dstack)
                dprobs = [dprobs[side] for side in sides]
                dscores = []
                for prob, dprob in zip(probs, dprobs):
                    prob32 = prob.astype(F32)
                    weighted = prob32 * dprob
                    dscores.append(low(weighted - prob32 * jnp.sum(weighted, axis=0, keepdims=True)))
                dq = dot_tn(wide([over_heads(dscore) for dscore in dscores]), kstack)
                dq = [dq[side, side] for side in sides]
                dk = dot(jnp.concatenate(dscores, axis=0), qstack)
                dk = [dk[side, side] for side in sides]
                dv = dot(jnp.concatenate(probs, axis=0), dstack)
                dv = [dv[side, side] for side in sides]
                qkv_s[block, span, :cols] = low(wide(dq) * score_scale)
                qkv_s[block, span, cols : 2 * cols] = low(wide(dk))
                qkv_s[block, span, 2 * cols :] = low(wide(dv))

        each_chunk(BACK_SELF, self_attention)
        advance((
            (UP, 3, earlier, again), (CROSS, 3, earlier, again), (DOWN, 2, block, True),
            (CROSS, 1, block, True), (TIME, 1, block, block == 0),
        ))

        gain_column, shift_column = 0.0, 0.0
        for place, (both, sums) in enumerate(
            put_scaled(SELF, 0, 0, qkv_s[block], (SHIFT + 3, KEYSUM, SHIFT + 4))
        ):
            matrix = weight(block, place * cols, (place + 1) * cols).astype(F32)
            gain_column += jnp.sum(both * matrix, axis=1, keepdims=True)
            shift_column += jnp.sum(sums * matrix, axis=1, keepdims=True)
        dvec_s[block, 0:1, :] = place_row(gain_column)
        dvec_s[block, SHIFT : SHIFT + 1, :] = place_row(shift_column)
        emit(block, SELF)
        if remote:
            pl.when(block == 0)(emit_vectors)

        def self_norm(rows, step):
            da = dot_nt(qkv_s[block, rows, :], weight(block, 0, 3 * cols))
            back, _, _ = normalize_back(
                da, unit_s[block, 0, rows, :].astype(F32), scale_of(block, rows, 0), vec(block, 0)
            )
            grad_ref[rows, :] = low(g_s[rows, :] + back)

        each_chunk(BACK_SELF, self_norm)
        advance(((SELF, 3, earlier, again),))
        return carried

    lax.fori_loop(0, blocks, backward, 0)
    if not remote:
        time_out[...] = time_gradient()
        dvec_ref[...] = dvec_s[...]
        return

    links.after_row(UP, 0)
    links.after_near(SELF)
    links.after_near(VECTOR)
    links.after_far(DOWN, 0)
    links.after_row(CROSS, 0)
    links.after_row(TIME, 0)
    links.after_last(UP, 1, store_up)
    links.after_last(CROSS, 1, store_cross)
    links.after_far(UP, 0)
    links.after_row(SELF, 0)
    links.after_row(VECTOR, 0)
    links.after_last(SELF, 1, store_self)
    links.after_last(DOWN, 0, store_down)
    links.after_far(CROSS, 0)
    links.after_far_all(TIME)
    links.after_last(UP, 0, store_up)
    links.after_far(SELF, 0)
    links.after_far_all(VECTOR)
    links.after_last(CROSS, 0, store_cross)
    time_out[...] = wide(links.after_last_all(TIME))
    links.after_last(SELF, 0, store_self)
    mine, _ = links.after_last_all(VECTOR)
    padded = jnp.concatenate([mine, jnp.zeros((SUB - ROWS, SUB), F32)], axis=0)
    flat_s[...] = jnp.transpose(padded)
    mine = flat_s[pl.ds(pl.multiple_of(section * VEC_ROWS, 8), VEC_ROWS), :]
    for row in range(SHIFT):
        gains_out[row] = mine[row : row + 1, :ROWS]
    for row in range(SHIFT, BIAS):
        shifts_out[row - SHIFT] = mine[row : row + 1, :ROWS]
    bias = mine[BIAS : BIAS + 1, :]
    for part in range(1, 4):
        bias = bias + pltpu.roll(mine[BIAS + part : BIAS + part + 1, :], part * ROWS, 1)
    bias_out[...] = bias
    links.finish_weights()


def run_blocks(remote, x, cot, obs, repeat, noise, time_weight, *weights, interpret=False):
    tokens, cols = x.shape
    blocks = 4
    samples = noise.shape[1]
    vmem = pl.BlockSpec(memory_space=pltpu.VMEM)
    hbm = pl.BlockSpec(memory_space=pl.ANY)
    half_rows = (NZ, NX, ROWS)
    scratch = [
        pltpu.VMEM((blocks, 3, tokens, cols), BF16),
        pltpu.VMEM((tokens, SUB), F32),
        pltpu.VMEM((blocks, tokens, 3 * cols), BF16),
        pltpu.VMEM((blocks, tokens // SUB, 2, SUB, 2 * SUB), BF16),
        pltpu.VMEM((blocks, tokens, cols), BF16),
        pltpu.VMEM((blocks, tokens, cols), BF16),
        pltpu.VMEM((blocks, tokens // SUB, WIDE, SUB), BF16),
        pltpu.VMEM((blocks, tokens, cols), BF16),
        pltpu.VMEM((blocks - 1, tokens, 4 * cols), BF16),
        pltpu.VMEM((blocks - 1, tokens, 4 * cols), BF16),
        pltpu.VMEM((2, tokens, cols), BF16),
        pltpu.VMEM((tokens, cols), F32),
        pltpu.VMEM((blocks, cols, W_END), BF16),
        pltpu.VMEM((blocks, 4 * cols, cols), BF16),
        pltpu.VMEM((blocks, VEC_ROWS, cols), F32),
        pltpu.VMEM((blocks, VEC_ROWS, cols), F32),
        pltpu.VMEM((tokens // SUB * KEYS, SUB), BF16),
        pltpu.VMEM((SUB, 2 * SUB), BF16),
        pltpu.VMEM((SUB, cols), BF16),
        pltpu.VMEM((tokens // SUB, WIDE, 2 * cols), BF16),
        pltpu.VMEM((tokens // SUB, KEYS, 2 * cols), F32),
        pltpu.VMEM((samples, cols), F32),
        pltpu.VMEM((samples, cols), BF16),
        pltpu.VMEM((SUB, SUB), F32),
        pltpu.VMEM((WIDE // 3, SUB), F32),
        pltpu.VMEM((SUB, SUB), F32),
        pltpu.SemaphoreType.DMA((12,)),
    ]
    scratch += [pltpu.VMEM((2,) + half_rows + (width,), BF16) for width in WIDTHS[:TIME]]
    if remote:
        scratch += [pltpu.SemaphoreType.DMA((5 * PIECES + 3,))] * 2
        for kind, width in enumerate(WIDTHS):
            if kind >= TIME:
                scratch.append(pltpu.VMEM((2,) + half_rows + (width,), BF16))
            scratch += [
                pltpu.VMEM(half_rows + (width,), BF16),
                pltpu.VMEM((NZ, ROWS, width), BF16),
                pltpu.VMEM(((2 if kind in TURNS else 1) * (NZ - 1), ROWS, width), BF16),
                pltpu.VMEM((3, ROWS, width), BF16),
                pltpu.VMEM((ROWS, width), BF16),
                pltpu.VMEM((NZ, ROWS, width), BF16),
                pltpu.SemaphoreType.DMA((3 + 2 * NZ,)),
                pltpu.SemaphoreType.DMA((3 + 2 * NZ,)),
            ]
        shapes = ((ROWS, 3 * cols), (ROWS, cols), (ROWS, cols), (ROWS, 2 * cols), (ROWS, cols),
                  (ROWS, 4 * cols), (4 * ROWS, cols), (SHIFT, 1, ROWS), (BIAS - SHIFT, 1, ROWS), (1, 4 * ROWS),
                  (ROWS, cols))
        outs = tuple(jax.ShapeDtypeStruct(shape, F32) for shape in shapes)
        in_specs = [hbm, hbm] + [vmem] * 4 + [hbm] * 7 + [vmem] * 3
        out_specs = (vmem,) * (2 + len(outs))
        params = pltpu.CompilerParams(
            vmem_limit_bytes=VMEM_BYTES, collective_id=0, has_side_effects=True)
    else:
        outs = (
            jax.ShapeDtypeStruct((blocks, VEC_ROWS, cols), F32),
            jax.ShapeDtypeStruct((cols, cols), F32),
        )
        outs = tuple(
            jax.ShapeDtypeStruct((blocks, 2) + half_rows + (width,), BF16) for width in WIDTHS[:TIME]
        ) + outs
        in_specs = [hbm, hbm] + [vmem] * 4 + [hbm] * 3
        out_specs = (vmem, vmem) + (hbm,) * 4 + (vmem, vmem)
        params = pltpu.CompilerParams(vmem_limit_bytes=VMEM_BYTES)
    low_out = jax.ShapeDtypeStruct((tokens, cols), BF16)
    away = jax.ShapeDtypeStruct((tokens, 4 * cols), BF16)
    return pl.pallas_call(
        functools.partial(block_kernel, remote),
        out_shape=(low_out, low_out) + outs + (away, away),
        in_specs=in_specs,
        out_specs=out_specs + (hbm, hbm),
        scratch_shapes=scratch,
        compiler_params=params,
        interpret=interpret,
    )(x, cot, obs, repeat, noise, time_weight, *weights)


def hand_out(*refs):
    count = (len(refs) - 1) // 3
    held, sem = refs[2 * count : 3 * count], refs[-1]
    arriving = [pltpu.make_async_copy(refs[i], held[i], sem.at[i]) for i in range(count)]
    leaving = []
    for copy in arriving:
        copy.start()
    for index in range(count):
        target = refs[count + index]
        if len(target.shape) > len(held[index].shape):
            target = target.at[0]
        arriving[index].wait()
        leaving.append(pltpu.make_async_copy(held[index], target, sem.at[index]))
        leaving[-1].start()
    for copy in leaving:
        copy.wait()


def finished(results):
    hbm = pl.BlockSpec(memory_space=pl.ANY)
    shapes = [(1,) + result.shape for result in results[:9]] + [result.shape for result in results[9:]]
    return pl.pallas_call(
        hand_out,
        out_shape=tuple(jax.ShapeDtypeStruct(shape, result.dtype) for shape, result in zip(shapes, results)),
        in_specs=[hbm] * len(results),
        out_specs=(hbm,) * len(results),
        scratch_shapes=[pltpu.VMEM(result.shape, result.dtype) for result in results]
        + [pltpu.SemaphoreType.DMA((len(results),))],
    )(*results)


def pack_weights(self_in, self_out, cross_q, cross_kv, cross_out, mlp_up, mlp_down):
    parts = (self_in, self_out, cross_kv, cross_q, cross_out, mlp_up)
    return jnp.concatenate([part[0] for part in parts], axis=1), mlp_down[0]


def pack_vectors(gains, shifts, mlp_bias):
    cols = gains.shape[-1]
    rows = jnp.concatenate([gains[0], shifts[0], mlp_bias.reshape(4, cols)], axis=0)
    return jnp.pad(rows, ((0, VEC_ROWS - rows.shape[0]), (0, 0)))


def natural(dweights):
    def joined(kind):
        parts = dweights[kind].reshape(-1, 2, GROUPS * ROWS, WIDTHS[kind])
        return jnp.concatenate([parts[:, 0], parts[:, 1]], axis=-1)

    blocks = dweights[DOWN].shape[0]
    down = dweights[DOWN].reshape(blocks, 2, GROUPS, ROWS, 4, SUB).transpose(0, 2, 5, 1, 4, 3)
    return joined(UP), joined(CROSS), joined(SELF), down.reshape(blocks, GROUPS * SUB, -1)


def gathered(data, packed_weights, packed_vectors):
    sections = lax.axis_size("section")
    groups = lax.axis_size("dp")
    cols = data[0].shape[-1]
    weights = [lax.all_gather(part, "section", axis=0) for part in packed_weights]
    vectors = lax.all_gather(packed_vectors, "section", axis=0)
    pred, grad, *dweights, dvectors, dtime, _, _ = run_blocks(False, *data, *weights, vectors)
    rows = cols // groups
    up, cross, own, down = natural(dweights)
    rest = jnp.concatenate([up, cross, own], axis=2).reshape(sections, groups, -1)
    down = down.reshape(sections, groups, -1)
    small = dvectors[:, :BIAS].reshape(sections, BIAS, groups, rows).transpose(0, 2, 1, 3)
    small = small.reshape(sections, groups, BIAS * rows)
    bias = dvectors[:, BIAS:KEYSUM].reshape(sections, groups, 4 * rows)
    term = jnp.broadcast_to(dtime.reshape(1, groups, rows * cols), (sections, groups, rows * cols))
    sent = jnp.concatenate([rest, down], axis=2).reshape(sections * groups, -1)
    sent_small = jnp.concatenate([small, bias, term], axis=2).reshape(sections * groups, -1)
    got = lax.psum_scatter(sent, ("section", "dp"), scatter_dimension=0, tiled=True)[0].astype(F32)
    got_small = lax.psum_scatter(sent_small, ("section", "dp"), scatter_dimension=0, tiled=True)[0]
    widths = (up.shape[-1], cross.shape[-1], own.shape[-1])
    split = sum(widths) * rows
    rest = got[:split].reshape(rows, sum(widths))
    down = got[split:].reshape(4 * rows, cols)
    small = got_small[: BIAS * rows].reshape(BIAS, rows)
    bias = got_small[BIAS * rows : (BIAS + 4) * rows].reshape(4, rows)
    term = got_small[(BIAS + 4) * rows :].reshape(rows, cols)
    up, cross, own = jnp.split(rest, (widths[0], widths[0] + widths[1]), axis=1)
    kv, query, out, self_out = jnp.split(cross, (2 * cols, 3 * cols, 4 * cols), axis=1)
    return (pred, grad, own, self_out, query, kv, out, up, down, small[:SHIFT], small[SHIFT:], bias, term)


def local(
    horizon, cotangent, obs_tokens, obs_repeat, noise_step, time_weight,
    self_in, self_out, cross_q, cross_kv, cross_out, mlp_up, mlp_down, gains, shifts, mlp_bias,
):
    cols = horizon.shape[-1]
    data = (horizon[0], cotangent[0], obs_tokens[0], obs_repeat, noise_step, time_weight)
    weights = (self_in, self_out, cross_q, cross_kv, cross_out, mlp_up, mlp_down)
    if lax.axis_size("dp") == GROUPS:
        vectors = (gains.transpose(1, 0, 2), shifts.transpose(1, 0, 2), mlp_bias)
        results = finished(run_blocks(True, *data, *weights, *vectors)[:-2])
        return results[:9] + (results[9].transpose(1, 0, 2), results[10].transpose(1, 0, 2)) + results[11:]
    results = gathered(data, pack_weights(*weights), pack_vectors(gains, shifts, mlp_bias))
    return tuple(result[None] for result in results[:11]) + (results[11].reshape(1, -1), results[12])


def solution(mesh):
    whole = P("section", None, None)
    return jax.shard_map(
        local,
        mesh=mesh,
        in_specs=(
            P("section", "dp", None), P("section", "dp", None), P("section", "dp", None, None),
            P(None, "dp", None), P(None, "dp"), P(),
            whole, whole, whole, whole, whole, whole, whole, whole, whole, P("section", None),
        ),
        out_specs=(P("section", "dp", None),) * 9
        + (P("section", None, "dp"), P("section", None, "dp"), P("section", "dp"), P("dp", None)),
        check_vma=False,
    )
```

```python
import functools
import math

import jax
import jax.numpy as jnp
from jax import lax
from jax.experimental import pallas as pl
from jax.experimental.pallas import tpu as pltpu
from jax.sharding import PartitionSpec as P

HEADS = 4
VMEM_BYTES = 63 * 1024 * 1024
SUB = 128
F32 = jnp.float32
BF16 = jnp.bfloat16

W_IN, W_SO, W_CKV, W_CQ, W_CO, W_UP, W_END = 0, 768, 1024, 1536, 1792, 2048, 3072
SHIFT, BIAS, KEYSUM, VEC_ROWS = 3, 13, 17, 24
SENT = ((W_IN, 512), (512, W_CKV), (W_CKV, W_CQ), (W_CQ, W_UP), (W_UP, W_END))
DOWN_PIECE, PIECES = 5, 6
DOWN, UP, CROSS, SELF, TIME, VECTOR = range(6)
WIDTHS = (512, 512, 640, 384, 128, 128)
FORWARD_SELF, FORWARD_CROSS, FORWARD_FF = 1024, 1024, 1024
BACK_FF, BACK_CROSS, BACK_SELF = 1024, 1024, 1024
ROWS, NZ, NX = 32, 4, 2
TURNS = (UP, SELF)
GROUPS = NZ * NX
KEYS, WIDE = 24, 96


def dot(left, right):
    return jnp.dot(left, right, preferred_element_type=F32)


def dot_nt(left, right):
    return lax.dot_general(left, right, (((1,), (1,)), ((), ())), preferred_element_type=F32)


def dot_tn(left, right):
    return lax.dot_general(left, right, (((0,), (0,)), ((), ())), preferred_element_type=F32)


def iota(shape, axis):
    return lax.broadcasted_iota(jnp.int32, shape, axis)


def low(values):
    return jnp.asarray(values, BF16)


def normalize(values):
    center = values - jnp.mean(values, axis=-1, keepdims=True)
    scale = lax.rsqrt(jnp.mean(center * center, axis=-1, keepdims=True) + 1e-05)
    return center * scale, scale


def normalize_back(grad, unit, scale, gain):
    ahead = grad * unit
    grad_unit = grad * gain
    mean_grad = jnp.mean(grad_unit, axis=-1, keepdims=True)
    mean_along = jnp.mean(ahead * gain, axis=-1, keepdims=True)
    back = (grad_unit - mean_grad - unit * mean_along) * scale
    return back, jnp.sum(ahead, axis=0, keepdims=True), jnp.sum(grad, axis=0, keepdims=True)


def half_masks():
    lane = iota((1, SUB), 1)
    first = (lane < SUB // 2).astype(F32)
    return low(first), low(1.0 - first)


def add_low(left, right):
    return left + right


def place_row(column):
    size = column.shape[0]
    diagonal = iota((size, size), 0) == iota((size, size), 1)
    return jnp.sum(jnp.where(diagonal, column, 0.0), axis=0, keepdims=True)


def place_column(row):
    size = row.shape[1]
    diagonal = iota((size, size), 0) == iota((size, size), 1)
    return jnp.sum(jnp.where(diagonal, row, 0.0), axis=1, keepdims=True)


class Links:
    def __init__(self, w_s, wd_s, vec_s, wsend, wrecv, sets):
        self.w, self.wd, self.vec, self.wsend, self.wrecv, self.sets = w_s, wd_s, vec_s, wsend, wrecv, sets
        self.section = lax.axis_index("section")
        self.group = lax.axis_index("dp")
        self.core, self.y = self.section % 2, self.section // 2
        self.x, self.z = self.group % NX, self.group // NX
        self.x_peer = self.z * NX + (self.x + 1) % NX

    def relative(self, step):
        return (self.y + step // 2) % 2 * 2 + (self.core + step % 2) % 2

    def relation(self, block):
        return (self.y + block // 2) % 2 * 2 + (self.core + block % 2) % 2

    def z_peer(self, step):
        return (self.z + step) % NZ * NX + self.x

    def greet(self):
        barrier = pltpu.get_barrier_semaphore()
        peers = [{"section": self.relative(step)} for step in (1, 2, 3)]
        peers += [{"dp": self.x_peer}] + [{"dp": self.z_peer(step)} for step in range(1, NZ)]
        for peer in peers:
            pl.semaphore_signal(barrier, inc=1, device_id=peer, device_id_type=pl.DeviceIdType.MESH)
        pl.semaphore_wait(barrier, len(peers))

    def remote(self, src, dst, send, recv, peer):
        return pltpu.make_async_remote_copy(
            src_ref=src, dst_ref=dst, send_sem=send, recv_sem=recv, device_id=peer,
            device_id_type=pl.DeviceIdType.MESH,
        )

    def weight_copy(self, slot, block, piece, half, peer):
        array, lanes = (self.wd, slice(None)) if piece == DOWN_PIECE else (self.w, slice(*SENT[piece]))
        part = array.at[block, :, lanes]
        if half is not None:
            rows = array.shape[1] // 2
            part = array.at[block, pl.ds(pl.multiple_of(half * rows, rows), rows), lanes]
        return self.remote(part, part, self.wsend.at[slot], self.wrecv.at[slot], peer)

    def vector_copy(self, slot, block, peer):
        part = self.vec.at[block]
        return self.remote(part, part, self.wsend.at[slot], self.wrecv.at[slot], peer)

    def to_sibling(self, piece, block):
        return self.weight_copy(piece, block, piece, None, {"section": self.relative(1)})

    def over_y(self, piece, block):
        return self.weight_copy(PIECES + piece, block, piece, self.x, {"section": self.relative(2)})

    def over_x(self, piece, block, half):
        return self.weight_copy(2 * PIECES + piece, block, piece, half, {"dp": self.x_peer})

    def forwarded(self, piece, block, half, which):
        return self.weight_copy((3 + which) * PIECES + piece, block, piece, half, {"section": self.relative(1)})

    def vectors(self, step, block, peer):
        return self.vector_copy(5 * PIECES + step, block, {"section": peer})

    def start_y(self, when, pieces):
        @pl.when(when & (self.core == 1))
        def _():
            for piece in pieces:
                self.over_y(piece, self.section).start()

    def pass_first(self, piece, block):
        self.over_y(piece, block).wait_recv()
        self.over_x(piece, block, self.x).start()
        self.forwarded(piece, block, self.x, 0).start()

    def pass_second(self, piece, block):
        self.over_x(piece, block, 1 - self.x).wait_recv()
        self.forwarded(piece, block, 1 - self.x, 1).start()

    def pass_on(self, block, when, *works):
        @pl.when(self.relation(block) == 2 if when is True else when & (self.relation(block) == 2))
        def _():
            for stage, piece in works:
                if stage == 1 and piece == 0:
                    self.vectors(1, block, self.relative(2)).wait_recv()
                    self.vectors(2, block, self.relative(1)).start()
                (self.pass_first if stage == 1 else self.pass_second)(piece, block)

    def arrive(self, block, pieces):
        relation = self.relation(block)

        @pl.when(relation == 1)
        def _():
            if 0 in pieces:
                self.vectors(0, block, self.relative(1)).wait_recv()
            for piece in pieces:
                self.to_sibling(piece, block).wait_recv()

        @pl.when(relation == 3)
        def _():
            if 0 in pieces:
                self.vectors(2, block, self.relative(1)).wait_recv()
            for piece in pieces:
                self.forwarded(piece, block, self.x, 0).wait_recv()
                self.forwarded(piece, block, 1 - self.x, 1).wait_recv()

    def finish_weights(self):
        own, passed = self.section, self.relative(2)
        self.vectors(0, own, self.relative(1)).wait_send()
        self.vectors(1, own, self.relative(2)).wait_send()
        self.vectors(2, passed, self.relative(1)).wait_send()
        for piece in range(PIECES):
            self.to_sibling(piece, own).wait_send()
            self.over_y(piece, own).wait_send()
            self.over_x(piece, passed, self.x).wait_send()
            self.forwarded(piece, passed, self.x, 0).wait_send()
            self.forwarded(piece, passed, 1 - self.x, 1).wait_send()

    def near(self, kind):
        group_s, near_s, _, _, _, _, _, send, recv = self.sets[kind]
        return self.remote(group_s.at[1 - self.core], near_s, send.at[0], recv.at[0],
                           {"section": self.relative(1)})

    def row(self, kind):
        group_s, _, row_s, _, _, _, _, send, recv = self.sets[kind]
        return self.remote(group_s.at[self.core, :, 1 - self.x], row_s, send.at[1], recv.at[1],
                           {"dp": self.x_peer})

    def far_slot(self, kind, step, block):
        return (block % 2) * (NZ - 1) + step - 1 if kind in TURNS else step - 1

    def far(self, kind, step, block):
        far_s, _, _, fold_s, send, recv = self.sets[kind][3:]
        slot = self.far_slot(kind, step, block)
        sem = slot + 2 if kind not in TURNS else 1 + step + (block % 2) * (NZ + 2)
        return self.remote(fold_s.at[(self.z + step) % NZ], far_s.at[slot], send.at[sem], recv.at[sem],
                           {"dp": self.z_peer(step)})

    def last(self, kind, step, peer):
        last_s, sum_s, _, send, recv = self.sets[kind][4:]
        slot = NZ + step
        return self.remote(sum_s, last_s.at[step - 1],
                           send.at[slot], recv.at[slot], {"section": peer})

    def after_near(self, kind):
        group_s, near_s = self.sets[kind][:2]
        self.near(kind).wait()
        group_s[self.core] = add_low(group_s[self.core], near_s[...])
        self.row(kind).start()

    def after_row(self, kind, block):
        group_s, row_s, fold_s = self.sets[kind][0], self.sets[kind][2], self.sets[kind][6]
        self.row(kind).wait()
        fold_s[...] = add_low(group_s[self.core, :, self.x], row_s[...])
        for step in range(1, NZ):
            self.far(kind, step, block).start()

    def sum_far(self, kind, block):
        far_s, _, sum_s, fold_s = self.sets[kind][3:7]
        for step in range(1, NZ):
            self.far(kind, step, block).wait()
        total = fold_s[self.z].astype(F32)
        for step in range(1, NZ):
            total = total + far_s[self.far_slot(kind, step, block)].astype(F32)
        sum_s[...] = low(total)

    def after_far(self, kind, block):
        self.sum_far(kind, block)
        relation = self.relation(block)

        @pl.when(relation > 0)
        def _():
            self.last(kind, relation, block).start()

    def halves(self, kind):
        last_s, sum_s = self.sets[kind][4:6]
        here = sum_s[...].astype(F32) + last_s[1].astype(F32)
        there = last_s[0].astype(F32) + last_s[2].astype(F32)
        return jnp.where(self.core == 0, here, there), jnp.where(self.core == 0, there, here)

    def after_last(self, kind, block, store):
        relation = self.relation(block)

        @pl.when(relation > 0)
        def _():
            self.last(kind, relation, block).wait_send()

        @pl.when(relation == 0)
        def _():
            for step in (1, 2, 3):
                self.last(kind, step, self.relative(step)).wait_recv()
            store(*self.halves(kind))

    def after_far_all(self, kind):
        self.sum_far(kind, 0)
        for step in (1, 2, 3):
            self.last(kind, step, self.relative(step)).start()

    def after_last_all(self, kind):
        for step in (1, 2, 3):
            self.last(kind, step, self.relative(step)).wait()
        return self.halves(kind)


def block_kernel(remote, *refs):
    (x_ref, cot_ref), data_refs, refs = refs[:2], refs[2:6], refs[6:]
    if remote:
        in_refs, refs = refs[:10], refs[10:]
        (pred_hbm, grad_hbm, in_out, so_out, cq_out, ckv_out, co_out, up_out, dn_out,
         gains_out, shifts_out, bias_out, time_out, hid_hbm, slope_hbm), refs = refs[:15], refs[15:]
    else:
        (w_hbm, wd_hbm, vec_hbm), refs = refs[:3], refs[3:]
        (pred_hbm, grad_hbm), dw_refs, refs = refs[:2], refs[2:6], refs[6:]
        (dvec_ref, time_out, hid_hbm, slope_hbm), refs = refs[:4], refs[4:]
    (unit_s, scale_s, qkv_s, prob_s, ctx_s, cq_s, cprob_s, cctx_s, hid_s, slope_s, dy_s, g_s,
     w_s, wd_s, vec_s, dvec_s, select_s, turned_s, tok_s, wide_s, folded_s, dmem_s, sinus_s, causal_s,
     own_s, flat_s, pred_ref, grad_ref, load_sem), groups, refs = refs[:29], refs[29:33], refs[33:]
    small, refs = refs[:7], refs[7:]
    obs_ref, repeat_ref, noise_ref, tw_ref, gains_ref, shifts_ref, bias_ref = small
    tokens, cols = x_ref.shape
    samples = sinus_s.shape[0]
    horizon = tokens // samples
    blocks = w_s.shape[0]
    per_sub = SUB // horizon
    score_scale = (cols // HEADS) ** (-0.5)
    section = lax.axis_index("section")
    ring = blocks - 1
    kept = ((hid_s, hid_hbm, load_sem.at[0]), (slope_s, slope_hbm, load_sem.at[1]))
    out_copies = [pltpu.make_async_copy(held.at[0], away, sem) for held, away, sem in kept]
    back_copies = [pltpu.make_async_copy(away, held.at[0], sem) for held, away, sem in kept]

    leaving = [pltpu.make_async_copy(pred_ref, pred_hbm, load_sem.at[20]),
               pltpu.make_async_copy(grad_ref, grad_hbm, load_sem.at[21])]
    sources = data_refs + (in_refs[7:] if remote else ())
    fetched = [pltpu.make_async_copy(source, held, load_sem.at[12 + index])
               for index, (source, held) in enumerate(zip(sources, small))]
    for copy in fetched:
        copy.start()
    loads = [pltpu.make_async_copy(x_ref, pred_ref, load_sem.at[0]),
             pltpu.make_async_copy(cot_ref, grad_ref, load_sem.at[1])]
    if remote:
        starts_at = (W_IN, W_SO, W_CKV, W_CQ, W_CO, W_UP)
        pieces = []
        for index, start in enumerate(starts_at):
            ref = in_refs[(0, 1, 3, 2, 4, 5)[index]]
            pieces.append(pltpu.make_async_copy(
                ref.at[0], w_s.at[section, :, start : start + ref.shape[2]], load_sem.at[2 + index]))
        pieces.append(pltpu.make_async_copy(in_refs[6].at[0], wd_s.at[section], load_sem.at[8]))
        for copy in pieces + loads:
            copy.start()
        for copy in fetched:
            copy.wait()
        vec_s[section] = jnp.zeros((VEC_ROWS, cols), F32)
        for row in range(SHIFT):
            vec_s[section, row : row + 1, :] = gains_ref[row]
        for row in range(SHIFT, BIAS):
            vec_s[section, row : row + 1, :] = shifts_ref[row - SHIFT]
        for part in range(4):
            vec_s[section, BIAS + part : BIAS + part + 1, :] = bias_ref[:, part * cols : (part + 1) * cols]
        sets = [(group,) + refs[2 + 8 * kind : 10 + 8 * kind] for kind, group in enumerate(groups)]
        sets += [refs[34 + 9 * index : 43 + 9 * index] for index in range(2)]
        links = Links(w_s, wd_s, vec_s, refs[0], refs[1], sets)
        links.greet()
        links.vectors(0, section, links.relative(1)).start()
        links.vectors(1, section, links.relative(2)).start()
        for piece, copies in enumerate((pieces[:1], pieces[1:2], pieces[2:3], pieces[3:5], pieces[5:6], pieces[6:])):
            for copy in copies:
                copy.wait()
            links.to_sibling(piece, section).start()

            @pl.when(links.core == 0)
            def _():
                links.over_y(piece, section).start()
    else:
        loads += [pltpu.make_async_copy(w_hbm, w_s, load_sem.at[2]),
                  pltpu.make_async_copy(wd_hbm, wd_s, load_sem.at[3]),
                  pltpu.make_async_copy(vec_hbm, vec_s, load_sem.at[4])]
        for copy in loads:
            copy.start()
        for copy in fetched:
            copy.wait()

    wide_masks = [jnp.concatenate([mask, mask], axis=1) for mask in half_masks()]
    lane_sub = iota((SUB, SUB), 1)
    row_sub = iota((SUB, SUB), 0)

    noise_row = noise_ref[pl.ds(section, 1), :].astype(F32)
    diagonal = iota((samples, samples), 0) == iota((samples, samples), 1)
    noise_col = jnp.sum(jnp.where(diagonal, noise_row, 0.0), axis=1, keepdims=True)
    half = cols // 2
    frequency = jnp.exp(iota((1, half), 1).astype(F32) * (-math.log(10000.0) / half))
    angles = noise_col * frequency
    sinus = low(jnp.concatenate([jnp.sin(angles), jnp.cos(angles)], axis=1))
    sinus_s[...] = sinus
    tok_s[:samples, :] = low(dot(sinus, tw_ref[...]))
    obs_count = repeat_ref.shape[-1]
    for index in range(obs_ref.shape[1]):
        tok_s[samples + index * obs_count : samples + (index + 1) * obs_count, :] = obs_ref[:, index, :]
    counts = low(repeat_ref[section].astype(F32))
    token_of = iota((obs_count, SUB), 1) - samples
    owner_of = iota((obs_count, SUB), 0)
    is_obs = token_of >= 0
    before = low((is_obs & (owner_of < token_of % obs_count)).astype(F32))
    upto = low((is_obs & (owner_of <= token_of % obs_count)).astype(F32))
    counts8 = jnp.broadcast_to(counts, (8, obs_count))
    starts = dot(counts8, before)[:1, :]
    ends = dot(counts8, upto)[:1, :]

    def select_rows(index, carried):
        key = iota((KEYS, SUB), 0) // per_sub
        lane = iota((KEYS, SUB), 1)
        sample = index * per_sub + iota((KEYS, SUB), 0) % per_sub
        sample_f = sample.astype(F32)
        time_hit = (key == 0) & (lane == sample)
        token = lane - samples
        owned = (sample_f >= starts) & (sample_f < ends)
        obs_hit = (token >= 0) & (token // obs_count == key - 1) & owned
        folded_s[index, :, :SUB] = (time_hit | obs_hit).astype(F32)
        return carried

    lax.fori_loop(0, tokens // SUB, select_rows, 0)
    selected = folded_s[...].reshape(-1, 2 * cols)[:, :SUB]
    select_s[...] = low(selected)
    selected = jnp.concatenate([selected, jnp.zeros((2 * SUB - selected.shape[0], SUB), F32)], axis=0)
    turned_s[...] = low(jnp.transpose(selected))
    same = row_sub // horizon == lane_sub // horizon
    causal_s[...] = jnp.where(same & (row_sub <= lane_sub), 0.0, -1e30)
    third = WIDE // 3
    own_s[...] = (iota((third, SUB), 0) % per_sub == iota((third, SUB), 1) // horizon).astype(F32)
    head_mask = (iota((third, cols), 0) // per_sub == iota((third, cols), 1) // (cols // HEADS)).astype(F32)
    dmem_s[...] = jnp.zeros_like(dmem_s)
    dvec_s[...] = jnp.zeros_like(dvec_s)
    for copy in loads:
        copy.wait()

    def vec(block, row):
        return vec_s[block, row : row + 1, :]

    def weight(block, start, stop):
        return w_s[block, :, start:stop]

    def condition(block):
        kv = dot(tok_s[...], weight(block, W_CKV, W_CQ))
        keys = low(kv[:, :cols])
        vals = low(kv[:, cols:] + vec(block, SHIFT + 7))

        spread = dot(select_s[...], jnp.concatenate([keys, vals], axis=1))
        both_masks = jnp.concatenate([head_mask, head_mask], axis=1)
        for index in range(tokens // SUB):
            for key in range(3):
                start = index * KEYS + key * per_sub
                copies = jnp.concatenate([spread[start : start + per_sub]] * HEADS, axis=0)
                wide_s[index, key * third : (key + 1) * third, :] = low(copies * both_masks)

    def fold(values):
        parts = []
        for part in thirds(values):
            part = part * head_mask
            parts.append(sum(part[head * per_sub : (head + 1) * per_sub] for head in range(HEADS)))
        return jnp.concatenate(parts, axis=0)

    def thirds(values):
        return [values[third * key : third * (key + 1)] for key in range(3)]

    def over_heads(values):
        return jnp.concatenate([values[:, :SUB], values[:, SUB:]], axis=0)

    def each_chunk(chunk, body):
        def at(step, carried):
            start = step * chunk
            body(pl.ds(start if isinstance(start, int) else pl.multiple_of(start, chunk), chunk), step)
            return carried

        if chunk == tokens:
            at(0, 0)
        else:
            lax.fori_loop(0, tokens // chunk, at, 0)

    def scale_of(block, rows, place):
        held = scale_s[rows, :]
        lane = iota(held.shape, 1)
        return jnp.sum(jnp.where(lane == 3 * block + place, held, 0.0), axis=1, keepdims=True)

    def keep_scale(block, rows, place, scale):
        held = scale_s[rows, :]
        scale_s[rows, :] = jnp.where(iota(held.shape, 1) == 3 * block + place, scale, held)

    def wide(values):
        return jnp.concatenate(values, axis=1)

    def both_heads(values):
        return jnp.concatenate([values * wide_masks[0], values * wide_masks[1]], axis=0)

    def both_pairs(values):
        zero = jnp.zeros((SUB, SUB), BF16)
        return jnp.concatenate([wide([values[:, :SUB], zero]), wide([zero, values[:, SUB:]])], axis=0)

    def forward(block, carried):
        after = jnp.minimum(block + 1, blocks - 1)
        if remote:
            links.arrive(block, (0, 1, 2))
        condition(block)

        def self_attention(rows, step):
            x = pred_ref[rows, :].astype(F32)
            unit0, scale0 = normalize(x)
            unit_s[block, 0, rows, :] = low(unit0)
            a = low(unit0 * vec(block, 0) + vec(block, SHIFT))
            q = low((dot(a, weight(block, 0, cols)) + vec(block, SHIFT + 3)) * score_scale)
            k = low(dot(a, weight(block, cols, 2 * cols)))
            v = low(dot(a, weight(block, 2 * cols, 3 * cols)) + vec(block, SHIFT + 4))
            qkv_s[block, rows, :cols] = q
            qkv_s[block, rows, cols : 2 * cols] = k
            qkv_s[block, rows, 2 * cols :] = v
            causal2 = wide([causal_s[...]] * 2)
            parts = []
            for sub in range(rows.size // SUB):
                span = slice(sub * SUB, (sub + 1) * SUB)
                scores = dot_nt(both_pairs(k[span]), both_heads(q[span]))
                stacked = []
                for pair in range(2):
                    score = scores[pair * SUB : (pair + 1) * SUB] + causal2
                    top = jnp.max(score, axis=0, keepdims=True)
                    expo = jnp.exp(score - top)
                    prob = low(expo * (1.0 / jnp.sum(expo, axis=0, keepdims=True)))
                    prob_s[block, step * (rows.size // SUB) + sub, pair] = prob
                    stacked.append(over_heads(prob))
                both = dot_tn(wide(stacked), both_heads(v[span]))
                parts.append(low(wide([both[:SUB, :SUB], both[SUB:, SUB:]])))
            context = jnp.concatenate(parts, axis=0)
            ctx_s[block, rows, :] = context
            x = x + (dot(context, weight(block, W_SO, W_CKV)) + vec(block, SHIFT + 5))
            g_s[rows, :] = x
            keep_scale(block, rows, 0, scale0)
            if remote:
                links.pass_on(block, block > 0, (2, 3))
                links.pass_on(block, block == 0, (2, 4), (2, 5))
                links.pass_on(after, block + 1 < blocks, (1, 0), (1, 1), (1, 2))
                links.start_y(block == 0, range(PIECES))

        each_chunk(FORWARD_SELF, self_attention)
        if remote:
            links.arrive(block, (3,))

        def cross_attention(rows, step):
            x = g_s[rows, :]
            unit1, scale1 = normalize(x)
            unit_s[block, 1, rows, :] = low(unit1)
            c = low(unit1 * vec(block, 1) + vec(block, SHIFT + 1))
            cq = low((dot(c, weight(block, W_CQ, W_CO)) + vec(block, SHIFT + 6)) * score_scale)
            cq_s[block, rows, :] = cq
            parts = []
            for sub in range(rows.size // SUB):
                index = step * (rows.size // SUB) + sub
                scores = thirds(dot_nt(wide_s[index, :, :cols], cq[sub * SUB : (sub + 1) * SUB]))
                top = jnp.maximum(jnp.maximum(scores[0], scores[1]), scores[2])
                expos = [jnp.exp(score - top) for score in scores]
                inverse = own_s[...] / (expos[0] + expos[1] + expos[2])
                prob = low(jnp.concatenate([expo * inverse for expo in expos], axis=0))
                cprob_s[block, index] = prob
                parts.append(low(dot_tn(prob, wide_s[index, :, cols:])))
            context = jnp.concatenate(parts, axis=0)
            cctx_s[block, rows, :] = context
            x = x + (dot(context, weight(block, W_CO, W_UP)) + vec(block, SHIFT + 8))
            unit2, scale2 = normalize(x)
            unit_s[block, 2, rows, :] = low(unit2)
            keep_scale(block, rows, 1, scale1)
            keep_scale(block, rows, 2, scale2)
            g_s[rows, :] = x + vec(block, SHIFT + 9)
            dy_s[0, rows, :] = low(unit2 * vec(block, 2) + vec(block, SHIFT + 2))
            if remote:
                links.pass_on(block, block > 0, (2, 4), (2, 5))
                links.pass_on(after, block + 1 < blocks, (1, 3))

        each_chunk(FORWARD_CROSS, cross_attention)
        if remote:
            links.arrive(block, (4, 5))

        def feed_forward(rows, step):
            e = dy_s[0, rows, :]
            root = math.sqrt(2.0 / math.pi)
            cube = root * 0.044715
            for part in range(4):
                lanes = slice(part * cols, (part + 1) * cols)
                u = low(dot(e, weight(block, W_UP + part * cols, W_UP + (part + 1) * cols)) + vec(
                    block, BIAS + part
                ))
                square = u * u
                gate = jnp.tanh(u * (square * low(cube) + low(root))) * low(0.5) + low(0.5)
                hidden = u * gate
                slope = gate + hidden * (low(1.0) - gate) * (square * low(6.0 * cube) + low(2.0 * root))
                hid_s[block % ring, rows, lanes] = hidden
                slope_s[block % ring, rows, lanes] = slope
            pred_ref[rows, :] = low(g_s[rows, :] + dot(hid_s[block % ring, rows, :], wd_s[block]))
            if remote:
                links.pass_on(after, block + 1 < blocks, (2, 0), (2, 1), (2, 2), (1, 4), (1, 5))

        @pl.when(block == ring)
        def _():
            for copy in out_copies:
                copy.wait()

        each_chunk(FORWARD_FF, feed_forward)

        @pl.when(block == 0)
        def _():
            for copy in out_copies:
                copy.start()

        return carried

    if remote:
        links.pass_on(0, True, (1, 0), (1, 1), (2, 0), (1, 2), (2, 1), (1, 3), (2, 2), (1, 4), (2, 3), (1, 5))
    lax.fori_loop(0, blocks, forward, 0)
    leaving[0].start()

    def put(kind, start, value):
        width, taken = WIDTHS[kind], 0
        while taken < value.shape[1]:
            index, place = (start + taken) // width, (start + taken) % width
            count = min(value.shape[1] - taken, width - place)
            part = low(value[:, taken : taken + count]).reshape(NZ, NX, ROWS, count)
            groups[kind][index, :, :, :, place : place + count] = part
            taken += count

    def emit(block, kind):
        if remote:
            links.near(kind).start()
        else:
            copy = pltpu.make_async_copy(groups[kind], dw_refs[kind].at[block], load_sem.at[2])
            copy.start()
            copy.wait()

    def store_down(first, second):
        blocks_of = [value[:, q * SUB : (q + 1) * SUB] for value in (first, second) for q in range(4)]
        dn_out[...] = jnp.transpose(jnp.concatenate(blocks_of, axis=0))

    def store_up(first, second):
        up_out[...] = wide([first, second])

    def store_cross(first, second):
        joined = wide([first, second])
        ckv_out[...] = joined[:, : 2 * cols]
        for place, out in enumerate((cq_out, co_out, so_out)):
            out[...] = joined[:, (2 + place) * cols : (3 + place) * cols]

    def store_self(first, second):
        in_out[...] = wide([first, second])

    stores = (store_down, store_up, store_cross, store_self)

    def advance(works):
        if not remote:
            return
        for kind, stage, block, there in works:

            def run(kind=kind, stage=stage, block=block):
                if stage == 1:
                    links.after_near(kind)
                elif stage == 2:
                    links.after_row(kind, block)
                elif stage == 3:
                    links.after_far(kind, block)
                else:
                    links.after_last(kind, block, stores[kind])

            if there is True:
                run()
            else:
                pl.when(there)(run)

    def time_gradient():
        dmem = dmem_s[...]
        dmem_high = low(dmem)
        dmem_low = low(dmem - dmem_high.astype(F32))
        return dot_tn(sinus_s[...], dmem_high) + dot_tn(sinus_s[...], dmem_low)

    def emit_vectors():
        vectors = dvec_s[...].reshape(blocks * VEC_ROWS, cols)
        vectors = jnp.concatenate([vectors, jnp.zeros((SUB - blocks * VEC_ROWS, cols), F32)], axis=0)
        turned = jnp.transpose(vectors).reshape(GROUPS, ROWS, SUB)
        lane = iota((ROWS, SUB), 1) % VEC_ROWS
        rows_out = []
        for group in range(GROUPS):
            part, high = group // 2, group % 2
            piece = turned[group]
            for j in range(4):
                source = turned[4 * high + j]
                if j != part:
                    source = pltpu.roll(source, (j - part) % SUB, 1)
                piece = jnp.where(lane == BIAS + j, source, piece)
            rows_out.append(piece)
        turned = jnp.concatenate(rows_out, axis=0)
        for index in range(2):
            sets[VECTOR][0][index] = low(turned).reshape(NZ, NX, ROWS, SUB)
        links.near(VECTOR).start()

    def backward(turn, carried):
        block = blocks - 1 - turn
        earlier, before = block + 1, block + 2
        again, third_turn = turn > 0, turn > 1

        def add_vec(row, values):
            dvec_s[block, row : row + 1, :] += values

        def turn_over_ones(left):
            return jnp.concatenate([jnp.transpose(left), jnp.ones((16, tokens), BF16)], axis=0)

        def put_scaled(kind, start, unit_row, right, sum_rows):
            turned = turn_over_ones(unit_s[block, unit_row])
            gain = place_column(vec(block, unit_row))
            shift = place_column(vec(block, SHIFT + unit_row))
            parts = []
            for place, row in enumerate(sum_rows):
                both = dot(turned, right[:, place * cols : (place + 1) * cols])
                sums = both[cols : cols + 1]
                dvec_s[block, row : row + 1, :] = sums
                put(kind, start + place * cols, both[:cols] * gain + shift * sums)
                parts.append((both[:cols], sums))
            return parts

        def put_plain(kind, start, left, right, row):
            both = dot(turn_over_ones(left), right)
            dvec_s[block, row : row + 1, :] = both[cols : cols + 1]
            put(kind, start, both[:cols])

        @pl.when(block == 0)
        def _():
            for copy in back_copies:
                copy.wait()

        turned = jnp.transpose(grad_ref[...])
        for part in range(4):
            piece = low(dot(turned, hid_s[block % ring, :, part * cols : (part + 1) * cols]))
            for index in range(2):
                for x in range(NX):
                    for q in range(4):
                        row = SUB * index + ROWS * q
                        groups[DOWN][index, part, x, :, q * SUB : (q + 1) * SUB] = piece[
                            row : row + ROWS, x * SUB : (x + 1) * SUB
                        ]
        def feed_forward(rows, step):
            dy3 = grad_ref[rows, :]
            g = dy3.astype(F32)
            add_vec(SHIFT + 9, jnp.sum(g, axis=0, keepdims=True))
            for part in range(4):
                lanes = slice(part * cols, (part + 1) * cols)
                dh = dot_nt(dy3, wd_s[block, lanes, :])
                slope_s[block % ring, rows, lanes] = low(dh) * slope_s[block % ring, rows, lanes]
            de = dot_nt(slope_s[block % ring, rows, :], weight(block, W_UP, W_END))
            back, along, flat = normalize_back(
                de, unit_s[block, 2, rows, :].astype(F32), scale_of(block, rows, 2), vec(block, 2)
            )
            add_vec(2, along)
            add_vec(SHIFT + 2, flat)
            g = g + back
            g_s[rows, :] = g
            dy_s[0, rows, :] = low(g)

        each_chunk(BACK_FF, feed_forward)
        advance((
            (DOWN, 3, earlier, again), (UP, 2, earlier, again), (SELF, 1, earlier, again),
            (UP, 4, before, third_turn), (CROSS, 4, before, third_turn), (SELF, 4, before, third_turn),
        ))
        emit(block, DOWN)
        pl.when(turn == 0)(back_copies[0].start)

        put_scaled(UP, 0, 2, slope_s[block % ring], [BIAS + part for part in range(4)])
        condition(block)
        advance(((CROSS, 2, earlier, again),))
        emit(block, UP)
        pl.when(turn == 0)(back_copies[1].start)

        def cross_attention(rows, step):
            dctx = low(dot_nt(dy_s[0, rows, :], weight(block, W_CO, W_UP)))
            for sub in range(rows.size // SUB):
                index = step * (rows.size // SUB) + sub
                span = pl.ds(index * SUB if isinstance(index, int) else pl.multiple_of(index * SUB, SUB), SUB)
                keys, vals = wide_s[index, :, :cols], wide_s[index, :, cols:]
                part = dctx[sub * SUB : (sub + 1) * SUB]
                prob = cprob_s[block, index]
                prob32 = prob.astype(F32)
                weighted = prob32 * dot_nt(vals, part)
                inner = sum(thirds(weighted))
                dscore = low(weighted - prob32 * jnp.concatenate([inner] * 3, axis=0))
                folded_s[index, :, :cols] = fold(dot(dscore, cq_s[block, span, :]))
                folded_s[index, :, cols:] = fold(dot(prob, part))
                cq_s[block, span, :] = low(dot_tn(dscore, keys) * score_scale)
            dcq = cq_s[block, rows, :]
            dc = dot_nt(dcq, weight(block, W_CQ, W_CO))
            back, along, flat = normalize_back(
                dc, unit_s[block, 1, rows, :].astype(F32), scale_of(block, rows, 1), vec(block, 1)
            )
            add_vec(1, along)
            add_vec(SHIFT + 1, flat)
            g = g_s[rows, :] + back
            g_s[rows, :] = g
            dy_s[1, rows, :] = low(g)

        each_chunk(BACK_CROSS, cross_attention)
        advance(((DOWN, 1, block, True), (DOWN, 4, earlier, again)))

        folded = folded_s[...].reshape(-1, 2 * cols)
        dkv32 = dot(turned_s[:, : folded.shape[0]], low(folded))
        dkv = low(dkv32)
        add_vec(SHIFT + 7, jnp.sum(dkv32[:, cols:], axis=0, keepdims=True))
        dmem_s[...] += dot_nt(dkv[:samples], weight(block, W_CKV, W_CQ))
        put(CROSS, 0, dot_tn(tok_s[...], dkv))
        put_scaled(CROSS, 2 * cols, 1, cq_s[block], [SHIFT + 6])
        put_plain(CROSS, 3 * cols, cctx_s[block], dy_s[0], SHIFT + 8)
        put_plain(CROSS, 4 * cols, ctx_s[block], dy_s[1], SHIFT + 5)
        advance(((SELF, 2, earlier, again), (UP, 1, block, True)))
        emit(block, CROSS)
        if remote:

            @pl.when(block == 0)
            def _():
                dtime = time_gradient()
                for index in range(2):
                    part = low(dtime[:, index * SUB : (index + 1) * SUB])
                    sets[TIME][0][index] = part.reshape(NZ, NX, ROWS, SUB)
                links.near(TIME).start()

        def self_attention(rows, step):
            dctx = low(dot_nt(dy_s[1, rows, :], weight(block, W_SO, W_CKV)))
            for sub in range(rows.size // SUB):
                index = step * (rows.size // SUB) + sub
                span = pl.ds(index * SUB if isinstance(index, int) else pl.multiple_of(index * SUB, SUB), SUB)
                part = dctx[sub * SUB : (sub + 1) * SUB]
                queries, keys, values = (qkv_s[block, span, place * cols : (place + 1) * cols] for place in range(3))
                sides = (slice(0, SUB), slice(SUB, 2 * SUB))
                dstack = both_heads(part)
                qstack = both_heads(queries)
                kstack = both_heads(keys)
                probs = [prob_s[block, index, pair] for pair in range(2)]
                dprobs = dot_nt(both_pairs(values), dstack)
                dprobs = [dprobs[side] for side in sides]
                dscores = []
                for prob, dprob in zip(probs, dprobs):
                    prob32 = prob.astype(F32)
                    weighted = prob32 * dprob
                    dscores.append(low(weighted - prob32 * jnp.sum(weighted, axis=0, keepdims=True)))
                dq = dot_tn(wide([over_heads(dscore) for dscore in dscores]), kstack)
                dq = [dq[side, side] for side in sides]
                dk = dot(jnp.concatenate(dscores, axis=0), qstack)
                dk = [dk[side, side] for side in sides]
                dv = dot(jnp.concatenate(probs, axis=0), dstack)
                dv = [dv[side, side] for side in sides]
                qkv_s[block, span, :cols] = low(wide(dq) * score_scale)
                qkv_s[block, span, cols : 2 * cols] = low(wide(dk))
                qkv_s[block, span, 2 * cols :] = low(wide(dv))

        each_chunk(BACK_SELF, self_attention)
        advance((
            (UP, 3, earlier, again), (CROSS, 3, earlier, again), (DOWN, 2, block, True),
            (CROSS, 1, block, True), (TIME, 1, block, block == 0),
        ))

        gain_column, shift_column = 0.0, 0.0
        for place, (both, sums) in enumerate(
            put_scaled(SELF, 0, 0, qkv_s[block], (SHIFT + 3, KEYSUM, SHIFT + 4))
        ):
            matrix = weight(block, place * cols, (place + 1) * cols).astype(F32)
            gain_column += jnp.sum(both * matrix, axis=1, keepdims=True)
            shift_column += jnp.sum(sums * matrix, axis=1, keepdims=True)
        dvec_s[block, 0:1, :] = place_row(gain_column)
        dvec_s[block, SHIFT : SHIFT + 1, :] = place_row(shift_column)
        emit(block, SELF)
        if remote:
            pl.when(block == 0)(emit_vectors)

        def self_norm(rows, step):
            da = dot_nt(qkv_s[block, rows, :], weight(block, 0, 3 * cols))
            back, _, _ = normalize_back(
                da, unit_s[block, 0, rows, :].astype(F32), scale_of(block, rows, 0), vec(block, 0)
            )
            grad_ref[rows, :] = low(g_s[rows, :] + back)

        each_chunk(BACK_SELF, self_norm)
        advance(((SELF, 3, earlier, again),))
        return carried

    lax.fori_loop(0, blocks, backward, 0)
    leaving[1].start()
    if not remote:
        for copy in leaving:
            copy.wait()
        time_out[...] = time_gradient()
        dvec_ref[...] = dvec_s[...]
        return

    links.after_row(UP, 0)
    links.after_near(SELF)
    links.after_near(VECTOR)
    links.after_far(DOWN, 0)
    links.after_row(CROSS, 0)
    links.after_row(TIME, 0)
    links.after_last(UP, 1, store_up)
    links.after_last(CROSS, 1, store_cross)
    links.after_far(UP, 0)
    links.after_row(SELF, 0)
    links.after_row(VECTOR, 0)
    links.after_last(SELF, 1, store_self)
    links.after_last(DOWN, 0, store_down)
    links.after_far(CROSS, 0)
    links.after_far_all(TIME)
    links.after_last(UP, 0, store_up)
    links.after_far(SELF, 0)
    links.after_far_all(VECTOR)
    links.after_last(CROSS, 0, store_cross)
    time_out[...] = wide(links.after_last_all(TIME))
    links.after_last(SELF, 0, store_self)
    mine, _ = links.after_last_all(VECTOR)
    padded = jnp.concatenate([mine, jnp.zeros((SUB - ROWS, SUB), F32)], axis=0)
    flat_s[...] = jnp.transpose(padded)
    mine = flat_s[pl.ds(pl.multiple_of(section * VEC_ROWS, 8), VEC_ROWS), :]
    for row in range(SHIFT):
        gains_out[row] = mine[row : row + 1, :ROWS]
    for row in range(SHIFT, BIAS):
        shifts_out[row - SHIFT] = mine[row : row + 1, :ROWS]
    bias = mine[BIAS : BIAS + 1, :]
    for part in range(1, 4):
        bias = bias + pltpu.roll(mine[BIAS + part : BIAS + part + 1, :], part * ROWS, 1)
    bias_out[...] = bias
    links.finish_weights()
    for copy in leaving:
        copy.wait()


def run_blocks(remote, x, cot, obs, repeat, noise, time_weight, *weights, interpret=False):
    tokens, cols = x.shape
    blocks = 4
    samples = noise.shape[1]
    vmem = pl.BlockSpec(memory_space=pltpu.VMEM)
    hbm = pl.BlockSpec(memory_space=pl.ANY)
    half_rows = (NZ, NX, ROWS)
    scratch = [
        pltpu.VMEM((blocks, 3, tokens, cols), BF16),
        pltpu.VMEM((tokens, SUB), F32),
        pltpu.VMEM((blocks, tokens, 3 * cols), BF16),
        pltpu.VMEM((blocks, tokens // SUB, 2, SUB, 2 * SUB), BF16),
        pltpu.VMEM((blocks, tokens, cols), BF16),
        pltpu.VMEM((blocks, tokens, cols), BF16),
        pltpu.VMEM((blocks, tokens // SUB, WIDE, SUB), BF16),
        pltpu.VMEM((blocks, tokens, cols), BF16),
        pltpu.VMEM((blocks - 1, tokens, 4 * cols), BF16),
        pltpu.VMEM((blocks - 1, tokens, 4 * cols), BF16),
        pltpu.VMEM((2, tokens, cols), BF16),
        pltpu.VMEM((tokens, cols), F32),
        pltpu.VMEM((blocks, cols, W_END), BF16),
        pltpu.VMEM((blocks, 4 * cols, cols), BF16),
        pltpu.VMEM((blocks, VEC_ROWS, cols), F32),
        pltpu.VMEM((blocks, VEC_ROWS, cols), F32),
        pltpu.VMEM((tokens // SUB * KEYS, SUB), BF16),
        pltpu.VMEM((SUB, 2 * SUB), BF16),
        pltpu.VMEM((SUB, cols), BF16),
        pltpu.VMEM((tokens // SUB, WIDE, 2 * cols), BF16),
        pltpu.VMEM((tokens // SUB, KEYS, 2 * cols), F32),
        pltpu.VMEM((samples, cols), F32),
        pltpu.VMEM((samples, cols), BF16),
        pltpu.VMEM((SUB, SUB), F32),
        pltpu.VMEM((WIDE // 3, SUB), F32),
        pltpu.VMEM((SUB, SUB), F32),
        pltpu.VMEM((tokens, cols), BF16),
        pltpu.VMEM((tokens, cols), BF16),
        pltpu.SemaphoreType.DMA((22,)),
    ]
    scratch += [pltpu.VMEM((2,) + half_rows + (width,), BF16) for width in WIDTHS[:TIME]]
    parts = (obs, repeat, noise, time_weight) + tuple(weights[7:])
    scratch += [pltpu.VMEM(part.shape, part.dtype) for part in parts]
    if not remote:
        scratch += [pltpu.VMEM((8, SUB), F32)] * 3
    if remote:
        scratch += [pltpu.SemaphoreType.DMA((5 * PIECES + 3,))] * 2
        for kind, width in enumerate(WIDTHS):
            if kind >= TIME:
                scratch.append(pltpu.VMEM((2,) + half_rows + (width,), BF16))
            scratch += [
                pltpu.VMEM(half_rows + (width,), BF16),
                pltpu.VMEM((NZ, ROWS, width), BF16),
                pltpu.VMEM(((2 if kind in TURNS else 1) * (NZ - 1), ROWS, width), BF16),
                pltpu.VMEM((3, ROWS, width), BF16),
                pltpu.VMEM((ROWS, width), BF16),
                pltpu.VMEM((NZ, ROWS, width), BF16),
                pltpu.SemaphoreType.DMA((3 + 2 * NZ,)),
                pltpu.SemaphoreType.DMA((3 + 2 * NZ,)),
            ]
        shapes = ((ROWS, 3 * cols), (ROWS, cols), (ROWS, cols), (ROWS, 2 * cols), (ROWS, cols),
                  (ROWS, 4 * cols), (4 * ROWS, cols), (SHIFT, 1, ROWS), (BIAS - SHIFT, 1, ROWS), (1, 4 * ROWS),
                  (ROWS, cols))
        outs = tuple(jax.ShapeDtypeStruct(shape, F32) for shape in shapes)
        in_specs = [hbm] * 16
        out_specs = (hbm, hbm) + (vmem,) * len(outs)
        params = pltpu.CompilerParams(
            vmem_limit_bytes=VMEM_BYTES, collective_id=0, has_side_effects=True)
    else:
        outs = (
            jax.ShapeDtypeStruct((blocks, VEC_ROWS, cols), F32),
            jax.ShapeDtypeStruct((cols, cols), F32),
        )
        outs = tuple(
            jax.ShapeDtypeStruct((blocks, 2) + half_rows + (width,), BF16) for width in WIDTHS[:TIME]
        ) + outs
        in_specs = [hbm] * 9
        out_specs = (hbm, hbm) + (hbm,) * 4 + (vmem, vmem)
        params = pltpu.CompilerParams(vmem_limit_bytes=VMEM_BYTES)
    low_out = jax.ShapeDtypeStruct((tokens, cols), BF16)
    away = jax.ShapeDtypeStruct((tokens, 4 * cols), BF16)
    return pl.pallas_call(
        functools.partial(block_kernel, remote),
        out_shape=(low_out, low_out) + outs + (away, away),
        in_specs=in_specs,
        out_specs=out_specs + (hbm, hbm),
        scratch_shapes=scratch,
        compiler_params=params,
        interpret=interpret,
    )(x, cot, obs, repeat, noise, time_weight, *weights)


def hand_out(*refs):
    count = (len(refs) - 1) // 3
    held, sem = refs[2 * count : 3 * count], refs[-1]
    arriving = [pltpu.make_async_copy(refs[i], held[i], sem.at[i]) for i in range(count)]
    leaving = []
    for copy in arriving:
        copy.start()
    for index in range(count):
        target = refs[count + index]
        if len(target.shape) > len(held[index].shape):
            target = target.at[0]
        arriving[index].wait()
        leaving.append(pltpu.make_async_copy(held[index], target, sem.at[index]))
        leaving[-1].start()
    for copy in leaving:
        copy.wait()


def finished(results):
    hbm = pl.BlockSpec(memory_space=pl.ANY)
    shapes = [(1,) + result.shape for result in results[:9]] + [result.shape for result in results[9:]]
    return pl.pallas_call(
        hand_out,
        out_shape=tuple(jax.ShapeDtypeStruct(shape, result.dtype) for shape, result in zip(shapes, results)),
        in_specs=[hbm] * len(results),
        out_specs=(hbm,) * len(results),
        scratch_shapes=[pltpu.VMEM(result.shape, result.dtype) for result in results]
        + [pltpu.SemaphoreType.DMA((len(results),))],
    )(*results)


def pack_weights(self_in, self_out, cross_q, cross_kv, cross_out, mlp_up, mlp_down):
    parts = (self_in, self_out, cross_kv, cross_q, cross_out, mlp_up)
    return jnp.concatenate([part[0] for part in parts], axis=1), mlp_down[0]


def pack_vectors(gains, shifts, mlp_bias):
    cols = gains.shape[-1]
    rows = jnp.concatenate([gains[0], shifts[0], mlp_bias.reshape(4, cols)], axis=0)
    return jnp.pad(rows, ((0, VEC_ROWS - rows.shape[0]), (0, 0)))


def natural(dweights):
    def joined(kind):
        parts = dweights[kind].reshape(-1, 2, GROUPS * ROWS, WIDTHS[kind])
        return jnp.concatenate([parts[:, 0], parts[:, 1]], axis=-1)

    blocks = dweights[DOWN].shape[0]
    down = dweights[DOWN].reshape(blocks, 2, GROUPS, ROWS, 4, SUB).transpose(0, 2, 5, 1, 4, 3)
    return joined(UP), joined(CROSS), joined(SELF), down.reshape(blocks, GROUPS * SUB, -1)


def gathered(data, packed_weights, packed_vectors):
    sections = lax.axis_size("section")
    groups = lax.axis_size("dp")
    cols = data[0].shape[-1]
    weights = [lax.all_gather(part, "section", axis=0) for part in packed_weights]
    vectors = lax.all_gather(packed_vectors, "section", axis=0)
    pred, grad, *dweights, dvectors, dtime, _, _ = run_blocks(False, *data, *weights, vectors)
    rows = cols // groups
    up, cross, own, down = natural(dweights)
    rest = jnp.concatenate([up, cross, own], axis=2).reshape(sections, groups, -1)
    down = down.reshape(sections, groups, -1)
    small = dvectors[:, :BIAS].reshape(sections, BIAS, groups, rows).transpose(0, 2, 1, 3)
    small = small.reshape(sections, groups, BIAS * rows)
    bias = dvectors[:, BIAS:KEYSUM].reshape(sections, groups, 4 * rows)
    term = jnp.broadcast_to(dtime.reshape(1, groups, rows * cols), (sections, groups, rows * cols))
    sent = jnp.concatenate([rest, down], axis=2).reshape(sections * groups, -1)
    sent_small = jnp.concatenate([small, bias, term], axis=2).reshape(sections * groups, -1)
    got = lax.psum_scatter(sent, ("section", "dp"), scatter_dimension=0, tiled=True)[0].astype(F32)
    got_small = lax.psum_scatter(sent_small, ("section", "dp"), scatter_dimension=0, tiled=True)[0]
    widths = (up.shape[-1], cross.shape[-1], own.shape[-1])
    split = sum(widths) * rows
    rest = got[:split].reshape(rows, sum(widths))
    down = got[split:].reshape(4 * rows, cols)
    small = got_small[: BIAS * rows].reshape(BIAS, rows)
    bias = got_small[BIAS * rows : (BIAS + 4) * rows].reshape(4, rows)
    term = got_small[(BIAS + 4) * rows :].reshape(rows, cols)
    up, cross, own = jnp.split(rest, (widths[0], widths[0] + widths[1]), axis=1)
    kv, query, out, self_out = jnp.split(cross, (2 * cols, 3 * cols, 4 * cols), axis=1)
    return (pred, grad, own, self_out, query, kv, out, up, down, small[:SHIFT], small[SHIFT:], bias, term)


def local(
    horizon, cotangent, obs_tokens, obs_repeat, noise_step, time_weight,
    self_in, self_out, cross_q, cross_kv, cross_out, mlp_up, mlp_down, gains, shifts, mlp_bias,
):
    cols = horizon.shape[-1]
    data = (horizon[0], cotangent[0], obs_tokens[0], obs_repeat, noise_step, time_weight)
    weights = (self_in, self_out, cross_q, cross_kv, cross_out, mlp_up, mlp_down)
    if lax.axis_size("dp") == GROUPS:
        vectors = (gains.transpose(1, 0, 2), shifts.transpose(1, 0, 2), mlp_bias)
        results = finished(run_blocks(True, *data, *weights, *vectors)[:-2])
        return results[:9] + (results[9].transpose(1, 0, 2), results[10].transpose(1, 0, 2)) + results[11:]
    results = gathered(data, pack_weights(*weights), pack_vectors(gains, shifts, mlp_bias))
    return tuple(result[None] for result in results[:11]) + (results[11].reshape(1, -1), results[12])


def solution(mesh):
    whole = P("section", None, None)
    return jax.shard_map(
        local,
        mesh=mesh,
        in_specs=(
            P("section", "dp", None), P("section", "dp", None), P("section", "dp", None, None),
            P(None, "dp", None), P(None, "dp"), P(),
            whole, whole, whole, whole, whole, whole, whole, whole, whole, P("section", None),
        ),
        out_specs=(P("section", "dp", None),) * 9
        + (P("section", None, "dp"), P("section", None, "dp"), P("section", "dp"), P("dp", None)),
        check_vma=False,
    )
```

```python
import functools
import math

import jax
import jax.numpy as jnp
from jax import lax
from jax.experimental import pallas as pl
from jax.experimental.pallas import tpu as pltpu
from jax.sharding import PartitionSpec as P

HEADS = 4
VMEM_BYTES = 63 * 1024 * 1024
SUB = 128
F32 = jnp.float32
BF16 = jnp.bfloat16

W_IN, W_SO, W_CKV, W_CQ, W_CO, W_UP, W_END = 0, 768, 1024, 1536, 1792, 2048, 3072
SHIFT, BIAS, KEYSUM, VEC_ROWS = 3, 13, 17, 24
SENT = ((W_IN, 512), (512, W_CKV), (W_CKV, W_CQ), (W_CQ, W_UP), (W_UP, W_END))
DOWN_PIECE, PIECES = 5, 6
DOWN, UP, CROSS, SELF, TIME, VECTOR = range(6)
WIDTHS = (512, 512, 640, 384, 128, 128)
FORWARD_SELF, FORWARD_CROSS, FORWARD_FF = 1024, 1024, 1024
BACK_FF, BACK_CROSS, BACK_SELF = 1024, 1024, 1024
ROWS, NZ, NX = 32, 4, 2
TURNS = (UP, SELF)
GROUPS = NZ * NX
KEYS, WIDE = 24, 96


def dot(left, right):
    return jnp.dot(left, right, preferred_element_type=F32)


def dot_nt(left, right):
    return lax.dot_general(left, right, (((1,), (1,)), ((), ())), preferred_element_type=F32)


def dot_tn(left, right):
    return lax.dot_general(left, right, (((0,), (0,)), ((), ())), preferred_element_type=F32)


def iota(shape, axis):
    return lax.broadcasted_iota(jnp.int32, shape, axis)


def low(values):
    return jnp.asarray(values, BF16)


def normalize(values):
    center = values - jnp.mean(values, axis=-1, keepdims=True)
    scale = lax.rsqrt(jnp.mean(center * center, axis=-1, keepdims=True) + 1e-05)
    return center * scale, scale


def normalize_back(grad, unit, scale, gain):
    ahead = grad * unit
    grad_unit = grad * gain
    mean_grad = jnp.mean(grad_unit, axis=-1, keepdims=True)
    mean_along = jnp.mean(ahead * gain, axis=-1, keepdims=True)
    back = (grad_unit - mean_grad - unit * mean_along) * scale
    return back, jnp.sum(ahead, axis=0, keepdims=True), jnp.sum(grad, axis=0, keepdims=True)


def half_masks():
    lane = iota((1, SUB), 1)
    first = (lane < SUB // 2).astype(F32)
    return low(first), low(1.0 - first)


def add_low(left, right):
    return left + right


def place_row(column):
    size = column.shape[0]
    diagonal = iota((size, size), 0) == iota((size, size), 1)
    return jnp.sum(jnp.where(diagonal, column, 0.0), axis=0, keepdims=True)


def place_column(row):
    size = row.shape[1]
    diagonal = iota((size, size), 0) == iota((size, size), 1)
    return jnp.sum(jnp.where(diagonal, row, 0.0), axis=1, keepdims=True)


class Links:
    def __init__(self, w_s, wd_s, vec_s, wsend, wrecv, sets):
        self.w, self.wd, self.vec, self.wsend, self.wrecv, self.sets = w_s, wd_s, vec_s, wsend, wrecv, sets
        self.section = lax.axis_index("section")
        self.group = lax.axis_index("dp")
        self.core, self.y = self.section % 2, self.section // 2
        self.x, self.z = self.group % NX, self.group // NX
        self.x_peer = self.z * NX + (self.x + 1) % NX

    def relative(self, step):
        return (self.y + step // 2) % 2 * 2 + (self.core + step % 2) % 2

    def relation(self, block):
        return (self.y + block // 2) % 2 * 2 + (self.core + block % 2) % 2

    def z_peer(self, step):
        return (self.z + step) % NZ * NX + self.x

    def greet(self):
        barrier = pltpu.get_barrier_semaphore()
        peers = [{"section": self.relative(step)} for step in (1, 2, 3)]
        peers += [{"dp": self.x_peer}] + [{"dp": self.z_peer(step)} for step in range(1, NZ)]
        for peer in peers:
            pl.semaphore_signal(barrier, inc=1, device_id=peer, device_id_type=pl.DeviceIdType.MESH)
        pl.semaphore_wait(barrier, len(peers))

    def remote(self, src, dst, send, recv, peer):
        return pltpu.make_async_remote_copy(
            src_ref=src, dst_ref=dst, send_sem=send, recv_sem=recv, device_id=peer,
            device_id_type=pl.DeviceIdType.MESH,
        )

    def weight_copy(self, slot, block, piece, half, peer):
        array, lanes = (self.wd, slice(None)) if piece == DOWN_PIECE else (self.w, slice(*SENT[piece]))
        part = array.at[block, :, lanes]
        if half is not None:
            rows = array.shape[1] // 2
            part = array.at[block, pl.ds(pl.multiple_of(half * rows, rows), rows), lanes]
        return self.remote(part, part, self.wsend.at[slot], self.wrecv.at[slot], peer)

    def vector_copy(self, slot, block, peer):
        part = self.vec.at[block]
        return self.remote(part, part, self.wsend.at[slot], self.wrecv.at[slot], peer)

    def to_sibling(self, piece, block):
        return self.weight_copy(piece, block, piece, None, {"section": self.relative(1)})

    def over_y(self, piece, block):
        return self.weight_copy(PIECES + piece, block, piece, self.x, {"section": self.relative(2)})

    def over_x(self, piece, block, half):
        return self.weight_copy(2 * PIECES + piece, block, piece, half, {"dp": self.x_peer})

    def forwarded(self, piece, block, half, which):
        return self.weight_copy((3 + which) * PIECES + piece, block, piece, half, {"section": self.relative(1)})

    def vectors(self, step, block, peer):
        return self.vector_copy(5 * PIECES + step, block, {"section": peer})

    def start_y(self, when, pieces):
        @pl.when(when & (self.core == 1))
        def _():
            for piece in pieces:
                self.over_y(piece, self.section).start()

    def pass_first(self, piece, block):
        self.over_y(piece, block).wait_recv()
        self.over_x(piece, block, self.x).start()
        self.forwarded(piece, block, self.x, 0).start()

    def pass_second(self, piece, block):
        self.over_x(piece, block, 1 - self.x).wait_recv()
        self.forwarded(piece, block, 1 - self.x, 1).start()

    def pass_on(self, block, when, *works):
        @pl.when(self.relation(block) == 2 if when is True else when & (self.relation(block) == 2))
        def _():
            for stage, piece in works:
                if stage == 1 and piece == 0:
                    self.vectors(1, block, self.relative(2)).wait_recv()
                    self.vectors(2, block, self.relative(1)).start()
                (self.pass_first if stage == 1 else self.pass_second)(piece, block)

    def arrive(self, block, pieces):
        relation = self.relation(block)

        @pl.when(relation == 1)
        def _():
            if 0 in pieces:
                self.vectors(0, block, self.relative(1)).wait_recv()
            for piece in pieces:
                self.to_sibling(piece, block).wait_recv()

        @pl.when(relation == 3)
        def _():
            if 0 in pieces:
                self.vectors(2, block, self.relative(1)).wait_recv()
            for piece in pieces:
                self.forwarded(piece, block, self.x, 0).wait_recv()
                self.forwarded(piece, block, 1 - self.x, 1).wait_recv()

    def finish_weights(self):
        own, passed = self.section, self.relative(2)
        self.vectors(0, own, self.relative(1)).wait_send()
        self.vectors(1, own, self.relative(2)).wait_send()
        self.vectors(2, passed, self.relative(1)).wait_send()
        for piece in range(PIECES):
            self.to_sibling(piece, own).wait_send()
            self.over_y(piece, own).wait_send()
            self.over_x(piece, passed, self.x).wait_send()
            self.forwarded(piece, passed, self.x, 0).wait_send()
            self.forwarded(piece, passed, 1 - self.x, 1).wait_send()

    def near(self, kind):
        group_s, near_s, _, _, _, _, _, send, recv = self.sets[kind]
        return self.remote(group_s.at[1 - self.core], near_s, send.at[0], recv.at[0],
                           {"section": self.relative(1)})

    def row(self, kind):
        group_s, _, row_s, _, _, _, _, send, recv = self.sets[kind]
        return self.remote(group_s.at[self.core, :, 1 - self.x], row_s, send.at[1], recv.at[1],
                           {"dp": self.x_peer})

    def far_slot(self, kind, step, block):
        return (block % 2) * (NZ - 1) + step - 1 if kind in TURNS else step - 1

    def far(self, kind, step, block):
        far_s, _, _, fold_s, send, recv = self.sets[kind][3:]
        slot = self.far_slot(kind, step, block)
        sem = slot + 2 if kind not in TURNS else 1 + step + (block % 2) * (NZ + 2)
        return self.remote(fold_s.at[(self.z + step) % NZ], far_s.at[slot], send.at[sem], recv.at[sem],
                           {"dp": self.z_peer(step)})

    def last(self, kind, step, peer):
        last_s, sum_s, _, send, recv = self.sets[kind][4:]
        slot = NZ + step
        return self.remote(sum_s, last_s.at[step - 1],
                           send.at[slot], recv.at[slot], {"section": peer})

    def after_near(self, kind):
        group_s, near_s = self.sets[kind][:2]
        self.near(kind).wait()
        group_s[self.core] = add_low(group_s[self.core], near_s[...])
        self.row(kind).start()

    def after_row(self, kind, block):
        group_s, row_s, fold_s = self.sets[kind][0], self.sets[kind][2], self.sets[kind][6]
        self.row(kind).wait()
        fold_s[...] = add_low(group_s[self.core, :, self.x], row_s[...])
        for step in range(1, NZ):
            self.far(kind, step, block).start()

    def sum_far(self, kind, block):
        far_s, _, sum_s, fold_s = self.sets[kind][3:7]
        for step in range(1, NZ):
            self.far(kind, step, block).wait()
        total = fold_s[self.z].astype(F32)
        for step in range(1, NZ):
            total = total + far_s[self.far_slot(kind, step, block)].astype(F32)
        sum_s[...] = low(total)

    def after_far(self, kind, block):
        self.sum_far(kind, block)
        relation = self.relation(block)

        @pl.when(relation > 0)
        def _():
            self.last(kind, relation, block).start()

    def halves(self, kind):
        last_s, sum_s = self.sets[kind][4:6]
        here = sum_s[...].astype(F32) + last_s[1].astype(F32)
        there = last_s[0].astype(F32) + last_s[2].astype(F32)
        return jnp.where(self.core == 0, here, there), jnp.where(self.core == 0, there, here)

    def after_last(self, kind, block, store):
        relation = self.relation(block)

        @pl.when(relation > 0)
        def _():
            self.last(kind, relation, block).wait_send()

        @pl.when(relation == 0)
        def _():
            for step in (1, 2, 3):
                self.last(kind, step, self.relative(step)).wait_recv()
            store(*self.halves(kind))

    def after_far_all(self, kind):
        self.sum_far(kind, 0)
        for step in (1, 2, 3):
            self.last(kind, step, self.relative(step)).start()

    def after_last_all(self, kind):
        for step in (1, 2, 3):
            self.last(kind, step, self.relative(step)).wait()
        return self.halves(kind)


def block_kernel(remote, *refs):
    (x_ref, cot_ref), data_refs, refs = refs[:2], refs[2:6], refs[6:]
    if remote:
        in_refs, refs = refs[:10], refs[10:]
        (pred_hbm, grad_hbm, in_out, so_out, cq_out, ckv_out, co_out, up_out, dn_out,
         gains_out, shifts_out, bias_out, time_out, hid_hbm, slope_hbm), refs = refs[:15], refs[15:]
    else:
        (w_hbm, wd_hbm, vec_hbm), refs = refs[:3], refs[3:]
        (pred_hbm, grad_hbm), dw_refs, refs = refs[:2], refs[2:6], refs[6:]
        (dvec_ref, time_out, hid_hbm, slope_hbm), refs = refs[:4], refs[4:]
    (unit_s, scale_s, qkv_s, prob_s, ctx_s, cq_s, cprob_s, cctx_s, hid_s, slope_s, dy_s, g_s,
     w_s, wd_s, vec_s, dvec_s, select_s, turned_s, tok_s, wide_s, folded_s, dmem_s, sinus_s, causal_s,
     own_s, flat_s, pred_ref, grad_ref, load_sem), groups, refs = refs[:29], refs[29:33], refs[33:]
    small, refs = refs[:7], refs[7:]
    obs_ref, repeat_ref, noise_ref, tw_ref, gains_ref, shifts_ref, bias_ref = small
    tokens, cols = x_ref.shape
    samples = sinus_s.shape[0]
    horizon = tokens // samples
    blocks = w_s.shape[0]
    per_sub = SUB // horizon
    score_scale = (cols // HEADS) ** (-0.5)
    section = lax.axis_index("section")
    ring = blocks - 1
    kept = ((hid_s, hid_hbm, load_sem.at[0]), (slope_s, slope_hbm, load_sem.at[1]))
    out_copies = [pltpu.make_async_copy(held.at[0], away, sem) for held, away, sem in kept]
    back_copies = [pltpu.make_async_copy(away, held.at[0], sem) for held, away, sem in kept]

    leaving = [pltpu.make_async_copy(pred_ref, pred_hbm, load_sem.at[20]),
               pltpu.make_async_copy(grad_ref, grad_hbm, load_sem.at[21])]
    sources = data_refs + (in_refs[7:] if remote else ())
    fetched = [pltpu.make_async_copy(source, held, load_sem.at[12 + index])
               for index, (source, held) in enumerate(zip(sources, small))]
    for copy in fetched:
        copy.start()
    loads = [pltpu.make_async_copy(x_ref, pred_ref, load_sem.at[0]),
             pltpu.make_async_copy(cot_ref, grad_ref, load_sem.at[1])]
    if remote:
        starts_at = (W_IN, W_SO, W_CKV, W_CQ, W_CO, W_UP)
        pieces = []
        for index, start in enumerate(starts_at):
            ref = in_refs[(0, 1, 3, 2, 4, 5)[index]]
            pieces.append(pltpu.make_async_copy(
                ref.at[0], w_s.at[section, :, start : start + ref.shape[2]], load_sem.at[2 + index]))
        pieces.append(pltpu.make_async_copy(in_refs[6].at[0], wd_s.at[section], load_sem.at[8]))
        for copy in pieces + loads:
            copy.start()
        for copy in fetched:
            copy.wait()
        vec_s[section] = jnp.zeros((VEC_ROWS, cols), F32)
        for row in range(SHIFT):
            vec_s[section, row : row + 1, :] = gains_ref[row]
        for row in range(SHIFT, BIAS):
            vec_s[section, row : row + 1, :] = shifts_ref[row - SHIFT]
        for part in range(4):
            vec_s[section, BIAS + part : BIAS + part + 1, :] = bias_ref[:, part * cols : (part + 1) * cols]
        sets = [(group,) + refs[2 + 8 * kind : 10 + 8 * kind] for kind, group in enumerate(groups)]
        sets += [refs[34 + 9 * index : 43 + 9 * index] for index in range(2)]
        links = Links(w_s, wd_s, vec_s, refs[0], refs[1], sets)
        links.greet()
        links.vectors(1, section, links.relative(2)).start()
        links.vectors(0, section, links.relative(1)).start()
        for piece, copies in enumerate((pieces[:1], pieces[1:2], pieces[2:3], pieces[3:5], pieces[5:6], pieces[6:])):
            for copy in copies:
                copy.wait()

            @pl.when(links.core == 0)
            def _():
                links.over_y(piece, section).start()

            links.to_sibling(piece, section).start()
    else:
        loads += [pltpu.make_async_copy(w_hbm, w_s, load_sem.at[2]),
                  pltpu.make_async_copy(wd_hbm, wd_s, load_sem.at[3]),
                  pltpu.make_async_copy(vec_hbm, vec_s, load_sem.at[4])]
        for copy in loads:
            copy.start()
        for copy in fetched:
            copy.wait()

    wide_masks = [jnp.concatenate([mask, mask], axis=1) for mask in half_masks()]
    lane_sub = iota((SUB, SUB), 1)
    row_sub = iota((SUB, SUB), 0)

    noise_row = noise_ref[pl.ds(section, 1), :].astype(F32)
    diagonal = iota((samples, samples), 0) == iota((samples, samples), 1)
    noise_col = jnp.sum(jnp.where(diagonal, noise_row, 0.0), axis=1, keepdims=True)
    half = cols // 2
    frequency = jnp.exp(iota((1, half), 1).astype(F32) * (-math.log(10000.0) / half))
    angles = noise_col * frequency
    sinus = low(jnp.concatenate([jnp.sin(angles), jnp.cos(angles)], axis=1))
    sinus_s[...] = sinus
    tok_s[:samples, :] = low(dot(sinus, tw_ref[...]))
    obs_count = repeat_ref.shape[-1]
    for index in range(obs_ref.shape[1]):
        tok_s[samples + index * obs_count : samples + (index + 1) * obs_count, :] = obs_ref[:, index, :]
    counts = low(repeat_ref[section].astype(F32))
    token_of = iota((obs_count, SUB), 1) - samples
    owner_of = iota((obs_count, SUB), 0)
    is_obs = token_of >= 0
    before = low((is_obs & (owner_of < token_of % obs_count)).astype(F32))
    upto = low((is_obs & (owner_of <= token_of % obs_count)).astype(F32))
    counts8 = jnp.broadcast_to(counts, (8, obs_count))
    starts = dot(counts8, before)[:1, :]
    ends = dot(counts8, upto)[:1, :]

    def select_rows(index, carried):
        key = iota((KEYS, SUB), 0) // per_sub
        lane = iota((KEYS, SUB), 1)
        sample = index * per_sub + iota((KEYS, SUB), 0) % per_sub
        sample_f = sample.astype(F32)
        time_hit = (key == 0) & (lane == sample)
        token = lane - samples
        owned = (sample_f >= starts) & (sample_f < ends)
        obs_hit = (token >= 0) & (token // obs_count == key - 1) & owned
        folded_s[index, :, :SUB] = (time_hit | obs_hit).astype(F32)
        return carried

    lax.fori_loop(0, tokens // SUB, select_rows, 0)
    selected = folded_s[...].reshape(-1, 2 * cols)[:, :SUB]
    select_s[...] = low(selected)
    selected = jnp.concatenate([selected, jnp.zeros((2 * SUB - selected.shape[0], SUB), F32)], axis=0)
    turned_s[...] = low(jnp.transpose(selected))
    same = row_sub // horizon == lane_sub // horizon
    causal_s[...] = jnp.where(same & (row_sub <= lane_sub), 0.0, -1e30)
    third = WIDE // 3
    own_s[...] = (iota((third, SUB), 0) % per_sub == iota((third, SUB), 1) // horizon).astype(F32)
    head_mask = (iota((third, cols), 0) // per_sub == iota((third, cols), 1) // (cols // HEADS)).astype(F32)
    dmem_s[...] = jnp.zeros_like(dmem_s)
    dvec_s[...] = jnp.zeros_like(dvec_s)
    for copy in loads:
        copy.wait()

    def vec(block, row):
        return vec_s[block, row : row + 1, :]

    def weight(block, start, stop):
        return w_s[block, :, start:stop]

    def condition(block):
        kv = dot(tok_s[...], weight(block, W_CKV, W_CQ))
        keys = low(kv[:, :cols])
        vals = low(kv[:, cols:] + vec(block, SHIFT + 7))

        spread = dot(select_s[...], jnp.concatenate([keys, vals], axis=1))
        both_masks = jnp.concatenate([head_mask, head_mask], axis=1)
        for index in range(tokens // SUB):
            for key in range(3):
                start = index * KEYS + key * per_sub
                copies = jnp.concatenate([spread[start : start + per_sub]] * HEADS, axis=0)
                wide_s[index, key * third : (key + 1) * third, :] = low(copies * both_masks)

    def fold(values):
        parts = []
        for part in thirds(values):
            part = part * head_mask
            parts.append(sum(part[head * per_sub : (head + 1) * per_sub] for head in range(HEADS)))
        return jnp.concatenate(parts, axis=0)

    def thirds(values):
        return [values[third * key : third * (key + 1)] for key in range(3)]

    def over_heads(values):
        return jnp.concatenate([values[:, :SUB], values[:, SUB:]], axis=0)

    def each_chunk(chunk, body):
        def at(step, carried):
            start = step * chunk
            body(pl.ds(start if isinstance(start, int) else pl.multiple_of(start, chunk), chunk), step)
            return carried

        if chunk == tokens:
            at(0, 0)
        else:
            lax.fori_loop(0, tokens // chunk, at, 0)

    def scale_of(block, rows, place):
        held = scale_s[rows, :]
        lane = iota(held.shape, 1)
        return jnp.sum(jnp.where(lane == 3 * block + place, held, 0.0), axis=1, keepdims=True)

    def keep_scale(block, rows, place, scale):
        held = scale_s[rows, :]
        scale_s[rows, :] = jnp.where(iota(held.shape, 1) == 3 * block + place, scale, held)

    def wide(values):
        return jnp.concatenate(values, axis=1)

    def both_heads(values):
        return jnp.concatenate([values * wide_masks[0], values * wide_masks[1]], axis=0)

    def both_pairs(values):
        zero = jnp.zeros((SUB, SUB), BF16)
        return jnp.concatenate([wide([values[:, :SUB], zero]), wide([zero, values[:, SUB:]])], axis=0)

    def forward(block, carried):
        after = jnp.minimum(block + 1, blocks - 1)
        if remote:
            links.arrive(block, (0, 1, 2))
        condition(block)

        def self_attention(rows, step):
            x = pred_ref[rows, :].astype(F32)
            unit0, scale0 = normalize(x)
            unit_s[block, 0, rows, :] = low(unit0)
            a = low(unit0 * vec(block, 0) + vec(block, SHIFT))
            q = low((dot(a, weight(block, 0, cols)) + vec(block, SHIFT + 3)) * score_scale)
            k = low(dot(a, weight(block, cols, 2 * cols)))
            v = low(dot(a, weight(block, 2 * cols, 3 * cols)) + vec(block, SHIFT + 4))
            qkv_s[block, rows, :cols] = q
            qkv_s[block, rows, cols : 2 * cols] = k
            qkv_s[block, rows, 2 * cols :] = v
            causal2 = wide([causal_s[...]] * 2)
            parts = []
            for sub in range(rows.size // SUB):
                span = slice(sub * SUB, (sub + 1) * SUB)
                scores = dot_nt(both_pairs(k[span]), both_heads(q[span]))
                stacked = []
                for pair in range(2):
                    score = scores[pair * SUB : (pair + 1) * SUB] + causal2
                    top = jnp.max(score, axis=0, keepdims=True)
                    expo = jnp.exp(score - top)
                    prob = low(expo * (1.0 / jnp.sum(expo, axis=0, keepdims=True)))
                    prob_s[block, step * (rows.size // SUB) + sub, pair] = prob
                    stacked.append(over_heads(prob))
                both = dot_tn(wide(stacked), both_heads(v[span]))
                parts.append(low(wide([both[:SUB, :SUB], both[SUB:, SUB:]])))
            context = jnp.concatenate(parts, axis=0)
            ctx_s[block, rows, :] = context
            x = x + (dot(context, weight(block, W_SO, W_CKV)) + vec(block, SHIFT + 5))
            g_s[rows, :] = x
            keep_scale(block, rows, 0, scale0)
            if remote:
                links.pass_on(block, block > 0, (2, 3))
                links.pass_on(block, block == 0, (2, 4), (2, 5))
                links.pass_on(after, block + 1 < blocks, (1, 0), (1, 1), (1, 2))
                links.start_y(block == 0, range(PIECES))

        each_chunk(FORWARD_SELF, self_attention)
        if remote:
            links.arrive(block, (3,))

        def cross_attention(rows, step):
            x = g_s[rows, :]
            unit1, scale1 = normalize(x)
            unit_s[block, 1, rows, :] = low(unit1)
            c = low(unit1 * vec(block, 1) + vec(block, SHIFT + 1))
            cq = low((dot(c, weight(block, W_CQ, W_CO)) + vec(block, SHIFT + 6)) * score_scale)
            cq_s[block, rows, :] = cq
            parts = []
            for sub in range(rows.size // SUB):
                index = step * (rows.size // SUB) + sub
                scores = thirds(dot_nt(wide_s[index, :, :cols], cq[sub * SUB : (sub + 1) * SUB]))
                top = jnp.maximum(jnp.maximum(scores[0], scores[1]), scores[2])
                expos = [jnp.exp(score - top) for score in scores]
                inverse = own_s[...] / (expos[0] + expos[1] + expos[2])
                prob = low(jnp.concatenate([expo * inverse for expo in expos], axis=0))
                cprob_s[block, index] = prob
                parts.append(low(dot_tn(prob, wide_s[index, :, cols:])))
            context = jnp.concatenate(parts, axis=0)
            cctx_s[block, rows, :] = context
            x = x + (dot(context, weight(block, W_CO, W_UP)) + vec(block, SHIFT + 8))
            unit2, scale2 = normalize(x)
            unit_s[block, 2, rows, :] = low(unit2)
            keep_scale(block, rows, 1, scale1)
            keep_scale(block, rows, 2, scale2)
            g_s[rows, :] = x + vec(block, SHIFT + 9)
            dy_s[0, rows, :] = low(unit2 * vec(block, 2) + vec(block, SHIFT + 2))
            if remote:
                links.pass_on(block, block > 0, (2, 4), (2, 5))
                links.pass_on(after, block + 1 < blocks, (1, 3))

        each_chunk(FORWARD_CROSS, cross_attention)
        if remote:
            links.arrive(block, (4, 5))

        def feed_forward(rows, step):
            e = dy_s[0, rows, :]
            root = math.sqrt(2.0 / math.pi)
            cube = root * 0.044715
            for part in range(4):
                lanes = slice(part * cols, (part + 1) * cols)
                u = low(dot(e, weight(block, W_UP + part * cols, W_UP + (part + 1) * cols)) + vec(
                    block, BIAS + part
                ))
                square = u * u
                gate = jnp.tanh(u * (square * low(cube) + low(root))) * low(0.5) + low(0.5)
                hidden = u * gate
                slope = gate + hidden * (low(1.0) - gate) * (square * low(6.0 * cube) + low(2.0 * root))
                hid_s[block % ring, rows, lanes] = hidden
                slope_s[block % ring, rows, lanes] = slope
            pred_ref[rows, :] = low(g_s[rows, :] + dot(hid_s[block % ring, rows, :], wd_s[block]))
            if remote:
                links.pass_on(after, block + 1 < blocks, (2, 0), (2, 1), (2, 2), (1, 4), (1, 5))

        @pl.when(block == ring)
        def _():
            for copy in out_copies:
                copy.wait()

        each_chunk(FORWARD_FF, feed_forward)

        @pl.when(block == 0)
        def _():
            for copy in out_copies:
                copy.start()

        return carried

    if remote:
        links.pass_on(0, True, (1, 0), (1, 1), (2, 0), (1, 2), (2, 1), (1, 3), (2, 2), (1, 4), (2, 3), (1, 5))
    lax.fori_loop(0, blocks, forward, 0)
    leaving[0].start()

    def put(kind, start, value):
        width, taken = WIDTHS[kind], 0
        while taken < value.shape[1]:
            index, place = (start + taken) // width, (start + taken) % width
            count = min(value.shape[1] - taken, width - place)
            part = low(value[:, taken : taken + count]).reshape(NZ, NX, ROWS, count)
            groups[kind][index, :, :, :, place : place + count] = part
            taken += count

    def emit(block, kind):
        if remote:
            links.near(kind).start()
        else:
            copy = pltpu.make_async_copy(groups[kind], dw_refs[kind].at[block], load_sem.at[2])
            copy.start()
            copy.wait()

    def store_down(first, second):
        blocks_of = [value[:, q * SUB : (q + 1) * SUB] for value in (first, second) for q in range(4)]
        dn_out[...] = jnp.transpose(jnp.concatenate(blocks_of, axis=0))

    def store_up(first, second):
        up_out[...] = wide([first, second])

    def store_cross(first, second):
        joined = wide([first, second])
        ckv_out[...] = joined[:, : 2 * cols]
        for place, out in enumerate((cq_out, co_out, so_out)):
            out[...] = joined[:, (2 + place) * cols : (3 + place) * cols]

    def store_self(first, second):
        in_out[...] = wide([first, second])

    stores = (store_down, store_up, store_cross, store_self)

    def advance(works):
        if not remote:
            return
        for kind, stage, block, there in works:

            def run(kind=kind, stage=stage, block=block):
                if stage == 1:
                    links.after_near(kind)
                elif stage == 2:
                    links.after_row(kind, block)
                elif stage == 3:
                    links.after_far(kind, block)
                else:
                    links.after_last(kind, block, stores[kind])

            if there is True:
                run()
            else:
                pl.when(there)(run)

    def time_gradient():
        dmem = dmem_s[...]
        dmem_high = low(dmem)
        dmem_low = low(dmem - dmem_high.astype(F32))
        return dot_tn(sinus_s[...], dmem_high) + dot_tn(sinus_s[...], dmem_low)

    def emit_vectors():
        vectors = dvec_s[...].reshape(blocks * VEC_ROWS, cols)
        vectors = jnp.concatenate([vectors, jnp.zeros((SUB - blocks * VEC_ROWS, cols), F32)], axis=0)
        turned = jnp.transpose(vectors).reshape(GROUPS, ROWS, SUB)
        lane = iota((ROWS, SUB), 1) % VEC_ROWS
        rows_out = []
        for group in range(GROUPS):
            part, high = group // 2, group % 2
            piece = turned[group]
            for j in range(4):
                source = turned[4 * high + j]
                if j != part:
                    source = pltpu.roll(source, (j - part) % SUB, 1)
                piece = jnp.where(lane == BIAS + j, source, piece)
            rows_out.append(piece)
        turned = jnp.concatenate(rows_out, axis=0)
        for index in range(2):
            sets[VECTOR][0][index] = low(turned).reshape(NZ, NX, ROWS, SUB)
        links.near(VECTOR).start()

    def backward(turn, carried):
        block = blocks - 1 - turn
        earlier, before = block + 1, block + 2
        again, third_turn = turn > 0, turn > 1

        def add_vec(row, values):
            dvec_s[block, row : row + 1, :] += values

        def turn_over_ones(left):
            return jnp.concatenate([jnp.transpose(left), jnp.ones((16, tokens), BF16)], axis=0)

        def put_scaled(kind, start, unit_row, right, sum_rows):
            turned = turn_over_ones(unit_s[block, unit_row])
            gain = place_column(vec(block, unit_row))
            shift = place_column(vec(block, SHIFT + unit_row))
            parts = []
            for place, row in enumerate(sum_rows):
                both = dot(turned, right[:, place * cols : (place + 1) * cols])
                sums = both[cols : cols + 1]
                dvec_s[block, row : row + 1, :] = sums
                put(kind, start + place * cols, both[:cols] * gain + shift * sums)
                parts.append((both[:cols], sums))
            return parts

        def put_plain(kind, start, left, right, row):
            both = dot(turn_over_ones(left), right)
            dvec_s[block, row : row + 1, :] = both[cols : cols + 1]
            put(kind, start, both[:cols])

        @pl.when(block == 0)
        def _():
            for copy in back_copies:
                copy.wait()

        turned = jnp.transpose(grad_ref[...])
        for part in range(4):
            piece = low(dot(turned, hid_s[block % ring, :, part * cols : (part + 1) * cols]))
            for index in range(2):
                for x in range(NX):
                    for q in range(4):
                        row = SUB * index + ROWS * q
                        groups[DOWN][index, part, x, :, q * SUB : (q + 1) * SUB] = piece[
                            row : row + ROWS, x * SUB : (x + 1) * SUB
                        ]
        def feed_forward(rows, step):
            dy3 = grad_ref[rows, :]
            g = dy3.astype(F32)
            add_vec(SHIFT + 9, jnp.sum(g, axis=0, keepdims=True))
            for part in range(4):
                lanes = slice(part * cols, (part + 1) * cols)
                dh = dot_nt(dy3, wd_s[block, lanes, :])
                slope_s[block % ring, rows, lanes] = low(dh) * slope_s[block % ring, rows, lanes]
            de = dot_nt(slope_s[block % ring, rows, :], weight(block, W_UP, W_END))
            back, along, flat = normalize_back(
                de, unit_s[block, 2, rows, :].astype(F32), scale_of(block, rows, 2), vec(block, 2)
            )
            add_vec(2, along)
            add_vec(SHIFT + 2, flat)
            g = g + back
            g_s[rows, :] = g
            dy_s[0, rows, :] = low(g)

        each_chunk(BACK_FF, feed_forward)
        advance((
            (DOWN, 3, earlier, again), (UP, 2, earlier, again), (SELF, 1, earlier, again),
            (UP, 4, before, third_turn), (CROSS, 4, before, third_turn), (SELF, 4, before, third_turn),
        ))
        emit(block, DOWN)
        pl.when(turn == 0)(back_copies[0].start)

        put_scaled(UP, 0, 2, slope_s[block % ring], [BIAS + part for part in range(4)])
        condition(block)
        advance(((CROSS, 2, earlier, again),))
        emit(block, UP)
        pl.when(turn == 0)(back_copies[1].start)

        def cross_attention(rows, step):
            dctx = low(dot_nt(dy_s[0, rows, :], weight(block, W_CO, W_UP)))
            for sub in range(rows.size // SUB):
                index = step * (rows.size // SUB) + sub
                span = pl.ds(index * SUB if isinstance(index, int) else pl.multiple_of(index * SUB, SUB), SUB)
                keys, vals = wide_s[index, :, :cols], wide_s[index, :, cols:]
                part = dctx[sub * SUB : (sub + 1) * SUB]
                prob = cprob_s[block, index]
                prob32 = prob.astype(F32)
                weighted = prob32 * dot_nt(vals, part)
                inner = sum(thirds(weighted))
                dscore = low(weighted - prob32 * jnp.concatenate([inner] * 3, axis=0))
                folded_s[index, :, :cols] = fold(dot(dscore, cq_s[block, span, :]))
                folded_s[index, :, cols:] = fold(dot(prob, part))
                cq_s[block, span, :] = low(dot_tn(dscore, keys) * score_scale)
            dcq = cq_s[block, rows, :]
            dc = dot_nt(dcq, weight(block, W_CQ, W_CO))
            back, along, flat = normalize_back(
                dc, unit_s[block, 1, rows, :].astype(F32), scale_of(block, rows, 1), vec(block, 1)
            )
            add_vec(1, along)
            add_vec(SHIFT + 1, flat)
            g = g_s[rows, :] + back
            g_s[rows, :] = g
            dy_s[1, rows, :] = low(g)

        each_chunk(BACK_CROSS, cross_attention)
        advance(((DOWN, 1, block, True), (DOWN, 4, earlier, again)))

        folded = folded_s[...].reshape(-1, 2 * cols)
        dkv32 = dot(turned_s[:, : folded.shape[0]], low(folded))
        dkv = low(dkv32)
        add_vec(SHIFT + 7, jnp.sum(dkv32[:, cols:], axis=0, keepdims=True))
        dmem_s[...] += dot_nt(dkv[:samples], weight(block, W_CKV, W_CQ))
        put(CROSS, 0, dot_tn(tok_s[...], dkv))
        put_scaled(CROSS, 2 * cols, 1, cq_s[block], [SHIFT + 6])
        put_plain(CROSS, 3 * cols, cctx_s[block], dy_s[0], SHIFT + 8)
        put_plain(CROSS, 4 * cols, ctx_s[block], dy_s[1], SHIFT + 5)
        advance(((SELF, 2, earlier, again), (UP, 1, block, True)))
        emit(block, CROSS)
        if remote:

            @pl.when(block == 0)
            def _():
                dtime = time_gradient()
                for index in range(2):
                    part = low(dtime[:, index * SUB : (index + 1) * SUB])
                    sets[TIME][0][index] = part.reshape(NZ, NX, ROWS, SUB)
                links.near(TIME).start()

        def self_attention(rows, step):
            dctx = low(dot_nt(dy_s[1, rows, :], weight(block, W_SO, W_CKV)))
            for sub in range(rows.size // SUB):
                index = step * (rows.size // SUB) + sub
                span = pl.ds(index * SUB if isinstance(index, int) else pl.multiple_of(index * SUB, SUB), SUB)
                part = dctx[sub * SUB : (sub + 1) * SUB]
                queries, keys, values = (qkv_s[block, span, place * cols : (place + 1) * cols] for place in range(3))
                sides = (slice(0, SUB), slice(SUB, 2 * SUB))
                dstack = both_heads(part)
                qstack = both_heads(queries)
                kstack = both_heads(keys)
                probs = [prob_s[block, index, pair] for pair in range(2)]
                dprobs = dot_nt(both_pairs(values), dstack)
                dprobs = [dprobs[side] for side in sides]
                dscores = []
                for prob, dprob in zip(probs, dprobs):
                    prob32 = prob.astype(F32)
                    weighted = prob32 * dprob
                    dscores.append(low(weighted - prob32 * jnp.sum(weighted, axis=0, keepdims=True)))
                dq = dot_tn(wide([over_heads(dscore) for dscore in dscores]), kstack)
                dq = [dq[side, side] for side in sides]
                dk = dot(jnp.concatenate(dscores, axis=0), qstack)
                dk = [dk[side, side] for side in sides]
                dv = dot(jnp.concatenate(probs, axis=0), dstack)
                dv = [dv[side, side] for side in sides]
                qkv_s[block, span, :cols] = low(wide(dq) * score_scale)
                qkv_s[block, span, cols : 2 * cols] = low(wide(dk))
                qkv_s[block, span, 2 * cols :] = low(wide(dv))

        each_chunk(BACK_SELF, self_attention)
        advance((
            (UP, 3, earlier, again), (CROSS, 3, earlier, again), (DOWN, 2, block, True),
            (CROSS, 1, block, True), (TIME, 1, block, block == 0),
        ))

        gain_column, shift_column = 0.0, 0.0
        for place, (both, sums) in enumerate(
            put_scaled(SELF, 0, 0, qkv_s[block], (SHIFT + 3, KEYSUM, SHIFT + 4))
        ):
            matrix = weight(block, place * cols, (place + 1) * cols).astype(F32)
            gain_column += jnp.sum(both * matrix, axis=1, keepdims=True)
            shift_column += jnp.sum(sums * matrix, axis=1, keepdims=True)
        dvec_s[block, 0:1, :] = place_row(gain_column)
        dvec_s[block, SHIFT : SHIFT + 1, :] = place_row(shift_column)
        emit(block, SELF)
        if remote:
            pl.when(block == 0)(emit_vectors)

        def self_norm(rows, step):
            da = dot_nt(qkv_s[block, rows, :], weight(block, 0, 3 * cols))
            back, _, _ = normalize_back(
                da, unit_s[block, 0, rows, :].astype(F32), scale_of(block, rows, 0), vec(block, 0)
            )
            grad_ref[rows, :] = low(g_s[rows, :] + back)

        each_chunk(BACK_SELF, self_norm)
        advance(((SELF, 3, earlier, again),))
        return carried

    lax.fori_loop(0, blocks, backward, 0)
    leaving[1].start()
    if not remote:
        for copy in leaving:
            copy.wait()
        time_out[...] = time_gradient()
        dvec_ref[...] = dvec_s[...]
        return

    links.after_row(UP, 0)
    links.after_near(SELF)
    links.after_near(VECTOR)
    links.after_far(DOWN, 0)
    links.after_row(CROSS, 0)
    links.after_row(TIME, 0)
    links.after_last(UP, 1, store_up)
    links.after_last(CROSS, 1, store_cross)
    links.after_far(UP, 0)
    links.after_row(SELF, 0)
    links.after_row(VECTOR, 0)
    links.after_last(SELF, 1, store_self)
    links.after_last(DOWN, 0, store_down)
    links.after_far(CROSS, 0)
    links.after_far_all(TIME)
    links.after_last(UP, 0, store_up)
    links.after_far(SELF, 0)
    links.after_far_all(VECTOR)
    links.after_last(CROSS, 0, store_cross)
    time_out[...] = wide(links.after_last_all(TIME))
    links.after_last(SELF, 0, store_self)
    mine, _ = links.after_last_all(VECTOR)
    padded = jnp.concatenate([mine, jnp.zeros((SUB - ROWS, SUB), F32)], axis=0)
    flat_s[...] = jnp.transpose(padded)
    mine = flat_s[pl.ds(pl.multiple_of(section * VEC_ROWS, 8), VEC_ROWS), :]
    for row in range(SHIFT):
        gains_out[row] = mine[row : row + 1, :ROWS]
    for row in range(SHIFT, BIAS):
        shifts_out[row - SHIFT] = mine[row : row + 1, :ROWS]
    bias = mine[BIAS : BIAS + 1, :]
    for part in range(1, 4):
        bias = bias + pltpu.roll(mine[BIAS + part : BIAS + part + 1, :], part * ROWS, 1)
    bias_out[...] = bias
    links.finish_weights()
    for copy in leaving:
        copy.wait()


def run_blocks(remote, x, cot, obs, repeat, noise, time_weight, *weights, interpret=False):
    tokens, cols = x.shape
    blocks = 4
    samples = noise.shape[1]
    vmem = pl.BlockSpec(memory_space=pltpu.VMEM)
    hbm = pl.BlockSpec(memory_space=pl.ANY)
    half_rows = (NZ, NX, ROWS)
    scratch = [
        pltpu.VMEM((blocks, 3, tokens, cols), BF16),
        pltpu.VMEM((tokens, SUB), F32),
        pltpu.VMEM((blocks, tokens, 3 * cols), BF16),
        pltpu.VMEM((blocks, tokens // SUB, 2, SUB, 2 * SUB), BF16),
        pltpu.VMEM((blocks, tokens, cols), BF16),
        pltpu.VMEM((blocks, tokens, cols), BF16),
        pltpu.VMEM((blocks, tokens // SUB, WIDE, SUB), BF16),
        pltpu.VMEM((blocks, tokens, cols), BF16),
        pltpu.VMEM((blocks - 1, tokens, 4 * cols), BF16),
        pltpu.VMEM((blocks - 1, tokens, 4 * cols), BF16),
        pltpu.VMEM((2, tokens, cols), BF16),
        pltpu.VMEM((tokens, cols), F32),
        pltpu.VMEM((blocks, cols, W_END), BF16),
        pltpu.VMEM((blocks, 4 * cols, cols), BF16),
        pltpu.VMEM((blocks, VEC_ROWS, cols), F32),
        pltpu.VMEM((blocks, VEC_ROWS, cols), F32),
        pltpu.VMEM((tokens // SUB * KEYS, SUB), BF16),
        pltpu.VMEM((SUB, 2 * SUB), BF16),
        pltpu.VMEM((SUB, cols), BF16),
        pltpu.VMEM((tokens // SUB, WIDE, 2 * cols), BF16),
        pltpu.VMEM((tokens // SUB, KEYS, 2 * cols), F32),
        pltpu.VMEM((samples, cols), F32),
        pltpu.VMEM((samples, cols), BF16),
        pltpu.VMEM((SUB, SUB), F32),
        pltpu.VMEM((WIDE // 3, SUB), F32),
        pltpu.VMEM((SUB, SUB), F32),
        pltpu.VMEM((tokens, cols), BF16),
        pltpu.VMEM((tokens, cols), BF16),
        pltpu.SemaphoreType.DMA((22,)),
    ]
    scratch += [pltpu.VMEM((2,) + half_rows + (width,), BF16) for width in WIDTHS[:TIME]]
    parts = (obs, repeat, noise, time_weight) + tuple(weights[7:])
    scratch += [pltpu.VMEM(part.shape, part.dtype) for part in parts]
    if not remote:
        scratch += [pltpu.VMEM((8, SUB), F32)] * 3
    if remote:
        scratch += [pltpu.SemaphoreType.DMA((5 * PIECES + 3,))] * 2
        for kind, width in enumerate(WIDTHS):
            if kind >= TIME:
                scratch.append(pltpu.VMEM((2,) + half_rows + (width,), BF16))
            scratch += [
                pltpu.VMEM(half_rows + (width,), BF16),
                pltpu.VMEM((NZ, ROWS, width), BF16),
                pltpu.VMEM(((2 if kind in TURNS else 1) * (NZ - 1), ROWS, width), BF16),
                pltpu.VMEM((3, ROWS, width), BF16),
                pltpu.VMEM((ROWS, width), BF16),
                pltpu.VMEM((NZ, ROWS, width), BF16),
                pltpu.SemaphoreType.DMA((3 + 2 * NZ,)),
                pltpu.SemaphoreType.DMA((3 + 2 * NZ,)),
            ]
        shapes = ((ROWS, 3 * cols), (ROWS, cols), (ROWS, cols), (ROWS, 2 * cols), (ROWS, cols),
                  (ROWS, 4 * cols), (4 * ROWS, cols), (SHIFT, 1, ROWS), (BIAS - SHIFT, 1, ROWS), (1, 4 * ROWS),
                  (ROWS, cols))
        outs = tuple(jax.ShapeDtypeStruct(shape, F32) for shape in shapes)
        in_specs = [hbm] * 16
        out_specs = (hbm, hbm) + (vmem,) * len(outs)
        params = pltpu.CompilerParams(
            vmem_limit_bytes=VMEM_BYTES, collective_id=0, has_side_effects=True)
    else:
        outs = (
            jax.ShapeDtypeStruct((blocks, VEC_ROWS, cols), F32),
            jax.ShapeDtypeStruct((cols, cols), F32),
        )
        outs = tuple(
            jax.ShapeDtypeStruct((blocks, 2) + half_rows + (width,), BF16) for width in WIDTHS[:TIME]
        ) + outs
        in_specs = [hbm] * 9
        out_specs = (hbm, hbm) + (hbm,) * 4 + (vmem, vmem)
        params = pltpu.CompilerParams(vmem_limit_bytes=VMEM_BYTES)
    low_out = jax.ShapeDtypeStruct((tokens, cols), BF16)
    away = jax.ShapeDtypeStruct((tokens, 4 * cols), BF16)
    return pl.pallas_call(
        functools.partial(block_kernel, remote),
        out_shape=(low_out, low_out) + outs + (away, away),
        in_specs=in_specs,
        out_specs=out_specs + (hbm, hbm),
        scratch_shapes=scratch,
        compiler_params=params,
        interpret=interpret,
    )(x, cot, obs, repeat, noise, time_weight, *weights)


def hand_out(*refs):
    count = (len(refs) - 1) // 3
    held, sem = refs[2 * count : 3 * count], refs[-1]
    arriving = [pltpu.make_async_copy(refs[i], held[i], sem.at[i]) for i in range(count)]
    leaving = []
    for copy in arriving:
        copy.start()
    for index in range(count):
        target = refs[count + index]
        if len(target.shape) > len(held[index].shape):
            target = target.at[0]
        arriving[index].wait()
        leaving.append(pltpu.make_async_copy(held[index], target, sem.at[index]))
        leaving[-1].start()
    for copy in leaving:
        copy.wait()


def finished(results):
    hbm = pl.BlockSpec(memory_space=pl.ANY)
    shapes = [(1,) + result.shape for result in results[:9]] + [result.shape for result in results[9:]]
    return pl.pallas_call(
        hand_out,
        out_shape=tuple(jax.ShapeDtypeStruct(shape, result.dtype) for shape, result in zip(shapes, results)),
        in_specs=[hbm] * len(results),
        out_specs=(hbm,) * len(results),
        scratch_shapes=[pltpu.VMEM(result.shape, result.dtype) for result in results]
        + [pltpu.SemaphoreType.DMA((len(results),))],
    )(*results)


def pack_weights(self_in, self_out, cross_q, cross_kv, cross_out, mlp_up, mlp_down):
    parts = (self_in, self_out, cross_kv, cross_q, cross_out, mlp_up)
    return jnp.concatenate([part[0] for part in parts], axis=1), mlp_down[0]


def pack_vectors(gains, shifts, mlp_bias):
    cols = gains.shape[-1]
    rows = jnp.concatenate([gains[0], shifts[0], mlp_bias.reshape(4, cols)], axis=0)
    return jnp.pad(rows, ((0, VEC_ROWS - rows.shape[0]), (0, 0)))


def natural(dweights):
    def joined(kind):
        parts = dweights[kind].reshape(-1, 2, GROUPS * ROWS, WIDTHS[kind])
        return jnp.concatenate([parts[:, 0], parts[:, 1]], axis=-1)

    blocks = dweights[DOWN].shape[0]
    down = dweights[DOWN].reshape(blocks, 2, GROUPS, ROWS, 4, SUB).transpose(0, 2, 5, 1, 4, 3)
    return joined(UP), joined(CROSS), joined(SELF), down.reshape(blocks, GROUPS * SUB, -1)


def gathered(data, packed_weights, packed_vectors):
    sections = lax.axis_size("section")
    groups = lax.axis_size("dp")
    cols = data[0].shape[-1]
    weights = [lax.all_gather(part, "section", axis=0) for part in packed_weights]
    vectors = lax.all_gather(packed_vectors, "section", axis=0)
    pred, grad, *dweights, dvectors, dtime, _, _ = run_blocks(False, *data, *weights, vectors)
    rows = cols // groups
    up, cross, own, down = natural(dweights)
    rest = jnp.concatenate([up, cross, own], axis=2).reshape(sections, groups, -1)
    down = down.reshape(sections, groups, -1)
    small = dvectors[:, :BIAS].reshape(sections, BIAS, groups, rows).transpose(0, 2, 1, 3)
    small = small.reshape(sections, groups, BIAS * rows)
    bias = dvectors[:, BIAS:KEYSUM].reshape(sections, groups, 4 * rows)
    term = jnp.broadcast_to(dtime.reshape(1, groups, rows * cols), (sections, groups, rows * cols))
    sent = jnp.concatenate([rest, down], axis=2).reshape(sections * groups, -1)
    sent_small = jnp.concatenate([small, bias, term], axis=2).reshape(sections * groups, -1)
    got = lax.psum_scatter(sent, ("section", "dp"), scatter_dimension=0, tiled=True)[0].astype(F32)
    got_small = lax.psum_scatter(sent_small, ("section", "dp"), scatter_dimension=0, tiled=True)[0]
    widths = (up.shape[-1], cross.shape[-1], own.shape[-1])
    split = sum(widths) * rows
    rest = got[:split].reshape(rows, sum(widths))
    down = got[split:].reshape(4 * rows, cols)
    small = got_small[: BIAS * rows].reshape(BIAS, rows)
    bias = got_small[BIAS * rows : (BIAS + 4) * rows].reshape(4, rows)
    term = got_small[(BIAS + 4) * rows :].reshape(rows, cols)
    up, cross, own = jnp.split(rest, (widths[0], widths[0] + widths[1]), axis=1)
    kv, query, out, self_out = jnp.split(cross, (2 * cols, 3 * cols, 4 * cols), axis=1)
    return (pred, grad, own, self_out, query, kv, out, up, down, small[:SHIFT], small[SHIFT:], bias, term)


def local(
    horizon, cotangent, obs_tokens, obs_repeat, noise_step, time_weight,
    self_in, self_out, cross_q, cross_kv, cross_out, mlp_up, mlp_down, gains, shifts, mlp_bias,
):
    cols = horizon.shape[-1]
    data = (horizon[0], cotangent[0], obs_tokens[0], obs_repeat, noise_step, time_weight)
    weights = (self_in, self_out, cross_q, cross_kv, cross_out, mlp_up, mlp_down)
    if lax.axis_size("dp") == GROUPS:
        vectors = (gains.transpose(1, 0, 2), shifts.transpose(1, 0, 2), mlp_bias)
        results = finished(run_blocks(True, *data, *weights, *vectors)[:-2])
        return results[:9] + (results[9].transpose(1, 0, 2), results[10].transpose(1, 0, 2)) + results[11:]
    results = gathered(data, pack_weights(*weights), pack_vectors(gains, shifts, mlp_bias))
    return tuple(result[None] for result in results[:11]) + (results[11].reshape(1, -1), results[12])


def solution(mesh):
    whole = P("section", None, None)
    return jax.shard_map(
        local,
        mesh=mesh,
        in_specs=(
            P("section", "dp", None), P("section", "dp", None), P("section", "dp", None, None),
            P(None, "dp", None), P(None, "dp"), P(),
            whole, whole, whole, whole, whole, whole, whole, whole, whole, P("section", None),
        ),
        out_specs=(P("section", "dp", None),) * 9
        + (P("section", None, "dp"), P("section", None, "dp"), P("section", "dp"), P("dp", None)),
        check_vma=False,
    )
```
